512 devices in a mesh: dp: 64 (over z, x, core), ctx: 8 (over y).
Axes of the slice: x: 4, y: 8, z: 8, core: 2. Of those that a mesh axis runs over, the one named last changes fastest.
Arguments:
- q_short: bfloat16 [65536, 2048], P(('dp', 'ctx')), may hold values from -32 to 32
- k_short: bfloat16 [65536, 512], P(('dp', 'ctx')), may hold values from -32 to 32
- v_short: bfloat16 [65536, 512], P(('dp', 'ctx')), may hold values from -6 to 6
- short_lengths: int32 [64, 8, 2, 3], P(None, 'ctx'), may hold values from 1 to 48, 64 in all within a row
- bin_dest: int32 [64, 8, 2], P(None, 'ctx'), may hold values from 0 to 63, as said below
- q_long: bfloat16 [65536, 2048], P(('dp', 'ctx')), may hold values from -32 to 32
- k_long: bfloat16 [65536, 512], P(('dp', 'ctx')), may hold values from -32 to 32
- v_long: bfloat16 [65536, 512], P(('dp', 'ctx')), may hold values from -6 to 6
- long_lengths: int32 [64, 3], P('dp'), may hold values from 1 to 960, 1024 in all within a row
Outputs:
- out_short: bfloat16 [65536, 2048], P(('dp', 'ctx'))
- out_long: bfloat16 [65536, 2048], P(('dp', 'ctx'))
The draws below stay inside these ranges and needn't reach their ends.
Inputs may be any that keep to these rules, and one draw needn't show every extreme that they name: bin_dest[s, c, j] = s XOR m[c, j], where for each c the 2 masks m[c, j] are distinct; so every dp rank receives exactly 2 bins at each ctx index, one of each j. At ctx index 0 one of the masks is 63. `short_lengths`: each bin holds 3 documents that fill its 64 tokens. `long_lengths`: the 3 documents of a region fill its 1024 tokens.
All inputs are finite; a program needn't handle non-finite values.
Results may differ from the reference program's by a relative error of at most 0.009.
Values may be sent and summed in bfloat16 or wider, within the bound.
A program may use at most 64 MiB of HBM per device.

```python
import math
import jax
import jax.numpy as jnp
import numpy as np
from jax import lax

QHEADS = 16
KVHEADS = 4
HEAD_DIM = 128
KWIDTH = 512
BIN_LEN = 64
BINS = 2
DOCS_BIN = 3
SHORT_MOST = 48
SPAN = 128
REGION = 1024
LONG_DOCS = 3
LONG_MOST = 960
SHORT_TOKENS = 65536
LONG_TOKENS = 65536
N_DP = 64
N_CTX = 8


def aligned_pair(key, row_count, query_heads, key_heads, head_dim, share):
    subkeys = jax.random.split(key, 5)
    key_base = jnp.clip(jax.random.normal(subkeys[0], (row_count, key_heads, head_dim), jnp.float32), -4.5, 4.5)
    query_base = jnp.clip(jax.random.normal(subkeys[1], (row_count, query_heads, head_dim), jnp.float32), -4.5, 4.5)
    chosen = jax.random.uniform(subkeys[2], (row_count,), jnp.float32) < share
    strength = jax.random.uniform(subkeys[3], (row_count, 1, 1), jnp.float32, minval=4.6, maxval=7.0)
    score_gap = jax.random.uniform(subkeys[4], (row_count, 1), jnp.float32, minval=1.0, maxval=3.0)
    slow_lane = jnp.arange(head_dim) % (head_dim // 2) >= head_dim // 4
    lifted = key_base * strength
    energy = jnp.sum(jnp.where(slow_lane, lifted * lifted, 0.0), axis=-1)
    shrink_ratio = jnp.maximum(1.0 - score_gap * math.sqrt(head_dim) / energy, 0.5)
    shrunk = jnp.roll(lifted * shrink_ratio[..., None], -1, axis=0)
    follows = jnp.roll(chosen, -1).at[-1].set(False)
    chosen_wide = chosen[:, None, None]
    key_rows = jnp.where(chosen_wide & slow_lane, lifted, key_base)
    key_rows = jnp.where(follows[:, None, None] & slow_lane & jnp.logical_not(chosen_wide), shrunk, key_rows)
    spread = jnp.repeat(key_rows, query_heads // key_heads, axis=1)
    query_rows = jnp.where(chosen_wide & slow_lane, spread, query_base)
    return (query_rows.reshape(row_count, query_heads * head_dim), key_rows.reshape(row_count, key_heads * head_dim))


def draw_q_short(key, part):
    share = 0.0
    pair = aligned_pair(key, N_DP * N_CTX * BINS * BIN_LEN, QHEADS, KVHEADS, HEAD_DIM, share)
    return pair[0].astype(jnp.bfloat16)


def draw_k_short(key, part):
    share = 0.0
    pair = aligned_pair(key, N_DP * N_CTX * BINS * BIN_LEN, QHEADS, KVHEADS, HEAD_DIM, share)
    return pair[1].astype(jnp.bfloat16)


def draw_q_long(key, part):
    share = 0.0
    pair = aligned_pair(jax.random.fold_in(key, 11), N_DP * N_CTX * SPAN, QHEADS, KVHEADS, HEAD_DIM, share)
    return pair[0].astype(jnp.bfloat16)


def draw_k_long(key, part):
    share = 0.0
    pair = aligned_pair(jax.random.fold_in(key, 11), N_DP * N_CTX * SPAN, QHEADS, KVHEADS, HEAD_DIM, share)
    return pair[1].astype(jnp.bfloat16)


def draw_bin_dest(key, part):
    key = jax.random.fold_in(key, 3)

    def one_ctx(ctx_key, ctx_id):
        first_key, second_key = jax.random.split(ctx_key)
        order = jax.random.permutation(first_key, N_DP).astype(jnp.int32)
        far_at = jnp.argmax(order == N_DP - 1).astype(jnp.int32)
        column = jax.random.randint(second_key, (), 0, BINS).astype(jnp.int32)
        lead = jnp.where(ctx_id == 0, far_at - column, 0).astype(jnp.int32)
        picks = (jnp.arange(BINS, dtype=jnp.int32) + lead) % N_DP
        return order[picks]
    masks = jax.vmap(one_ctx)(jax.random.split(key, N_CTX), jnp.arange(N_CTX, dtype=jnp.int32))
    homes = jnp.arange(N_DP, dtype=jnp.int32)
    return jnp.bitwise_xor(homes[:, None, None], masks[None, :, :]).astype(jnp.int32)


def block_levels(stream_key, shape, cuts, least, top_value):
    loudness, own = 1.0, jax.random.fold_in(stream_key, 6)
    for axis_at, shards_of in cuts:
        draws = jnp.exp(jax.random.uniform(jax.random.fold_in(own, axis_at), (shards_of,), jnp.float32, least / len(cuts), top_value / len(cuts)))
        loudness = loudness * jnp.repeat(draws, shape[axis_at] // shards_of).reshape([-1 if axis == axis_at else 1 for axis in range(len(shape))])
    return loudness


def length_profile(number_of, total, most, slope):
    loads = [(1 << 20) // math.isqrt(rank ** slope) + 1 for rank in range(2, number_of + 1)]
    surplus, given = total - most - (number_of - 1), [1] * (number_of - 1)
    while surplus > 0:
        free = [i for i in range(number_of - 1) if given[i] < most]
        pool, left = sum([loads[i] for i in free]), surplus
        for i in free:
            more = min(most - given[i], max(1, left * loads[i] // pool), surplus)
            given[i] = given[i] + more
            surplus = surplus - more
    return np.array([most] + given)


def ragged_sizes(own_key, count, total, most, skew):
    if count == 2:
        one = jax.random.randint(own_key, (), max(1, total - most), min(most, total - 1) + 1)
        return jnp.stack([one, total - one])
    sizes = jnp.asarray(length_profile(count, total, most, skew), jnp.int32)
    couples = (count - 1) // 2
    donor, sink = sizes[1:1 + 2 * couples:2], sizes[2:2 + 2 * couples:2]
    slack = jnp.minimum(donor - 1, most - sink)
    passed = jax.random.randint(jax.random.fold_in(own_key, 1), (couples,), 0, 1 << 20) % (slack + 1)
    sizes = sizes.at[1:1 + 2 * couples:2].set(donor - passed).at[2:2 + 2 * couples:2].set(sink + passed)
    return sizes[jax.random.permutation(jax.random.fold_in(own_key, 2), count)]


def gaussian(rng, dims, deviation, most, pieces=(), kind=jnp.bfloat16):
    values = jax.random.normal(rng, dims, jnp.float32) * deviation
    if len(pieces) > 0:
        values = block_levels(rng, dims, pieces, -0.22, 0.18) * values
    return jnp.clip(values, min=-most, max=most).astype(kind)


def setup_inputs(seed: int = 0) -> dict:
    splits = jax.random.split(jax.random.key(seed), 10)
    q_short = draw_q_short(jax.random.fold_in(splits[9], 71), 0)
    k_short = draw_k_short(jax.random.fold_in(splits[9], 71), 0)
    v_short = gaussian(splits[2], (SHORT_TOKENS, KWIDTH), 1.0, 6.0, ((0, 512),))
    short_lengths = jax.vmap(lambda own: ragged_sizes(own, DOCS_BIN, BIN_LEN, SHORT_MOST, 1))(jax.random.split(splits[3], N_DP * N_CTX * BINS)).reshape((N_DP, N_CTX, BINS, DOCS_BIN)).astype(jnp.int32)
    bin_dest = draw_bin_dest(jax.random.fold_in(splits[9], 71), 0)
    q_long = draw_q_long(jax.random.fold_in(splits[9], 71), 0)
    k_long = draw_k_long(jax.random.fold_in(splits[9], 71), 0)
    v_long = gaussian(splits[7], (LONG_TOKENS, KWIDTH), 1.0, 6.0, ((0, 512),))
    long_lengths = jax.vmap(lambda own: ragged_sizes(own, LONG_DOCS, REGION, LONG_MOST, 1))(jax.random.split(splits[8], N_DP)).reshape((N_DP, LONG_DOCS)).astype(jnp.int32)
    return {"q_short": q_short, "k_short": k_short, "v_short": v_short, "short_lengths": short_lengths, "bin_dest": bin_dest, "q_long": q_long, "k_long": k_long, "v_long": v_long, "long_lengths": long_lengths}


THETA = 500000.0
NEGATIVE = -1e+30

def doc_layout(lengths, extent):
    lengths = lengths.astype(jnp.int32)
    doc_ends = jnp.cumsum(lengths, axis=-1).astype(jnp.int32)
    doc_starts = (doc_ends - lengths).astype(jnp.int32)
    token_index = jnp.arange(extent, dtype=jnp.int32)
    covered = (token_index[:, None] >= doc_starts[..., None, :]) & (token_index[:, None] < doc_ends[..., None, :])
    doc_labels = jnp.arange(lengths.shape[-1], dtype=jnp.int32)
    segment = lax.optimization_barrier(jnp.sum(jnp.where(covered, doc_labels, 0), axis=-1)).astype(jnp.int32)
    offset = lax.optimization_barrier(jnp.sum(jnp.where(covered, token_index[:, None] - doc_starts[..., None, :], 0), axis=-1)).astype(jnp.int32)
    return (segment, offset)

def rotary(values, position, heads):
    row_count = values.shape[0]
    half_dim = HEAD_DIM // 2
    inverse = THETA ** (-(jnp.arange(half_dim, dtype=jnp.float32) * (2.0 / HEAD_DIM)))
    angles = position.astype(jnp.float32)[:, None] * inverse[None, :]
    cosine = jnp.cos(angles)[:, None, :]
    sine_part = jnp.sin(angles)[:, None, :]
    shaped = values.astype(jnp.float32).reshape(row_count, heads, HEAD_DIM)
    first_half = shaped[..., :half_dim]
    second_half = shaped[..., half_dim:]
    turned = jnp.concatenate([first_half * cosine - second_half * sine_part, second_half * cosine + first_half * sine_part], axis=-1)
    return turned.reshape(row_count, heads * HEAD_DIM).astype(jnp.bfloat16)

def masked_attention(query_rows, key_rows, value_rows, allowed):
    batch_count, row_count = (query_rows.shape[0], query_rows.shape[1])
    col_count = key_rows.shape[1]
    group_size = QHEADS // KVHEADS
    query_wide = query_rows.astype(jnp.float32).reshape(batch_count, row_count, KVHEADS, group_size, HEAD_DIM)
    key_wide = key_rows.astype(jnp.float32).reshape(batch_count, col_count, KVHEADS, HEAD_DIM)
    value_wide = value_rows.astype(jnp.float32).reshape(batch_count, col_count, KVHEADS, HEAD_DIM)
    scores = jnp.einsum('brkgd,bckd->bkgrc', query_wide, key_wide, precision=lax.Precision.HIGHEST) * (1.0 / math.sqrt(HEAD_DIM))
    mask_wide = allowed[:, None, None]
    scores = jnp.where(mask_wide, scores, NEGATIVE)
    row_max = lax.optimization_barrier(jnp.max(scores, axis=-1, keepdims=True))
    weight = jnp.where(mask_wide, jnp.exp(scores - row_max), 0.0)
    weight_sum = lax.optimization_barrier(jnp.sum(weight, axis=-1))
    rounded = lax.optimization_barrier(weight.astype(jnp.bfloat16)).astype(jnp.float32)
    blended = jnp.einsum('bkgrc,bckd->brkgd', rounded, value_wide, precision=lax.Precision.HIGHEST)
    blended = blended / jnp.transpose(weight_sum, (0, 3, 1, 2))[..., None]
    return blended.reshape(batch_count, row_count, QHEADS * HEAD_DIM).astype(jnp.bfloat16)

def reference(q_short, k_short, v_short, short_lengths, bin_dest, q_long, k_long, v_long, long_lengths):
    query_width = QHEADS * HEAD_DIM
    key_width = KVHEADS * HEAD_DIM
    segment, position = doc_layout(short_lengths, BIN_LEN)
    short_query = rotary(q_short, position.reshape(-1), QHEADS)
    short_key = rotary(k_short, position.reshape(-1), KVHEADS)
    per_rank = N_CTX * BINS
    token_order = jnp.arange(BIN_LEN, dtype=jnp.int32)
    causal = token_order[None, :] <= token_order[:, None]

    def one_rank(bundle):
        query_b, key_b, value_b, segment_b = bundle
        allowed = (segment_b[:, :, None] == segment_b[:, None, :]) & causal[None]
        return masked_attention(query_b, key_b, value_b, allowed)
    short_bins = lax.map(one_rank, (short_query.reshape(N_DP, per_rank, BIN_LEN, query_width), short_key.reshape(N_DP, per_rank, BIN_LEN, key_width), v_short.reshape(N_DP, per_rank, BIN_LEN, key_width), segment.reshape(N_DP, per_rank, BIN_LEN)))
    short_bins = short_bins.reshape(N_DP * per_rank, BIN_LEN, query_width)
    ranks = jnp.arange(N_DP, dtype=jnp.int32)
    incidence = jnp.any(bin_dest[..., None] == ranks[None, None, None, :], axis=2).astype(jnp.int32)
    before = (jnp.cumsum(incidence, axis=0).astype(jnp.int32) - incidence).astype(jnp.int32)
    slot = jnp.take_along_axis(before, bin_dest.astype(jnp.int32), axis=2).astype(jnp.int32)
    ctx_ids = jnp.arange(N_CTX, dtype=jnp.int32)[None, :, None]
    dest_block = ((bin_dest * N_CTX + ctx_ids) * BINS + slot).astype(jnp.int32).reshape(-1)
    out_short = jnp.zeros((N_DP * per_rank, BIN_LEN, query_width), jnp.bfloat16).at[dest_block].set(short_bins)
    out_short = out_short.reshape(-1, query_width)
    region = N_CTX * SPAN

    def one_region(bundle):
        query_r, key_r, value_r, lengths = bundle
        segment_r, position_r = doc_layout(lengths, region)
        query_rot = rotary(query_r, position_r, QHEADS)
        key_rot = rotary(key_r, position_r, KVHEADS)
        key_index = jnp.arange(region, dtype=jnp.int32)

        def one_block(block_start):
            query_block = lax.dynamic_slice_in_dim(query_rot, block_start, SPAN, 0)
            segment_block = lax.dynamic_slice_in_dim(segment_r, block_start, SPAN, 0)
            query_index = block_start + jnp.arange(SPAN, dtype=jnp.int32)
            allowed = (segment_block[:, None] == segment_r[None, :]) & (key_index[None, :] <= query_index[:, None])
            return masked_attention(query_block[None], key_rot[None], value_r[None], allowed[None])[0]
        blocks = lax.map(one_block, jnp.arange(N_CTX, dtype=jnp.int32) * SPAN)
        return blocks.reshape(region, query_width)
    out_long = lax.map(one_region, (q_long.reshape(N_DP, region, query_width), k_long.reshape(N_DP, region, key_width), v_long.reshape(N_DP, region, key_width), long_lengths))
    return (out_short, out_long.reshape(-1, query_width))
```

```python
import functools
import math

import jax
import jax.numpy as jnp
import numpy as np
from jax import lax
from jax.experimental import pallas as pl
from jax.experimental.pallas import tpu as pltpu
from jax.sharding import PartitionSpec as P

QHEADS = 16
KVHEADS = 4
GROUP = QHEADS // KVHEADS
HEAD_DIM = 128
HALF = HEAD_DIM // 2
WIDE = GROUP * HEAD_DIM
BIN_LEN = 64
BINS = 2
THETA = 500000.0
NEGATIVE = -1e30
SCALE = math.log2(math.e) / math.sqrt(HEAD_DIM)

NZ, NX, NY = 8, 4, 8
CHUNKS = KVHEADS
STEPS = 8
DIRS = 4
OWN = 2 * CHUNKS
POOL = OWN + DIRS * STEPS
ROUTE = DIRS * STEPS + CHUNKS
HOPS = NY // 2
Y_SENDS = 3 * KVHEADS + KVHEADS // 2
MESH = pl.DeviceIdType.MESH


def moved(place, direction):
    z, x = divmod(place, NX)
    if direction < 2:
        x = (x + (1, -1)[direction]) % NX
    else:
        z = (z + (1, -1)[direction - 2]) % NZ
    return z * NX + x


@functools.cache
def route_table():
    table = np.zeros((NZ * NX, NZ * NX, ROUTE), np.int32)
    for mask in range(NZ * NX):
        packets = []
        for place in range(NZ * NX):
            z, x = divmod(place, NX)
            goal_z, goal_x = divmod(place ^ mask, NX)
            for chunk in range(CHUNKS):
                dz, dx = (goal_z - z) % NZ, (goal_x - x) % NX
                if dz > NZ // 2 or (dz == NZ // 2 and chunk % 2):
                    dz -= NZ
                if dx > NX // 2 or (dx == NX // 2 and (chunk // (2 if mask // NX == NZ // 2 else 1)) % 2):
                    dx -= NX
                packets.append([place, dz, dx, chunk, chunk])
        step = 0
        while any(p[1] or p[2] for p in packets):
            order = sorted(packets, key=lambda p: (-abs(p[1]) - abs(p[2]), -abs(p[1]), p[4]))
            taken, moves = set(), []
            for p in order:
                options = []
                if p[1]:
                    options.append(2 if p[1] > 0 else 3)
                if p[2]:
                    options.append(0 if p[2] > 0 else 1)
                for d in options:
                    if (p[0], d) not in taken:
                        taken.add((p[0], d))
                        moves.append((p, d))
                        break
            for p, d in moves:
                table[mask, p[0], step * DIRS + d] = p[3]
                p[0] = moved(p[0], d)
                p[2 if d < 2 else 1] -= (1, -1)[d % 2]
                p[3] = OWN + DIRS * step + d
            step += 1
        assert step <= STEPS
        for p in packets:
            table[mask, p[0], DIRS * STEPS + p[4]] = p[3]
    return table


def doc_start(lengths, index):
    first = lengths[..., 0:1]
    second = first + lengths[..., 1:2]
    return jnp.where(index >= second, second, jnp.where(index >= first, first, 0))


def turn_tables(position):
    inverse = THETA ** (-(jnp.arange(HALF, dtype=jnp.float32) * (2.0 / HEAD_DIM)))
    angles = position.astype(jnp.float32)[:, None] * inverse[None, :]
    cosine, sine = jnp.cos(angles), jnp.sin(angles)
    return jnp.concatenate([cosine, cosine], 1), jnp.concatenate([-sine, sine], 1)


def rotated(block, cosine, sine):
    wide = block.astype(jnp.float32)
    return (wide * cosine + pltpu.roll(wide, HALF, 1) * sine).astype(jnp.bfloat16)


def columns(g, width):
    return pl.ds(pl.multiple_of(g * width, width), width)


def turned_heads(q_ref, rows, g, cosine, sine):
    block = q_ref[rows, columns(g, WIDE)]
    parts = [block[:, i * HEAD_DIM : (i + 1) * HEAD_DIM] for i in range(GROUP)]
    return jnp.concatenate([rotated(part, cosine, sine) for part in parts], 0)


def side_by_side(block):
    rows = block.shape[0] // GROUP
    return jnp.concatenate([block[i * rows : (i + 1) * rows] for i in range(GROUP)], 1)


def score(query, key):
    return SCALE * lax.dot_general(
        query, key, (((1,), (1,)), ((), ())), preferred_element_type=jnp.float32
    )


def kernel(
    route_ref, order_ref, q_short, k_short, v_short, short_cos, short_sin, short_start,
    q_long, k_long, v_long, long_cos, long_sin, long_start,
    out_short, out_long,
    pool0, pool1, stage, landing, kv, query, top, total, acc, bias_ref,
    mate_send, mate_recv, route_send, route_recv, y_send, y_recv,
):
    dp, ctx = lax.axis_index("dp"), lax.axis_index("ctx")
    core, x, z = dp % 2, (dp // 2) % NX, dp // (2 * NX)
    span = q_long.shape[0]

    def at(z_to, x_to):
        return (((z_to + NZ) % NZ * NX + (x_to + NX) % NX) * 2 + core, ctx)

    mate = (dp + 1 - 2 * core, ctx)
    routes = [at(z, x + 1), at(z, x - 1), at(z + 1, x), at(z - 1, x)]
    rings = [(dp, (ctx + 1) % NY), (dp, (ctx + NY - 1) % NY)]

    barrier = pltpu.get_barrier_semaphore()
    for other in [mate, *routes, *rings]:
        pl.semaphore_signal(barrier, inc=1, device_id=other, device_id_type=MESH)
    pl.semaphore_wait(barrier, 3 + DIRS)

    def copy(source, target, send, recv, other):
        return pltpu.make_async_remote_copy(
            src_ref=source, dst_ref=target, send_sem=send, recv_sem=recv,
            device_id=other, device_id_type=MESH,
        )

    def ring_copy(n, way):
        hop = n // KVHEADS
        g = (n + way * (KVHEADS // 2)) % KVHEADS
        if way == 0:
            source, target = hop, hop + 1
        else:
            source = jnp.where(hop == 0, 0, hop + HOPS)
            target = jnp.where(hop == HOPS - 1, HOPS, hop + HOPS + 1)
        return copy(
            kv.at[source, g], kv.at[target, g], y_send.at[way, n], y_recv.at[way, n], rings[way]
        )

    cosine, sine = long_cos[...], long_sin[...]
    for g in range(KVHEADS):
        kv[0, g, :, :HEAD_DIM] = rotated(
            k_long[:, g * HEAD_DIM : (g + 1) * HEAD_DIM], cosine, sine
        )
        kv[0, g, :, HEAD_DIM:] = v_long[:, g * HEAD_DIM : (g + 1) * HEAD_DIM]
    for n in range(KVHEADS):
        for way in range(2):
            ring_copy(n, way).start()

    pools = [pool0, pool1]

    def mate_copy(j, g):
        return copy(
            pools[j].at[g], pools[j].at[CHUNKS + g], mate_send.at[j, g], mate_recv.at[j, g], mate
        )

    for j in range(BINS):
        rows = slice(j * BIN_LEN, (j + 1) * BIN_LEN)
        bin_cos, bin_sin = short_cos[rows], short_sin[rows]
        row = lax.broadcasted_iota(jnp.int32, (BIN_LEN, BIN_LEN), 0)
        col = lax.broadcasted_iota(jnp.int32, (BIN_LEN, BIN_LEN), 1)
        allowed = (col >= short_start[rows]) & (col <= row)
        bias = jnp.where(allowed, 0.0, NEGATIVE)
        bias = jnp.concatenate([bias] * GROUP, 0)
        for g in range(CHUNKS):
            lanes = slice(g * HEAD_DIM, (g + 1) * HEAD_DIM)
            heads = turned_heads(q_short, rows, g, bin_cos, bin_sin)
            scores = score(heads, rotated(k_short[rows, lanes], bin_cos, bin_sin)) + bias
            weight = jnp.exp2(scores - jnp.max(scores, axis=1, keepdims=True))
            blended = jnp.dot(
                weight.astype(jnp.bfloat16), v_short[rows, lanes], preferred_element_type=jnp.float32
            )
            blended = blended / jnp.sum(weight, axis=1, keepdims=True)
            pools[j][g] = side_by_side(blended.astype(jnp.bfloat16))
            mate_copy(j, g).start()

    shift = [0] + [-h for h in range(1, HOPS + 1)] + [h for h in range(1, NY - HOPS)]
    row = lax.broadcasted_iota(jnp.int32, (span, span), 0) + ctx * span
    col = lax.broadcasted_iota(jnp.int32, (span, span), 1)
    for i in range(NY):
        key_index = col + (ctx + NY + shift[i]) % NY * span
        allowed = (key_index >= long_start[...]) & (key_index <= row)
        bias_ref[i] = jnp.where(allowed, 0.0, NEGATIVE)

    def attend(g, blocks):
        first, last = 0 in blocks, HOPS in blocks
        if first:
            query[g] = turned_heads(q_long, slice(None), g, long_cos[...], long_sin[...])
        keys = jnp.concatenate([kv[i, g, :, :HEAD_DIM] for i in blocks], 0)
        values = jnp.concatenate([kv[i, g, :, HEAD_DIM:] for i in blocks], 0)
        bias = jnp.concatenate([bias_ref[i] for i in blocks], 1)
        for i in range(GROUP):
            part = pl.ds(i * span, span)
            scores = score(query[g, part], keys) + bias
            peak = jnp.max(scores, axis=1, keepdims=True)
            if not first:
                old = top[g, part]
                peak = jnp.maximum(peak, old[:, :1])
            weight = jnp.exp2(scores - peak)
            amount = jnp.sum(weight, axis=1, keepdims=True)
            blended = jnp.dot(
                weight.astype(jnp.bfloat16), values, preferred_element_type=jnp.float32
            )
            if not first:
                shrink = jnp.exp2(old[:, :1] - peak)
                amount = amount + total[g, part][:, :1] * shrink
                blended = blended + acc[g, part] * shrink
            if last:
                out_long[:, columns(g * GROUP + i, HEAD_DIM)] = (blended / amount).astype(
                    jnp.bfloat16
                )
            else:
                top[g, part] = jnp.broadcast_to(peak, (span, HEAD_DIM))
                total[g, part] = jnp.broadcast_to(amount, (span, HEAD_DIM))
                acc[g, part] = blended

    near = [0, 1, HOPS + 1]
    middle = [2, HOPS + 2]
    far = [3, HOPS, HOPS + 3]

    def route_copy(slot, d):
        return copy(
            stage.at[slot, d], landing.at[slot, d], route_send.at[slot, d], route_recv.at[slot, d],
            routes[d],
        )

    def entry(j, place):
        index = route_ref[j, place]
        return index + jnp.where(index < CHUNKS, order_ref[1 + j], 0)

    def collect(j, step):
        slot = BINS * step + j
        for d in range(DIRS):
            route_copy(slot, d).wait_recv()
            pools[j][OWN + DIRS * step + d] = landing[slot, d]

    def send(j, step):
        slot = BINS * step + j
        for d in range(DIRS):
            stage[slot, d] = pools[j][entry(j, step * DIRS + d)]
            route_copy(slot, d).start()

    def ring(n):
        for way in range(2):
            ring_copy(n, way).wait_recv()

        @pl.when(n + KVHEADS < Y_SENDS)
        def _():
            for way in range(2):
                ring_copy(n + KVHEADS, way).start()

    for j in range(BINS):
        for g in range(CHUNKS):
            mate_copy(j, g).wait_recv()
        send(j, 0)
        ring(j)

    def pair(step, work):
        for j in range(BINS):
            collect(j, step - 1)
            send(j, step)
            ring(BINS * step + j)
            work(BINS * step + j)

    @pl.loop(1, 2)
    def _(step):
        pair(step, lambda n: None)

    @pl.loop(2, 4)
    def _(step):
        pair(step, lambda n: attend(n - 4, near))

    @pl.loop(4, 6)
    def _(step):
        pair(step, lambda n: attend(n - 8, middle))

    @pl.loop(6, 7)
    def _(step):
        def work(n):
            attend(n - 12, far)
            attend(n - 10, far)

        pair(step, work)

    for j in range(BINS):
        collect(j, STEPS - 2)
        send(j, STEPS - 1)
    for j in range(BINS):
        collect(j, STEPS - 1)

    swap = order_ref[0]
    for g in range(CHUNKS):
        chunk0 = pool0[entry(0, DIRS * STEPS + g)]
        chunk1 = pool1[entry(1, DIRS * STEPS + g)]
        lanes = slice(g * WIDE, (g + 1) * WIDE)
        out_short[:BIN_LEN, lanes] = jnp.where(swap == 0, chunk0, chunk1)
        out_short[BIN_LEN:, lanes] = jnp.where(swap == 0, chunk1, chunk0)

    for j in range(BINS):
        for g in range(CHUNKS):
            mate_copy(j, g).wait_send()

    @pl.loop(0, BINS * STEPS)
    def _(slot):
        for d in range(DIRS):
            route_copy(slot, d).wait_send()

    @pl.loop(0, Y_SENDS)
    def _(n):
        for way in range(2):
            ring_copy(n, way).wait_send()


VMEM = pl.BlockSpec(memory_space=pltpu.VMEM)
SMEM = pl.BlockSpec(memory_space=pltpu.SMEM)


def local(q_short, k_short, v_short, short_lengths, bin_dest, q_long, k_long, v_long, long_lengths):
    dp_index = lax.axis_index("dp")
    ctx_index = lax.axis_index("ctx")
    span = q_long.shape[0]

    my_rows = ctx_index * span + jnp.arange(span, dtype=jnp.int32)
    my_start = doc_start(long_lengths[0], my_rows)
    long_cos, long_sin = turn_tables(my_rows - my_start)

    home = lax.dynamic_index_in_dim(short_lengths[:, 0], dp_index, 0, keepdims=False)
    token = jnp.arange(BIN_LEN, dtype=jnp.int32)[None, :]
    start = doc_start(home, token)
    short_cos, short_sin = turn_tables((token - start).reshape(-1))

    masks = bin_dest[0, 0]
    route = jnp.asarray(route_table())[masks // 2, dp_index // 2]
    swap = ((dp_index ^ masks[0]) > (dp_index ^ masks[1])).astype(jnp.int32)
    order = jnp.concatenate([swap[None], masks % 2 * CHUNKS])

    bf16, f32 = jnp.bfloat16, jnp.float32
    slots = BINS * STEPS
    dma = pltpu.SemaphoreType.DMA
    out_short, out_long = pl.pallas_call(
        kernel,
        out_shape=[jax.ShapeDtypeStruct(q_short.shape, bf16), jax.ShapeDtypeStruct(q_long.shape, bf16)],
        in_specs=[SMEM, SMEM] + [VMEM] * 12,
        out_specs=[VMEM, VMEM],
        scratch_shapes=[
            pltpu.VMEM((POOL, BIN_LEN, WIDE), bf16),
            pltpu.VMEM((POOL, BIN_LEN, WIDE), bf16),
            pltpu.VMEM((slots, DIRS, BIN_LEN, WIDE), bf16),
            pltpu.VMEM((slots, DIRS, BIN_LEN, WIDE), bf16),
            pltpu.VMEM((NY, KVHEADS, span, 2 * HEAD_DIM), bf16),
            pltpu.VMEM((KVHEADS, GROUP * span, HEAD_DIM), bf16),
            pltpu.VMEM((KVHEADS, GROUP * span, HEAD_DIM), f32),
            pltpu.VMEM((KVHEADS, GROUP * span, HEAD_DIM), f32),
            pltpu.VMEM((KVHEADS, GROUP * span, HEAD_DIM), f32),
            pltpu.VMEM((NY, span, span), f32),
            dma((BINS, CHUNKS)),
            dma((BINS, CHUNKS)),
            dma((slots, DIRS)),
            dma((slots, DIRS)),
            dma((2, Y_SENDS)),
            dma((2, Y_SENDS)),
        ],
        compiler_params=pltpu.CompilerParams(
            collective_id=0, has_side_effects=True, vmem_limit_bytes=48 * 2**20
        ),
    )(
        route, order, q_short, k_short, v_short, short_cos, short_sin, start.reshape(-1)[:, None],
        q_long, k_long, v_long, long_cos, long_sin, my_start[:, None],
    )
    return (out_short, out_long)


def solution(mesh):
    in_specs = (
        P(("dp", "ctx"), None),
        P(("dp", "ctx"), None),
        P(("dp", "ctx"), None),
        P(None, "ctx", None, None),
        P(None, "ctx", None),
        P(("dp", "ctx"), None),
        P(("dp", "ctx"), None),
        P(("dp", "ctx"), None),
        P("dp", None),
    )
    out_specs = (P(("dp", "ctx"), None), P(("dp", "ctx"), None))
    return jax.shard_map(local, mesh=mesh, in_specs=in_specs, out_specs=out_specs, check_vma=False)
```

```python
import functools
import math

import jax
import jax.numpy as jnp
import numpy as np
from jax import lax
from jax.experimental import pallas as pl
from jax.experimental.pallas import tpu as pltpu
from jax.sharding import PartitionSpec as P

QHEADS = 16
KVHEADS = 4
GROUP = QHEADS // KVHEADS
HEAD_DIM = 128
HALF = HEAD_DIM // 2
WIDE = GROUP * HEAD_DIM
BIN_LEN = 64
BINS = 2
THETA = 500000.0
NEGATIVE = -1e30
SCALE = math.log2(math.e) / math.sqrt(HEAD_DIM)

NZ, NX, NY = 8, 4, 8
HALVES = 2
PART = WIDE // HALVES
CHUNKS = KVHEADS
STEPS = 8
DIRS = 4
OWN = 2 * CHUNKS
POOL = OWN + DIRS * STEPS
ROUTE = 64
HOPS = NY // 2
Y_SENDS = 3 * KVHEADS + KVHEADS // 2
MESH = pl.DeviceIdType.MESH


def moved(place, direction):
    z, x = divmod(place, NX)
    if direction < 2:
        x = (x + (1, -1)[direction]) % NX
    else:
        z = (z + (1, -1)[direction - 2]) % NZ
    return z * NX + x


@functools.cache
def route_table():
    table = np.zeros((NZ * NX, NZ * NX, ROUTE), np.int32)
    for mask in range(NZ * NX):
        packets = []
        for place in range(NZ * NX):
            z, x = divmod(place, NX)
            goal_z, goal_x = divmod(place ^ mask, NX)
            for chunk in range(CHUNKS):
                dz, dx = (goal_z - z) % NZ, (goal_x - x) % NX
                if dz > NZ // 2 or (dz == NZ // 2 and chunk % 2):
                    dz -= NZ
                if dx > NX // 2 or (dx == NX // 2 and (chunk // (2 if mask // NX == NZ // 2 else 1)) % 2):
                    dx -= NX
                packets.append([place, dz, dx, chunk, chunk])
        step = 0
        while any(p[1] or p[2] for p in packets):
            order = sorted(packets, key=lambda p: (-abs(p[1]) - abs(p[2]), -abs(p[1]), p[4]))
            taken, moves = set(), []
            for p in order:
                options = []
                if p[1]:
                    options.append(2 if p[1] > 0 else 3)
                if p[2]:
                    options.append(0 if p[2] > 0 else 1)
                for d in options:
                    if (p[0], d) not in taken:
                        taken.add((p[0], d))
                        moves.append((p, d))
                        break
            for p, d in moves:
                table[mask, p[0], step * DIRS + d] = p[3]
                p[0] = moved(p[0], d)
                p[2 if d < 2 else 1] -= (1, -1)[d % 2]
                p[3] = OWN + DIRS * step + d
            step += 1
        assert step <= STEPS
        for p in packets:
            table[mask, p[0], DIRS * STEPS + p[4]] = p[3]
    return np.ascontiguousarray(table.transpose(1, 0, 2)).reshape(-1)


INVERSE = np.power(THETA, -np.arange(HALF, dtype=np.float64) * (2.0 / HEAD_DIM)).astype(np.float32)
QUARTER1 = float(np.float32(1.5703125))
QUARTER2 = float(np.float32(math.floor((math.pi / 2 - QUARTER1) * 2**23) / 2**23))
QUARTER3 = float(np.float32(math.pi / 2 - QUARTER1 - QUARTER2))


def turns(angle):
    quarters = jnp.floor(angle * (2.0 / math.pi) + 0.5)
    r = ((angle - quarters * QUARTER1) - quarters * QUARTER2) - quarters * QUARTER3
    s = r * r
    sine = 1.0 / 362880
    for k in (-1.0 / 5040, 1.0 / 120, -1.0 / 6):
        sine = sine * s + k
    sine = r + r * s * sine
    cosine = 1.0 / 40320
    for k in (-1.0 / 720, 1.0 / 24, -0.5, 1.0):
        cosine = cosine * s + k
    count = quarters.astype(jnp.int32)
    odd, turned = (count & 1) == 1, (count & 2) == 2
    first, second = jnp.where(odd, sine, cosine), jnp.where(odd, cosine, sine)
    flip = turned != odd
    return jnp.where(flip, -first, first), jnp.where(turned, -second, second)


def doc_start(first, second, index):
    return jnp.where(index >= second, second, jnp.where(index >= first, first, 0))


def rotated(block, cosine, sine):
    wide = block.astype(jnp.float32)
    return (wide * cosine + pltpu.roll(wide, HALF, 1) * sine).astype(jnp.bfloat16)


def lanes(i, width):
    return slice(i * width, (i + 1) * width)


def stacked_heads(q_ref, g, cosine, sine):
    heads = range(g * GROUP, (g + 1) * GROUP)
    return jnp.concatenate([rotated(q_ref[:, lanes(h, HEAD_DIM)], cosine, sine) for h in heads], 0)


def score(query, key):
    return SCALE * lax.dot_general(
        query, key, (((1,), (1,)), ((), ())), preferred_element_type=jnp.float32
    )


def blend(weight, values):
    wide = jnp.concatenate([values, jnp.ones_like(values)], 1)
    return jnp.dot(weight.astype(jnp.bfloat16), wide, preferred_element_type=jnp.float32)


def kernel(
    table_any, inverse_any, lengths_any, dest_any, long_lengths_any,
    k_long_any, v_long_any, q_short_any, k_short_any, v_short_any, q_long_any,
    out_short, out_long,
    table, dest, inverse, lengths, long_lengths,
    k_long, v_long, q_short, k_short, v_short, q_long,
    pool00, pool01, pool10, pool11, stage, landing, kv, query, top, acc, bias_ref,
    load_sem, mate_send, mate_recv, route_send, route_recv, y_send, y_recv,
):
    dp, ctx = lax.axis_index("dp"), lax.axis_index("ctx")
    core, x, z = dp % 2, (dp // 2) % NX, dp // (2 * NX)
    span = q_long.shape[0]

    loads = [
        (table_any.at[pl.ds(pl.multiple_of((dp // 2) * (NZ * NX * ROUTE), NZ * NX * ROUTE), NZ * NX * ROUTE)], table),
        (dest_any, dest),
        (inverse_any, inverse),
        (lengths_any, lengths),
        (long_lengths_any, long_lengths),
        (k_long_any, k_long),
        (v_long_any, v_long),
        (q_short_any, q_short),
        (k_short_any, k_short),
        (v_short_any, v_short),
        (q_long_any, q_long),
    ]
    loads = [pltpu.make_async_copy(a, b, load_sem.at[i]) for i, (a, b) in enumerate(loads)]
    for load in loads[2:] + loads[:2]:
        load.start()

    def at(z_to, x_to):
        return (((z_to + NZ) % NZ * NX + (x_to + NX) % NX) * 2 + core, ctx)

    mate = (dp + 1 - 2 * core, ctx)
    routes = [at(z, x + 1), at(z, x - 1), at(z + 1, x), at(z - 1, x)]
    rings = [(dp, (ctx + 1) % NY), (dp, (ctx + NY - 1) % NY)]

    barrier = pltpu.get_barrier_semaphore()
    for other in [mate, *routes, *rings]:
        pl.semaphore_signal(barrier, inc=1, device_id=other, device_id_type=MESH)

    def copy(source, target, send, recv, other):
        return pltpu.make_async_remote_copy(
            src_ref=source, dst_ref=target, send_sem=send, recv_sem=recv,
            device_id=other, device_id_type=MESH,
        )

    def ring_copy(n, way):
        hop = n // KVHEADS
        g = (n + way * (KVHEADS // 2)) % KVHEADS
        if way == 0:
            source, target = hop, hop + 1
        else:
            source = jnp.where(hop == 0, 0, hop + HOPS)
            target = jnp.where(hop == HOPS - 1, HOPS, hop + HOPS + 1)
        return copy(
            kv.at[source, g], kv.at[target, g], y_send.at[way, n], y_recv.at[way, n], rings[way]
        )

    for load in loads[2:5]:
        load.wait()
    row = lax.broadcasted_iota(jnp.int32, (span, HEAD_DIM), 0)
    lane = lax.broadcasted_iota(jnp.int32, (span, HEAD_DIM), 1)
    mine = lax.broadcasted_iota(jnp.int32, lengths.shape[2:], 1) == dp
    home = [jnp.sum(jnp.where(mine, lengths[0, d], 0), axis=1, keepdims=True) for d in range(2)]
    first = jnp.where(row < BIN_LEN, home[0][0:1], home[0][1:2])
    second = first + jnp.where(row < BIN_LEN, home[1][0:1], home[1][1:2])
    token = row % BIN_LEN
    short_start = doc_start(first, second, token)
    my_row = row + ctx * span
    first = long_lengths[:, 0:1]
    long_start = doc_start(first, first + long_lengths[:, 1:2], my_row)
    position = jnp.where(lane < HALF, token - short_start, my_row - long_start)
    cosine, sine = turns(position.astype(jnp.float32) * inverse[...])
    cosine_swap, sine_swap = pltpu.roll(cosine, HALF, 1), pltpu.roll(sine, HALF, 1)
    low = lane < HALF
    short_cos, short_sin = jnp.where(low, cosine, cosine_swap), jnp.where(low, -sine, sine_swap)
    long_cos, long_sin = jnp.where(low, cosine_swap, cosine), jnp.where(low, -sine_swap, sine)

    for load in loads[5:7]:
        load.wait()
    for g in range(KVHEADS):
        kv[0, g, :, :HEAD_DIM] = rotated(k_long[:, lanes(g, HEAD_DIM)], long_cos, long_sin)
        kv[0, g, :, HEAD_DIM:] = v_long[:, lanes(g, HEAD_DIM)]
    pl.semaphore_wait(barrier, 3 + DIRS)
    for n in range(KVHEADS):
        for way in range(2):
            ring_copy(n, way).start()

    pools = [pool00, pool01, pool10, pool11]
    streams = range(BINS * HALVES)

    def mate_copy(t, g):
        return copy(
            pools[t].at[pl.ds(g, 2)], pools[t].at[pl.ds(CHUNKS + g, 2)],
            mate_send.at[t, g // 2], mate_recv.at[t, g // 2], mate,
        )

    for load in loads[7:10]:
        load.wait()
    allowed = (lane >= short_start + (row - token)) & (lane <= row)
    bias = jnp.where(allowed, 0.0, NEGATIVE)
    bias = jnp.concatenate([bias] * GROUP, 0)
    for g in range(CHUNKS):
        heads = stacked_heads(q_short, g, short_cos, short_sin)
        keys = rotated(k_short[:, lanes(g, HEAD_DIM)], short_cos, short_sin)
        scores = score(heads, keys) + bias
        weight = jnp.exp2(scores - jnp.max(scores, axis=1, keepdims=True))
        blended = blend(weight, v_short[:, lanes(g, HEAD_DIM)])
        result = (blended[:, :HEAD_DIM] / blended[:, HEAD_DIM:]).astype(jnp.bfloat16)
        for j in range(BINS):
            for h in range(HALVES):
                parts = [2 * h * span + j * BIN_LEN, (2 * h + 1) * span + j * BIN_LEN]
                pools[j * HALVES + h][g] = jnp.concatenate(
                    [result[p : p + BIN_LEN] for p in parts], 1
                )
        if g % 2:
            for t in streams:
                mate_copy(t, g - 1).start()

    for load in loads[:2]:
        load.wait()
    masks = [dest[0, j, 0] for j in range(BINS)]

    def entry(t, place):
        mask = masks[t // HALVES]
        index = table[(mask >> 1) * ROUTE + place]
        return index + jnp.where(index < CHUNKS, (mask & 1) * CHUNKS, 0)

    def route_copy(slot, d):
        return copy(
            stage.at[slot, d], landing.at[slot, d], route_send.at[slot], route_recv.at[slot], routes[d]
        )

    def all_of(slot):
        return copy(stage.at[slot], landing.at[slot], route_send.at[slot], route_recv.at[slot], routes[0])

    def collect(t, step):
        slot = len(streams) * step + t
        all_of(slot).wait_recv()
        for d in range(DIRS):
            pools[t][OWN + DIRS * step + d] = landing[slot, d]

    def send(t, step):
        slot = len(streams) * step + t
        for d in range(DIRS):
            stage[slot, d] = pools[t][entry(t, step * DIRS + d)]
            route_copy(slot, d).start()

    def ring(n):
        for way in range(2):
            ring_copy(n, way).wait_recv()

        @pl.when(n + KVHEADS < Y_SENDS)
        def _():
            for way in range(2):
                ring_copy(n + KVHEADS, way).start()

    shift = [0] + [-h for h in range(1, HOPS + 1)] + [h for h in range(1, NY - HOPS)]

    def prepare(t):
        query[t] = stacked_heads(q_long, t, long_cos, long_sin)
        for i in (2 * t, 2 * t + 1):
            key_index = lane + (ctx + NY + shift[i]) % NY * span
            allowed = (key_index >= long_start) & (key_index <= my_row)
            bias_ref[i] = jnp.where(allowed, 0.0, NEGATIVE)

    rows = GROUP * span // 2

    def attend(g, half, blocks):
        begins, ends = 0 in blocks, HOPS in blocks
        part = pl.ds(half * rows, rows)
        keys = jnp.concatenate([kv[i, g, :, :HEAD_DIM] for i in blocks], 0)
        values = jnp.concatenate([kv[i, g, :, HEAD_DIM:] for i in blocks], 0)
        bias = jnp.concatenate([bias_ref[i] for i in blocks], 1)
        scores = score(query[g, part], keys) + jnp.concatenate([bias] * (GROUP // 2), 0)
        peak = jnp.max(scores, axis=1, keepdims=True)
        if not begins:
            old = top[g, part]
            peak = jnp.maximum(peak, old[:, :1])
        blended = blend(jnp.exp2(scores - peak), values)
        if not begins:
            blended = blended + acc[g, part] * jnp.exp2(old[:, :1] - peak)
        if ends:
            result = (blended[:, :HEAD_DIM] / blended[:, HEAD_DIM:]).astype(jnp.bfloat16)
            result = jnp.concatenate([result[i * span : (i + 1) * span] for i in range(GROUP // 2)], 1)
            width = GROUP // 2 * HEAD_DIM
            out_long[:, pl.ds(pl.multiple_of((g * 2 + half) * width, width), width)] = result
        else:
            top[g, part] = jnp.broadcast_to(peak, (rows, HEAD_DIM))
            acc[g, part] = blended

    near = [0, 1, HOPS + 1]
    middle = [2, HOPS + 2]
    far = [3, HOPS, HOPS + 3]

    def one_step(step, work, with_ring=True):
        for t in streams:
            collect(t, step - 1)
            send(t, step)
            if t % 2 == 0 and with_ring:
                ring(BINS * step + t // 2)
            work(t)
            all_of(len(streams) * (step - 1) + t).wait_send()

    loads[10].wait()
    for t in streams:
        for g in (0, 2):
            mate_copy(t, g).wait()
        send(t, 0)
        if t % 2 == 0:
            ring(t // 2)
        prepare(t)

    @pl.loop(1, 2)
    def _(step):
        one_step(step, lambda t: None)

    def unit(step, t, blocks):
        u = len(streams) * step + t
        attend(u // 2, u % 2, blocks)

    @pl.loop(2, 4)
    def _(step):
        one_step(step, lambda t: unit(step - 2, t, near))

    @pl.loop(4, 6)
    def _(step):
        one_step(step, lambda t: unit(step - 4, t, middle))

    one_step(6, lambda t: attend([0, 0, 2, 2][t], t % 2, far))
    one_step(7, lambda t: attend([1, 1, 3, 3][t], t % 2, far), False)

    for t in streams:
        collect(t, STEPS - 1)
    swap = (dp ^ masks[0]) > (dp ^ masks[1])
    for h in range(HALVES):
        for g in range(CHUNKS):
            chunk0 = pools[h][entry(h, DIRS * STEPS + g)]
            chunk1 = pools[HALVES + h][entry(HALVES + h, DIRS * STEPS + g)]
            part = lanes(g * HALVES + h, PART)
            out_short[:BIN_LEN, part] = jnp.where(swap, chunk1, chunk0)
            out_short[BIN_LEN:, part] = jnp.where(swap, chunk0, chunk1)

    for t in streams:
        all_of(len(streams) * (STEPS - 1) + t).wait_send()

    @pl.loop(0, Y_SENDS)
    def _(n):
        for way in range(2):
            ring_copy(n, way).wait_send()


VMEM = pl.BlockSpec(memory_space=pltpu.VMEM)
ANY = pl.BlockSpec(memory_space=pl.ANY)


def local(q_short, k_short, v_short, short_lengths, bin_dest, q_long, k_long, v_long, long_lengths):
    span = q_long.shape[0]
    table = jnp.asarray(route_table())
    inverse = jnp.asarray(np.concatenate([INVERSE, INVERSE])[None, :])
    lengths = jnp.transpose(short_lengths, (1, 3, 2, 0))
    dest = jnp.transpose(bin_dest, (1, 2, 0))

    bf16, f32, i32 = jnp.bfloat16, jnp.float32, jnp.int32
    slots = BINS * HALVES * STEPS
    dma = pltpu.SemaphoreType.DMA
    inputs = [k_long, v_long, q_short, k_short, v_short, q_long]
    out_short, out_long = pl.pallas_call(
        kernel,
        out_shape=[jax.ShapeDtypeStruct(q_short.shape, bf16), jax.ShapeDtypeStruct(q_long.shape, bf16)],
        in_specs=[ANY] * 11,
        out_specs=[VMEM, VMEM],
        scratch_shapes=[
            pltpu.SMEM((NZ * NX * ROUTE,), i32),
            pltpu.SMEM(dest.shape, i32),
            pltpu.VMEM(inverse.shape, f32),
            pltpu.VMEM(lengths.shape, i32),
            pltpu.VMEM(long_lengths.shape, i32),
            *[pltpu.VMEM(a.shape, bf16) for a in inputs],
            *[pltpu.VMEM((POOL, BIN_LEN, PART), bf16)] * (BINS * HALVES),
            pltpu.VMEM((slots, DIRS, BIN_LEN, PART), bf16),
            pltpu.VMEM((slots, DIRS, BIN_LEN, PART), bf16),
            pltpu.VMEM((NY, KVHEADS, span, 2 * HEAD_DIM), bf16),
            pltpu.VMEM((KVHEADS, GROUP * span, HEAD_DIM), bf16),
            pltpu.VMEM((KVHEADS, GROUP * span, HEAD_DIM), f32),
            pltpu.VMEM((KVHEADS, GROUP * span, 2 * HEAD_DIM), f32),
            pltpu.VMEM((NY, span, span), f32),
            dma((11,)),
            dma((BINS * HALVES, CHUNKS // 2)),
            dma((BINS * HALVES, CHUNKS // 2)),
            dma((slots,)),
            dma((slots,)),
            dma((2, Y_SENDS)),
            dma((2, Y_SENDS)),
        ],
        compiler_params=pltpu.CompilerParams(
            collective_id=0, has_side_effects=True, vmem_limit_bytes=56 * 2**20
        ),
    )(table, inverse, lengths, dest, long_lengths, *inputs)
    return (out_short, out_long)


def solution(mesh):
    in_specs = (
        P(("dp", "ctx"), None),
        P(("dp", "ctx"), None),
        P(("dp", "ctx"), None),
        P(None, "ctx", None, None),
        P(None, "ctx", None),
        P(("dp", "ctx"), None),
        P(("dp", "ctx"), None),
        P(("dp", "ctx"), None),
        P("dp", None),
    )
    out_specs = (P(("dp", "ctx"), None), P(("dp", "ctx"), None))
    return jax.shard_map(local, mesh=mesh, in_specs=in_specs, out_specs=out_specs, check_vma=False)
```

```python
import functools
import math

import jax
import jax.numpy as jnp
import numpy as np
from jax import lax
from jax.experimental import pallas as pl
from jax.experimental.pallas import tpu as pltpu
from jax.sharding import PartitionSpec as P

QHEADS = 16
KVHEADS = 4
GROUP = QHEADS // KVHEADS
HEAD_DIM = 128
HALF = HEAD_DIM // 2
WIDE = GROUP * HEAD_DIM
BIN_LEN = 64
BINS = 2
THETA = 500000.0
NEGATIVE = -1e30
SCALE = math.log2(math.e) / math.sqrt(HEAD_DIM)

NZ, NX, NY = 8, 4, 8
HALVES = 1
EARLY = BIN_LEN // 2
ROWS = EARLY // HALVES
CUTS = (0, HEAD_DIM, 2 * HEAD_DIM, 4 * HEAD_DIM, 5 * HEAD_DIM)
CHUNKS = KVHEADS
STEPS = 8
DIRS = 4
OWN = 2 * CHUNKS
POOL = OWN + DIRS * STEPS
PIECES = 4
ROUTE = 64
HOPS = NY // 2
Y_SENDS = 3 * KVHEADS + KVHEADS // 2
MESH = pl.DeviceIdType.MESH


def moved(place, direction):
    z, x = divmod(place, NX)
    if direction < 2:
        x = (x + (1, -1)[direction]) % NX
    else:
        z = (z + (1, -1)[direction - 2]) % NZ
    return z * NX + x


@functools.cache
def route_table():
    table = np.zeros((NZ * NX, NZ * NX, ROUTE), np.int32)
    for mask in range(NZ * NX):
        packets = []
        for place in range(NZ * NX):
            z, x = divmod(place, NX)
            goal_z, goal_x = divmod(place ^ mask, NX)
            for chunk in range(CHUNKS):
                dz, dx = (goal_z - z) % NZ, (goal_x - x) % NX
                if dz > NZ // 2 or (dz == NZ // 2 and chunk % 2):
                    dz -= NZ
                if dx > NX // 2 or (dx == NX // 2 and (chunk // (2 if mask // NX == NZ // 2 else 1)) % 2):
                    dx -= NX
                packets.append([place, dz, dx, chunk, chunk])
        step = 0
        while any(p[1] or p[2] for p in packets):
            order = sorted(packets, key=lambda p: (-abs(p[1]) - abs(p[2]), -abs(p[1]), p[4]))
            taken, moves = set(), []
            for p in order:
                options = []
                if p[1]:
                    options.append(2 if p[1] > 0 else 3)
                if p[2]:
                    options.append(0 if p[2] > 0 else 1)
                for d in options:
                    if (p[0], d) not in taken:
                        taken.add((p[0], d))
                        moves.append((p, d))
                        break
            for p, d in moves:
                table[mask, p[0], step * DIRS + d] = p[3]
                p[0] = moved(p[0], d)
                p[2 if d < 2 else 1] -= (1, -1)[d % 2]
                p[3] = OWN + DIRS * step + d
            step += 1
        assert step <= STEPS
        for p in packets:
            table[mask, p[0], DIRS * STEPS + p[4]] = p[3]
    return np.ascontiguousarray(table.transpose(1, 0, 2)).reshape(-1)


INVERSE = np.power(THETA, -np.arange(HALF, dtype=np.float64) * (2.0 / HEAD_DIM)).astype(np.float32)
QUARTER1 = float(np.float32(1.5703125))
QUARTER2 = float(np.float32(math.floor((math.pi / 2 - QUARTER1) * 2**23) / 2**23))
QUARTER3 = float(np.float32(math.pi / 2 - QUARTER1 - QUARTER2))


def turns(angle):
    quarters = jnp.floor(angle * (2.0 / math.pi) + 0.5)
    r = ((angle - quarters * QUARTER1) - quarters * QUARTER2) - quarters * QUARTER3
    s = r * r
    sine = 1.0 / 362880
    for k in (-1.0 / 5040, 1.0 / 120, -1.0 / 6):
        sine = sine * s + k
    sine = r + r * s * sine
    cosine = 1.0 / 40320
    for k in (-1.0 / 720, 1.0 / 24, -0.5, 1.0):
        cosine = cosine * s + k
    count = quarters.astype(jnp.int32)
    odd, turned = (count & 1) == 1, (count & 2) == 2
    first, second = jnp.where(odd, sine, cosine), jnp.where(odd, cosine, sine)
    flip = turned != odd
    return jnp.where(flip, -first, first), jnp.where(turned, -second, second)


def doc_start(first, second, index):
    return jnp.where(index >= second, second, jnp.where(index >= first, first, 0))


def rotated(block, cosine, sine):
    wide = block.astype(jnp.float32)
    return (wide * cosine + pltpu.roll(wide, HALF, 1) * sine).astype(jnp.bfloat16)


def lanes(i, width):
    return slice(i * width, (i + 1) * width)


def lanes_at(i, width):
    return pl.ds(i * width, width)


def stacked_heads(q_ref, g, cosine, sine):
    heads = range(g * GROUP, (g + 1) * GROUP)
    return jnp.concatenate([rotated(q_ref[:, lanes(h, HEAD_DIM)], cosine, sine) for h in heads], 0)


def score(query, key):
    return SCALE * lax.dot_general(
        query, key, (((1,), (1,)), ((), ())), preferred_element_type=jnp.float32
    )


def blend(weight, values):
    wide = jnp.concatenate([values, jnp.ones_like(values)], 1)
    return jnp.dot(weight.astype(jnp.bfloat16), wide, preferred_element_type=jnp.float32)


def kernel(
    table_any, inverse_any, lengths_any, dest_any, long_lengths_any,
    k_long_any, v_long_any, q_short_any, k_short_any, v_short_any, q_long_any,
    bin_out, long_out,
    table, dest, inverse, lengths, long_lengths,
    k_long, v_long, q_short, k_short, v_short, q_long,
    pool_refs, stage, landing, kv, query, top, acc, bias_ref, bin_result, long_result,
    load_sem, out_sem, mate_send, mate_recv, route_send, route_recv, y_send, y_recv,
):
    dp, ctx = lax.axis_index("dp"), lax.axis_index("ctx")
    core, x, z = dp % 2, (dp // 2) % NX, dp // (2 * NX)
    span = q_long.shape[0]

    loads = [
        (table_any.at[pl.ds(pl.multiple_of((dp // 2) * (NZ * NX * ROUTE), NZ * NX * ROUTE), NZ * NX * ROUTE)], table),
        (dest_any, dest),
        (inverse_any, inverse),
        (lengths_any, lengths),
        (long_lengths_any, long_lengths),
        (k_long_any, k_long),
        (v_long_any, v_long),
        (q_short_any, q_short),
        (k_short_any, k_short),
        (v_short_any, v_short),
        (q_long_any, q_long),
    ]
    loads = [pltpu.make_async_copy(a, b, load_sem.at[i]) for i, (a, b) in enumerate(loads)]
    for load in loads[2:] + loads[:2]:
        load.start()

    def at(z_to, x_to):
        return (((z_to + NZ) % NZ * NX + (x_to + NX) % NX) * 2 + core, ctx)

    mate = (dp + 1 - 2 * core, ctx)
    routes = [at(z, x + 1), at(z, x - 1), at(z + 1, x), at(z - 1, x)]
    rings = [(dp, (ctx + 1) % NY), (dp, (ctx + NY - 1) % NY)]

    barrier = pltpu.get_barrier_semaphore()
    for other in [mate, *routes, *rings]:
        pl.semaphore_signal(barrier, inc=1, device_id=other, device_id_type=MESH)

    def copy(source, target, send, recv, other):
        return pltpu.make_async_remote_copy(
            src_ref=source, dst_ref=target, send_sem=send, recv_sem=recv,
            device_id=other, device_id_type=MESH,
        )

    def ring_copy(n, way):
        hop = n // KVHEADS
        g = (n + way * (KVHEADS // 2)) % KVHEADS
        if way == 0:
            source, target = hop, hop + 1
        else:
            source = jnp.where(hop == 0, 0, hop + HOPS)
            target = jnp.where(hop == HOPS - 1, HOPS, hop + HOPS + 1)
        return copy(
            kv.at[source, g], kv.at[target, g], y_send.at[way, n], y_recv.at[way, n], rings[way]
        )

    for load in loads[2:5]:
        load.wait()
    row = lax.broadcasted_iota(jnp.int32, (span, HEAD_DIM), 0)
    lane = lax.broadcasted_iota(jnp.int32, (span, HEAD_DIM), 1)
    mine = lax.broadcasted_iota(jnp.int32, lengths.shape[2:], 1) == dp
    home = [jnp.sum(jnp.where(mine, lengths[0, d], 0), axis=1, keepdims=True) for d in range(2)]
    first = jnp.where(row < BIN_LEN, home[0][0:1], home[0][1:2])
    second = first + jnp.where(row < BIN_LEN, home[1][0:1], home[1][1:2])
    token = row % BIN_LEN
    short_start = doc_start(first, second, token)
    my_row = row + ctx * span
    first = long_lengths[:, 0:1]
    long_start = doc_start(first, first + long_lengths[:, 1:2], my_row)
    position = jnp.where(lane < HALF, token - short_start, my_row - long_start)
    cosine, sine = turns(position.astype(jnp.float32) * inverse[...])
    cosine_swap, sine_swap = pltpu.roll(cosine, HALF, 1), pltpu.roll(sine, HALF, 1)
    low = lane < HALF
    short_cos, short_sin = jnp.where(low, cosine, cosine_swap), jnp.where(low, -sine, sine_swap)
    long_cos, long_sin = jnp.where(low, cosine_swap, cosine), jnp.where(low, -sine_swap, sine)

    for load in loads[5:7]:
        load.wait()
    for g in range(KVHEADS):
        kv[0, g, :, :HEAD_DIM] = rotated(k_long[:, lanes(g, HEAD_DIM)], long_cos, long_sin)
        kv[0, g, :, HEAD_DIM:] = v_long[:, lanes(g, HEAD_DIM)]
    pl.semaphore_wait(barrier, 3 + DIRS)
    for n in range(KVHEADS):
        for way in range(2):
            ring_copy(n, way).start()

    pools = [*pool_refs]
    streams = range(BINS * HALVES)

    def mate_copy(t):
        return copy(
            pools[t].at[pl.ds(0, CHUNKS)], pools[t].at[pl.ds(CHUNKS, CHUNKS)],
            mate_send.at[t], mate_recv.at[t], mate,
        )

    for load in loads[7:10]:
        load.wait()

    def bias_of(rows, reach):
        index = lane[rows] % reach
        allowed = (index >= short_start[rows]) & (index <= token[rows])
        return jnp.concatenate([jnp.where(allowed, 0.0, NEGATIVE)] * GROUP, 0)

    spot = lane[:EARLY]
    for j in range(BINS):
        rows = slice(j * BIN_LEN, (j + 1) * BIN_LEN)
        early = slice(j * BIN_LEN, j * BIN_LEN + EARLY)
        late = slice(j * BIN_LEN + EARLY, (j + 1) * BIN_LEN)
        early_bias, late_bias = bias_of(early, EARLY), bias_of(late, BIN_LEN)
        early_scores, late_scores = [], []
        for g in range(CHUNKS):
            heads = [
                rotated(q_short[rows, lanes(g * GROUP + i, HEAD_DIM)], short_cos[rows], short_sin[rows])
                for i in range(GROUP)
            ]
            key = rotated(k_short[rows, lanes(g, HEAD_DIM)], short_cos[rows], short_sin[rows])
            first = jnp.concatenate([q[:EARLY] for q in heads], 0)
            second = jnp.concatenate([q[EARLY:] for q in heads], 0)
            keys = jnp.concatenate([key[:EARLY]] * GROUP, 0)
            early_scores.append(score(first, keys) + early_bias)
            late_scores.append(score(second, jnp.concatenate([key] * 2, 0)) + late_bias)
        scores = jnp.concatenate(early_scores + late_scores, 0)
        weight = jnp.exp2(scores - jnp.max(scores, axis=1, keepdims=True))
        for g in range(CHUNKS):
            w = [weight[(g * GROUP + i) * EARLY :][:EARLY] for i in range(GROUP)]
            packed = w[0]
            for i in range(1, GROUP):
                packed = jnp.where(spot // EARLY == i, w[i], packed)
            w = [weight[((CHUNKS + g) * GROUP + i) * EARLY :][:EARLY] for i in range(GROUP)]
            left = jnp.where(spot < BIN_LEN, w[0], w[1])
            right = jnp.where(spot < BIN_LEN, w[2], w[3])
            pieces = [
                packed.astype(jnp.bfloat16), v_short[early, lanes(g, HEAD_DIM)],
                jnp.concatenate([left, right], 1).astype(jnp.bfloat16), v_short[late, lanes(g, HEAD_DIM)],
            ]
            for h in range(HALVES):
                for i, piece in enumerate(pieces):
                    part = slice(CUTS[i], CUTS[i + 1])
                    pools[j * HALVES + h][g, :, part] = piece[h * ROWS : (h + 1) * ROWS]
        for h in range(HALVES):
            mate_copy(j * HALVES + h).start()

    for load in loads[:2]:
        load.wait()
    masks = [dest[0, j, 0] for j in range(BINS)]

    def entry(t, place):
        mask = masks[t // HALVES]
        index = table[(mask >> 1) * ROUTE + place]
        return index + jnp.where(index < CHUNKS, (mask & 1) * CHUNKS, 0)

    def route_copy(slot, d):
        return copy(
            stage.at[slot, d], landing.at[slot, d], route_send.at[slot], route_recv.at[slot], routes[d]
        )

    def all_of(slot):
        return copy(stage.at[slot], landing.at[slot], route_send.at[slot], route_recv.at[slot], routes[0])

    def collect(t, step):
        slot = len(streams) * step + t
        all_of(slot).wait_recv()
        for d in range(DIRS):
            pools[t][OWN + DIRS * step + d] = landing[slot, d]

    def send(t, step):
        slot = len(streams) * step + t
        for d in range(DIRS):
            stage[slot, d] = pools[t][entry(t, step * DIRS + d)]
            route_copy(slot, d).start()

    def ring(n):
        for way in range(2):
            ring_copy(n, way).wait_recv()

        @pl.when(n + KVHEADS < Y_SENDS)
        def _():
            for way in range(2):
                ring_copy(n + KVHEADS, way).start()

    shift = [0] + [-h for h in range(1, HOPS + 1)] + [h for h in range(1, NY - HOPS)]

    def prepare(t):
        query[t] = stacked_heads(q_long, t, long_cos, long_sin)
        for i in (2 * t, 2 * t + 1):
            key_index = lane + (ctx + NY + shift[i]) % NY * span
            allowed = (key_index >= long_start) & (key_index <= my_row)
            bias_ref[i] = jnp.where(allowed, 0.0, NEGATIVE)

    def attend(heads, blocks):
        begins, ends = 0 in blocks, HOPS in blocks
        bias = jnp.concatenate([bias_ref[i] for i in blocks], 1)
        bias = jnp.concatenate([bias] * GROUP, 0)
        keys = [jnp.concatenate([kv[i, g, :, :HEAD_DIM] for i in blocks], 0) for g in heads]
        values = [jnp.concatenate([kv[i, g, :, HEAD_DIM:] for i in blocks], 0) for g in heads]
        scores = [score(query[g], k) + bias for g, k in zip(heads, keys)]
        peaks = [jnp.max(s, axis=1, keepdims=True) for s in scores]
        if not begins:
            olds = [top[g][:, :1] for g in heads]
            peaks = [jnp.maximum(peak, old) for peak, old in zip(peaks, olds)]
        weights = [jnp.exp2(s - peak) for s, peak in zip(scores, peaks)]
        blended = [blend(w, v) for w, v in zip(weights, values)]
        for n, g in enumerate(heads):
            both = blended[n]
            if not begins:
                both = both + acc[g] * jnp.exp2(olds[n] - peaks[n])
            if ends:
                result = (both[:, :HEAD_DIM] / both[:, HEAD_DIM:]).astype(jnp.bfloat16)
                for i in range(GROUP):
                    long_result[:, lanes(g * GROUP + i, HEAD_DIM)] = result[i * span : (i + 1) * span]
                long_copy(g).start()
            else:
                top[g] = jnp.broadcast_to(peaks[n], top.shape[1:])
                acc[g] = both

    def long_copy(g):
        return pltpu.make_async_copy(
            long_result.at[:, lanes_at(g, WIDE)], long_out.at[:, lanes_at(g, WIDE)], out_sem.at[BINS * CHUNKS + g]
        )

    def bin_copy(m, g):
        return pltpu.make_async_copy(bin_result.at[m, g], bin_out.at[m, g], out_sem.at[m * CHUNKS + g])

    near = [0, 1, HOPS + 1]
    middle = [2, HOPS + 2]
    third = [3, HOPS + 3]
    far = [HOPS]

    def one_step(step, work, rings=(True, True)):
        for t in streams:
            phase, half = 2 * step + t // HALVES, t % HALVES
            if not (isinstance(step, int) and step == 0):
                collect(t, step - 1)
            send(t, step)
            if half == 0 and rings[t // HALVES]:
                ring(phase - 1)
            work(phase, [half] if HALVES > 1 else [0, 1])
            if not (isinstance(step, int) and step == 0):
                all_of(len(streams) * (step - 1) + t).wait_send()

    def preparing(phase, halves):
        if 0 in halves:
            prepare(phase)

    def attending(pick, blocks):
        def work(phase, halves):
            if 0 in halves:
                attend(pick(phase), blocks)

        return work

    loads[10].wait()
    for t in streams:
        mate_copy(t).wait()
    one_step(0, preparing, (False, True))
    one_step(1, preparing)

    @pl.loop(2, 4)
    def _(step):
        one_step(step, attending(lambda p: [p - 4], near))

    @pl.loop(4, 6)
    def _(step):
        one_step(step, attending(lambda p: [p - 8], middle))

    one_step(6, attending(lambda p: {12: (0, 1), 13: (2, 3)}[p], third))
    one_step(7, attending(lambda p: {14: (0, 2), 15: (1, 3)}[p], far), (True, False))

    for t in streams:
        collect(t, STEPS - 1)

    swap = (dp ^ masks[0]) > (dp ^ masks[1])
    for g in range(CHUNKS):
        chunks = [
            jnp.concatenate(
                [pools[t][entry(t, DIRS * STEPS + g)] for t in range(j * HALVES, (j + 1) * HALVES)], 0
            )
            for j in range(BINS)
        ]
        bin_result[0, g] = jnp.where(swap, chunks[1], chunks[0])
        bin_result[1, g] = jnp.where(swap, chunks[0], chunks[1])
        for m in range(BINS):
            bin_copy(m, g).start()

    for t in streams:
        all_of(len(streams) * (STEPS - 1) + t).wait_send()

    @pl.loop(0, Y_SENDS)
    def _(n):
        for way in range(2):
            ring_copy(n, way).wait_send()

    for g in range(CHUNKS):
        long_copy(g).wait()
        for m in range(BINS):
            bin_copy(m, g).wait()


def finish(bins_any, long_any, out_short, out_long, bins, short, long, sem_in, sem_out):
    rows = long.shape[0] // PIECES

    def long_copies(p):
        part = pl.ds(p * rows, rows)
        return (
            pltpu.make_async_copy(long_any.at[part], long.at[part], sem_in.at[BINS + p]),
            pltpu.make_async_copy(long.at[part], out_long.at[part], sem_out.at[BINS + p]),
        )

    def short_copies(m):
        part = pl.ds(m * BIN_LEN, BIN_LEN)
        return (
            pltpu.make_async_copy(bins_any.at[m], bins.at[m], sem_in.at[m]),
            pltpu.make_async_copy(short.at[part], out_short.at[part], sem_out.at[m]),
        )

    pieces = [short_copies(m) for m in range(BINS)] + [long_copies(p) for p in range(PIECES)]
    for load, _ in pieces:
        load.start()

    spot = lax.broadcasted_iota(jnp.int32, (EARLY, HEAD_DIM), 1)

    def chosen(test):
        return jnp.where(test, 1.0, 0.0).astype(jnp.bfloat16)

    quarter = [chosen(spot // EARLY == i) for i in range(GROUP)]
    side = [chosen(spot < BIN_LEN), chosen(spot >= BIN_LEN)]

    def finished(weight, values):
        blended = blend(weight, values)
        result = (blended[:, :HEAD_DIM] / blended[:, HEAD_DIM:]).astype(jnp.bfloat16)
        return jnp.concatenate([result[i * EARLY : (i + 1) * EARLY] for i in range(GROUP)], 1)

    for m in range(BINS):
        pieces[m][0].wait()
        for g in range(CHUNKS):
            chunk = bins[m, g]
            first, first_v, second, second_v = [chunk[:, CUTS[i] : CUTS[i + 1]] for i in range(4)]
            early = jnp.concatenate([first * q for q in quarter], 0)
            late = [second[:, lanes(i // 2, HEAD_DIM)] * side[i % 2] for i in range(GROUP)]
            late = jnp.concatenate(late, 0)
            start = m * BIN_LEN
            short[start : start + EARLY, lanes(g, WIDE)] = finished(
                early, jnp.concatenate([first_v] * GROUP, 0)
            )
            short[start + EARLY : start + BIN_LEN, lanes(g, WIDE)] = finished(
                late, jnp.concatenate([first_v, second_v] * 2, 0)
            )
        if m == 0:
            for load, store in pieces[BINS:]:
                load.wait()
                store.start()
        pieces[m][1].start()
    for _, store in pieces:
        store.wait()


HBM = pl.BlockSpec(memory_space=pltpu.HBM)


def local(q_short, k_short, v_short, short_lengths, bin_dest, q_long, k_long, v_long, long_lengths):
    span = q_long.shape[0]
    table = jnp.asarray(route_table())
    inverse = jnp.asarray(np.concatenate([INVERSE, INVERSE])[None, :])
    lengths = jnp.transpose(short_lengths, (1, 3, 2, 0))
    dest = jnp.transpose(bin_dest, (1, 2, 0))

    bf16, f32, i32 = jnp.bfloat16, jnp.float32, jnp.int32
    slots = BINS * HALVES * STEPS
    dma = pltpu.SemaphoreType.DMA
    inputs = [k_long, v_long, q_short, k_short, v_short, q_long]
    bins_shape = (BINS, CHUNKS, EARLY, CUTS[-1])
    bins, long = pl.pallas_call(
        kernel,
        out_shape=[jax.ShapeDtypeStruct(bins_shape, bf16), jax.ShapeDtypeStruct(q_long.shape, bf16)],
        in_specs=[HBM] * 11,
        out_specs=[HBM, HBM],
        scratch_shapes=[
            pltpu.SMEM((NZ * NX * ROUTE,), i32),
            pltpu.SMEM(dest.shape, i32),
            pltpu.VMEM(inverse.shape, f32),
            pltpu.VMEM(lengths.shape, i32),
            pltpu.VMEM(long_lengths.shape, i32),
            *[pltpu.VMEM(a.shape, bf16) for a in inputs],
            [pltpu.VMEM((POOL, ROWS, CUTS[-1]), bf16)] * (BINS * HALVES),
            pltpu.VMEM((slots, DIRS, ROWS, CUTS[-1]), bf16),
            pltpu.VMEM((slots, DIRS, ROWS, CUTS[-1]), bf16),
            pltpu.VMEM((NY, KVHEADS, span, 2 * HEAD_DIM), bf16),
            pltpu.VMEM((KVHEADS, GROUP * span, HEAD_DIM), bf16),
            pltpu.VMEM((KVHEADS, GROUP * span, HEAD_DIM), f32),
            pltpu.VMEM((KVHEADS, GROUP * span, 2 * HEAD_DIM), f32),
            pltpu.VMEM((NY, span, span), f32),
            pltpu.VMEM(bins_shape, bf16),
            pltpu.VMEM(q_long.shape, bf16),
            dma((11,)),
            dma((BINS * CHUNKS + KVHEADS,)),
            dma((BINS * HALVES,)),
            dma((BINS * HALVES,)),
            dma((slots,)),
            dma((slots,)),
            dma((2, Y_SENDS)),
            dma((2, Y_SENDS)),
        ],
        compiler_params=pltpu.CompilerParams(
            collective_id=0, has_side_effects=True, vmem_limit_bytes=56 * 2**20
        ),
    )(table, inverse, lengths, dest, long_lengths, *inputs)
    return pl.pallas_call(
        finish,
        out_shape=[jax.ShapeDtypeStruct(q_short.shape, bf16), jax.ShapeDtypeStruct(q_long.shape, bf16)],
        in_specs=[HBM, HBM],
        out_specs=[HBM, HBM],
        scratch_shapes=[
            pltpu.VMEM(bins_shape, bf16),
            pltpu.VMEM(q_short.shape, bf16),
            pltpu.VMEM(q_long.shape, bf16),
            dma((BINS + PIECES,)),
            dma((BINS + PIECES,)),
        ],
        compiler_params=pltpu.CompilerParams(vmem_limit_bytes=56 * 2**20),
    )(bins, long)


def solution(mesh):
    in_specs = (
        P(("dp", "ctx"), None),
        P(("dp", "ctx"), None),
        P(("dp", "ctx"), None),
        P(None, "ctx", None, None),
        P(None, "ctx", None),
        P(("dp", "ctx"), None),
        P(("dp", "ctx"), None),
        P(("dp", "ctx"), None),
        P("dp", None),
    )
    out_specs = (P(("dp", "ctx"), None), P(("dp", "ctx"), None))
    return jax.shard_map(local, mesh=mesh, in_specs=in_specs, out_specs=out_specs, check_vma=False)
```

```python
import functools
import math

import jax
import jax.numpy as jnp
import numpy as np
from jax import lax
from jax.experimental import pallas as pl
from jax.experimental.pallas import tpu as pltpu
from jax.sharding import PartitionSpec as P

QHEADS = 16
KVHEADS = 4
GROUP = QHEADS // KVHEADS
HEAD_DIM = 128
HALF = HEAD_DIM // 2
WIDE = GROUP * HEAD_DIM
BIN_LEN = 64
BINS = 2
THETA = 500000.0
NEGATIVE = -1e30
SCALE = math.log2(math.e) / math.sqrt(HEAD_DIM)

NZ, NX, NY = 8, 4, 8
HALVES = 1
EARLY = BIN_LEN // 2
ROWS = EARLY // HALVES
CUTS = (0, HEAD_DIM, 2 * HEAD_DIM, 4 * HEAD_DIM, 5 * HEAD_DIM)
CHUNKS = KVHEADS
STEPS = 8
DIRS = 4
OWN = 2 * CHUNKS
POOL = OWN + DIRS * STEPS
PIECES = 4
ROUTE = 64
HOPS = NY // 2
Y_SENDS = 3 * KVHEADS + KVHEADS // 2
MESH = pl.DeviceIdType.MESH


def moved(place, direction):
    z, x = divmod(place, NX)
    if direction < 2:
        x = (x + (1, -1)[direction]) % NX
    else:
        z = (z + (1, -1)[direction - 2]) % NZ
    return z * NX + x


@functools.cache
def route_table():
    table = np.zeros((NZ * NX, NZ * NX, ROUTE), np.int32)
    for mask in range(NZ * NX):
        packets = []
        for place in range(NZ * NX):
            z, x = divmod(place, NX)
            goal_z, goal_x = divmod(place ^ mask, NX)
            for chunk in range(CHUNKS):
                dz, dx = (goal_z - z) % NZ, (goal_x - x) % NX
                if dz > NZ // 2 or (dz == NZ // 2 and chunk % 2):
                    dz -= NZ
                if dx > NX // 2 or (dx == NX // 2 and (chunk // (2 if mask // NX == NZ // 2 else 1)) % 2):
                    dx -= NX
                packets.append([place, dz, dx, chunk, chunk])
        step = 0
        while any(p[1] or p[2] for p in packets):
            order = sorted(packets, key=lambda p: (-abs(p[1]) - abs(p[2]), -abs(p[1]), p[4]))
            taken, moves = set(), []
            for p in order:
                options = []
                if p[1]:
                    options.append(2 if p[1] > 0 else 3)
                if p[2]:
                    options.append(0 if p[2] > 0 else 1)
                for d in options:
                    if (p[0], d) not in taken:
                        taken.add((p[0], d))
                        moves.append((p, d))
                        break
            for p, d in moves:
                table[mask, p[0], step * DIRS + d] = p[3]
                p[0] = moved(p[0], d)
                p[2 if d < 2 else 1] -= (1, -1)[d % 2]
                p[3] = OWN + DIRS * step + d
            step += 1
        assert step <= STEPS
        for p in packets:
            table[mask, p[0], DIRS * STEPS + p[4]] = p[3]
    return np.ascontiguousarray(table.transpose(1, 0, 2)).reshape(-1)


INVERSE = np.power(THETA, -np.arange(HALF, dtype=np.float64) * (2.0 / HEAD_DIM)).astype(np.float32)
QUARTER1 = float(np.float32(1.5703125))
QUARTER2 = float(np.float32(math.floor((math.pi / 2 - QUARTER1) * 2**23) / 2**23))
QUARTER3 = float(np.float32(math.pi / 2 - QUARTER1 - QUARTER2))


def turns(angle):
    quarters = jnp.floor(angle * (2.0 / math.pi) + 0.5)
    r = ((angle - quarters * QUARTER1) - quarters * QUARTER2) - quarters * QUARTER3
    s = r * r
    sine = 1.0 / 362880
    for k in (-1.0 / 5040, 1.0 / 120, -1.0 / 6):
        sine = sine * s + k
    sine = r + r * s * sine
    cosine = 1.0 / 40320
    for k in (-1.0 / 720, 1.0 / 24, -0.5, 1.0):
        cosine = cosine * s + k
    count = quarters.astype(jnp.int32)
    odd, turned = (count & 1) == 1, (count & 2) == 2
    first, second = jnp.where(odd, sine, cosine), jnp.where(odd, cosine, sine)
    flip = turned != odd
    return jnp.where(flip, -first, first), jnp.where(turned, -second, second)


def doc_start(first, second, index):
    return jnp.where(index >= second, second, jnp.where(index >= first, first, 0))


def rotated(block, cosine, sine):
    wide = block.astype(jnp.float32)
    return (wide * cosine + pltpu.roll(wide, HALF, 1) * sine).astype(jnp.bfloat16)


def lanes(i, width):
    return slice(i * width, (i + 1) * width)


def lanes_at(i, width):
    return pl.ds(i * width, width)


def stacked_heads(q_ref, g, cosine, sine):
    heads = range(g * GROUP, (g + 1) * GROUP)
    return jnp.concatenate([rotated(q_ref[:, lanes(h, HEAD_DIM)], cosine, sine) for h in heads], 0)


def score(query, key):
    return SCALE * lax.dot_general(
        query, key, (((1,), (1,)), ((), ())), preferred_element_type=jnp.float32
    )


def blend(weight, values):
    wide = jnp.concatenate([values, jnp.ones_like(values)], 1)
    return jnp.dot(weight.astype(jnp.bfloat16), wide, preferred_element_type=jnp.float32)


def kernel(
    table_any, inverse_any, lengths_any, dest_any, long_lengths_any,
    k_long_any, v_long_any, q_short_any, k_short_any, v_short_any, q_long_any,
    bin_out, long_out,
    table, dest, inverse, lengths, long_lengths,
    k_long, v_long, q_short, k_short, v_short, q_long,
    pool_refs, stage, landing, kv, query, top, acc, bias_ref, bin_result, long_result,
    load_sem, out_sem, mate_send, mate_recv, route_send, route_recv, y_send, y_recv,
):
    dp, ctx = lax.axis_index("dp"), lax.axis_index("ctx")
    core, x, z = dp % 2, (dp // 2) % NX, dp // (2 * NX)
    span = q_long.shape[0]

    loads = [
        (table_any.at[pl.ds(pl.multiple_of((dp // 2) * (NZ * NX * ROUTE), NZ * NX * ROUTE), NZ * NX * ROUTE)], table),
        (dest_any, dest),
        (inverse_any, inverse),
        (lengths_any, lengths),
        (long_lengths_any, long_lengths),
        (k_long_any, k_long),
        (v_long_any, v_long),
        (q_short_any, q_short),
        (k_short_any, k_short),
        (v_short_any, v_short),
        (q_long_any, q_long),
    ]
    loads = [pltpu.make_async_copy(a, b, load_sem.at[i]) for i, (a, b) in enumerate(loads)]
    for load in loads[2:] + loads[:2]:
        load.start()

    def at(z_to, x_to):
        return (((z_to + NZ) % NZ * NX + (x_to + NX) % NX) * 2 + core, ctx)

    mate = (dp + 1 - 2 * core, ctx)
    routes = [at(z, x + 1), at(z, x - 1), at(z + 1, x), at(z - 1, x)]
    rings = [(dp, (ctx + 1) % NY), (dp, (ctx + NY - 1) % NY)]

    barrier = pltpu.get_barrier_semaphore()
    for other in [mate, *routes, *rings]:
        pl.semaphore_signal(barrier, inc=1, device_id=other, device_id_type=MESH)

    def copy(source, target, send, recv, other):
        return pltpu.make_async_remote_copy(
            src_ref=source, dst_ref=target, send_sem=send, recv_sem=recv,
            device_id=other, device_id_type=MESH,
        )

    def ring_copy(n, way):
        hop = n // KVHEADS
        g = (n + way * (KVHEADS // 2)) % KVHEADS
        if way == 0:
            source, target = hop, hop + 1
        else:
            source = jnp.where(hop == 0, 0, hop + HOPS)
            target = jnp.where(hop == HOPS - 1, HOPS, hop + HOPS + 1)
        return copy(
            kv.at[source, g], kv.at[target, g], y_send.at[way, n], y_recv.at[way, n], rings[way]
        )

    for load in loads[2:5]:
        load.wait()
    row = lax.broadcasted_iota(jnp.int32, (span, HEAD_DIM), 0)
    lane = lax.broadcasted_iota(jnp.int32, (span, HEAD_DIM), 1)
    mine = lax.broadcasted_iota(jnp.int32, lengths.shape[2:], 1) == dp
    home = [jnp.sum(jnp.where(mine, lengths[0, d], 0), axis=1, keepdims=True) for d in range(2)]
    first = jnp.where(row < BIN_LEN, home[0][0:1], home[0][1:2])
    second = first + jnp.where(row < BIN_LEN, home[1][0:1], home[1][1:2])
    token = row % BIN_LEN
    short_start = doc_start(first, second, token)
    my_row = row + ctx * span
    first = long_lengths[:, 0:1]
    long_start = doc_start(first, first + long_lengths[:, 1:2], my_row)
    position = jnp.where(lane < HALF, token - short_start, my_row - long_start)
    cosine, sine = turns(position.astype(jnp.float32) * inverse[...])
    cosine_swap, sine_swap = pltpu.roll(cosine, HALF, 1), pltpu.roll(sine, HALF, 1)
    low = lane < HALF
    short_cos, short_sin = jnp.where(low, cosine, cosine_swap), jnp.where(low, -sine, sine_swap)
    long_cos, long_sin = jnp.where(low, cosine_swap, cosine), jnp.where(low, -sine_swap, sine)

    for load in loads[5:7]:
        load.wait()
    for g in range(KVHEADS):
        kv[0, g, :, :HEAD_DIM] = rotated(k_long[:, lanes(g, HEAD_DIM)], long_cos, long_sin)
        kv[0, g, :, HEAD_DIM:] = v_long[:, lanes(g, HEAD_DIM)]
    pl.semaphore_wait(barrier, 3 + DIRS)
    for n in range(KVHEADS):
        for way in range(2):
            ring_copy(n, way).start()

    pools = [*pool_refs]
    streams = range(BINS * HALVES)

    def mate_copy(t):
        return copy(
            pools[t].at[pl.ds(0, CHUNKS)], pools[t].at[pl.ds(CHUNKS, CHUNKS)],
            mate_send.at[t], mate_recv.at[t], mate,
        )

    for load in loads[7:10]:
        load.wait()

    def bias_of(rows, reach):
        index = lane[rows] % reach
        allowed = (index >= short_start[rows]) & (index <= token[rows])
        return jnp.concatenate([jnp.where(allowed, 0.0, NEGATIVE)] * GROUP, 0)

    spot = lane[:EARLY]
    for j in range(BINS):
        rows = slice(j * BIN_LEN, (j + 1) * BIN_LEN)
        early = slice(j * BIN_LEN, j * BIN_LEN + EARLY)
        late = slice(j * BIN_LEN + EARLY, (j + 1) * BIN_LEN)
        early_bias, late_bias = bias_of(early, EARLY), bias_of(late, BIN_LEN)
        early_scores, late_scores = [], []
        for g in range(CHUNKS):
            heads = [
                rotated(q_short[rows, lanes(g * GROUP + i, HEAD_DIM)], short_cos[rows], short_sin[rows])
                for i in range(GROUP)
            ]
            key = rotated(k_short[rows, lanes(g, HEAD_DIM)], short_cos[rows], short_sin[rows])
            first = jnp.concatenate([q[:EARLY] for q in heads], 0)
            second = jnp.concatenate([q[EARLY:] for q in heads], 0)
            keys = jnp.concatenate([key[:EARLY]] * GROUP, 0)
            early_scores.append(score(first, keys) + early_bias)
            late_scores.append(score(second, jnp.concatenate([key] * 2, 0)) + late_bias)
        scores = jnp.concatenate(early_scores + late_scores, 0)
        weight = jnp.exp2(scores - jnp.max(scores, axis=1, keepdims=True))
        for g in range(CHUNKS):
            w = [weight[(g * GROUP + i) * EARLY :][:EARLY] for i in range(GROUP)]
            packed = w[0]
            for i in range(1, GROUP):
                packed = jnp.where(spot // EARLY == i, w[i], packed)
            w = [weight[((CHUNKS + g) * GROUP + i) * EARLY :][:EARLY] for i in range(GROUP)]
            left = jnp.where(spot < BIN_LEN, w[0], w[1])
            right = jnp.where(spot < BIN_LEN, w[2], w[3])
            pieces = [
                packed.astype(jnp.bfloat16), v_short[early, lanes(g, HEAD_DIM)],
                jnp.concatenate([left, right], 1).astype(jnp.bfloat16), v_short[late, lanes(g, HEAD_DIM)],
            ]
            for h in range(HALVES):
                for i, piece in enumerate(pieces):
                    part = slice(CUTS[i], CUTS[i + 1])
                    pools[j * HALVES + h][g, :, part] = piece[h * ROWS : (h + 1) * ROWS]
        for h in range(HALVES):
            mate_copy(j * HALVES + h).start()

    for load in loads[:2]:
        load.wait()
    masks = [dest[0, j, 0] for j in range(BINS)]

    def entry(t, place):
        mask = masks[t // HALVES]
        index = table[(mask >> 1) * ROUTE + place]
        return index + jnp.where(index < CHUNKS, (mask & 1) * CHUNKS, 0)

    def route_copy(slot, d):
        return copy(
            stage.at[slot, d], landing.at[slot, d], route_send.at[slot], route_recv.at[slot], routes[d]
        )

    def all_of(slot):
        return copy(stage.at[slot], landing.at[slot], route_send.at[slot], route_recv.at[slot], routes[0])

    def collect(t, step):
        slot = len(streams) * step + t
        all_of(slot).wait_recv()
        for d in range(DIRS):
            pools[t][OWN + DIRS * step + d] = landing[slot, d]

    def send(t, step):
        slot = len(streams) * step + t
        for d in range(DIRS):
            stage[slot, d] = pools[t][entry(t, step * DIRS + d)]
            route_copy(slot, d).start()

    def ring(n):
        for way in range(2):
            ring_copy(n, way).wait()
        if n + KVHEADS < Y_SENDS:
            for way in range(2):
                ring_copy(n + KVHEADS, way).start()

    shift = [0] + [-h for h in range(1, HOPS + 1)] + [h for h in range(1, NY - HOPS)]

    def prepare(t):
        query[t] = stacked_heads(q_long, t, long_cos, long_sin)
        for i in (2 * t, 2 * t + 1):
            key_index = lane + (ctx + NY + shift[i]) % NY * span
            allowed = (key_index >= long_start) & (key_index <= my_row)
            bias_ref[i] = jnp.where(allowed, 0.0, NEGATIVE)

    def attend(heads, blocks):
        begins, ends = 0 in blocks, HOPS in blocks
        bias = jnp.concatenate([bias_ref[i] for i in blocks], 1)
        bias = jnp.concatenate([bias] * GROUP, 0)
        keys = [jnp.concatenate([kv[i, g, :, :HEAD_DIM] for i in blocks], 0) for g in heads]
        values = [jnp.concatenate([kv[i, g, :, HEAD_DIM:] for i in blocks], 0) for g in heads]
        scores = [score(query[g], k) + bias for g, k in zip(heads, keys)]
        peaks = [jnp.max(s, axis=1, keepdims=True) for s in scores]
        if not begins:
            olds = [top[g][:, :1] for g in heads]
            peaks = [jnp.maximum(peak, old) for peak, old in zip(peaks, olds)]
        weights = [jnp.exp2(s - peak) for s, peak in zip(scores, peaks)]
        blended = [blend(w, v) for w, v in zip(weights, values)]
        for n, g in enumerate(heads):
            both = blended[n]
            if not begins:
                both = both + acc[g] * jnp.exp2(olds[n] - peaks[n])
            if ends:
                result = (both[:, :HEAD_DIM] / both[:, HEAD_DIM:]).astype(jnp.bfloat16)
                for i in range(GROUP):
                    long_result[:, lanes(g * GROUP + i, HEAD_DIM)] = result[i * span : (i + 1) * span]
                long_copy(g).start()
            else:
                top[g] = jnp.broadcast_to(peaks[n], top.shape[1:])
                acc[g] = both

    def long_copy(g):
        return pltpu.make_async_copy(
            long_result.at[:, lanes_at(g, WIDE)], long_out.at[:, lanes_at(g, WIDE)], out_sem.at[BINS * CHUNKS + g]
        )

    def bin_copy(m, g):
        return pltpu.make_async_copy(bin_result.at[m, g], bin_out.at[m, g], out_sem.at[m * CHUNKS + g])

    near = [0, 1, HOPS + 1]
    middle = [2, HOPS + 2]
    third = [3, HOPS + 3]
    far = [HOPS]

    plan = [
        [(ring, 0), (prepare, 0)],
        [(ring, 1), (prepare, 1)],
        [(prepare, 2), (prepare, 3)],
        [(ring, 2)],
        [(ring, 3), (attend, [0], near)],
        [(ring, 4), (attend, [1], near)],
        [(ring, 5), (attend, [2], near)],
        [(attend, [3], near)],
        [(ring, 6)],
        [(ring, 7), (attend, [0], middle)],
        [(ring, 8), (attend, [1], middle)],
        [(ring, 9), (attend, [2], middle)],
        [(attend, [3], middle)],
        [(ring, 10)],
        [(ring, 11), (attend, [1], third)],
        [(ring, 12), (attend, [3], third)],
    ]
    last = [[(attend, [0], third + far)], [(attend, [2], third + far)]]

    def work(tasks):
        for task, *arguments in tasks:
            task(*arguments)

    loads[10].wait()
    for step in range(STEPS):
        for t in streams:
            if step == 0:
                mate_copy(t).wait()
            else:
                collect(t, step - 1)
            send(t, step)
            if t % HALVES == 0:
                work(plan[2 * step + t // HALVES])
            if step > 0:
                all_of(len(streams) * (step - 1) + t).wait_send()

    for t in streams:
        collect(t, STEPS - 1)
        if t % HALVES == 0:
            work(last[t // HALVES])

    swap = (dp ^ masks[0]) > (dp ^ masks[1])
    for g in range(CHUNKS):
        chunks = [
            jnp.concatenate(
                [pools[t][entry(t, DIRS * STEPS + g)] for t in range(j * HALVES, (j + 1) * HALVES)], 0
            )
            for j in range(BINS)
        ]
        bin_result[0, g] = jnp.where(swap, chunks[1], chunks[0])
        bin_result[1, g] = jnp.where(swap, chunks[0], chunks[1])
        for m in range(BINS):
            bin_copy(m, g).start()
    ring(Y_SENDS - 1)
    attend([1, 3], far)

    for t in streams:
        all_of(len(streams) * (STEPS - 1) + t).wait_send()

    for g in range(CHUNKS):
        long_copy(g).wait()
        for m in range(BINS):
            bin_copy(m, g).wait()


def finish(bins_any, long_any, out_short, out_long, bins, short, long, sem_in, sem_out):
    rows = long.shape[0] // PIECES

    def long_copies(p):
        part = pl.ds(p * rows, rows)
        return (
            pltpu.make_async_copy(long_any.at[part], long.at[part], sem_in.at[BINS + p]),
            pltpu.make_async_copy(long.at[part], out_long.at[part], sem_out.at[BINS + p]),
        )

    def short_copies(m):
        part = pl.ds(m * BIN_LEN, BIN_LEN)
        return (
            pltpu.make_async_copy(bins_any.at[m], bins.at[m], sem_in.at[m]),
            pltpu.make_async_copy(short.at[part], out_short.at[part], sem_out.at[m]),
        )

    pieces = [short_copies(m) for m in range(BINS)] + [long_copies(p) for p in range(PIECES)]
    for load, _ in pieces:
        load.start()

    spot = lax.broadcasted_iota(jnp.int32, (EARLY, HEAD_DIM), 1)

    def chosen(test):
        return jnp.where(test, 1.0, 0.0).astype(jnp.bfloat16)

    quarter = [chosen(spot // EARLY == i) for i in range(GROUP)]
    side = [chosen(spot < BIN_LEN), chosen(spot >= BIN_LEN)]

    def finished(weight, values):
        blended = blend(weight, values)
        result = (blended[:, :HEAD_DIM] / blended[:, HEAD_DIM:]).astype(jnp.bfloat16)
        return jnp.concatenate([result[i * EARLY : (i + 1) * EARLY] for i in range(GROUP)], 1)

    for m in range(BINS):
        pieces[m][0].wait()
        for g in range(CHUNKS):
            chunk = bins[m, g]
            first, first_v, second, second_v = [chunk[:, CUTS[i] : CUTS[i + 1]] for i in range(4)]
            early = jnp.concatenate([first * q for q in quarter], 0)
            late = [second[:, lanes(i // 2, HEAD_DIM)] * side[i % 2] for i in range(GROUP)]
            late = jnp.concatenate(late, 0)
            start = m * BIN_LEN
            short[start : start + EARLY, lanes(g, WIDE)] = finished(
                early, jnp.concatenate([first_v] * GROUP, 0)
            )
            short[start + EARLY : start + BIN_LEN, lanes(g, WIDE)] = finished(
                late, jnp.concatenate([first_v, second_v] * 2, 0)
            )
        if m == 0:
            for load, store in pieces[BINS:]:
                load.wait()
                store.start()
        pieces[m][1].start()
    for _, store in pieces:
        store.wait()


HBM = pl.BlockSpec(memory_space=pltpu.HBM)


def local(q_short, k_short, v_short, short_lengths, bin_dest, q_long, k_long, v_long, long_lengths):
    span = q_long.shape[0]
    table = jnp.asarray(route_table())
    inverse = jnp.asarray(np.concatenate([INVERSE, INVERSE])[None, :])
    lengths = jnp.transpose(short_lengths, (1, 3, 2, 0))
    dest = jnp.transpose(bin_dest, (1, 2, 0))

    bf16, f32, i32 = jnp.bfloat16, jnp.float32, jnp.int32
    slots = BINS * HALVES * STEPS
    dma = pltpu.SemaphoreType.DMA
    inputs = [k_long, v_long, q_short, k_short, v_short, q_long]
    bins_shape = (BINS, CHUNKS, EARLY, CUTS[-1])
    bins, long = pl.pallas_call(
        kernel,
        out_shape=[jax.ShapeDtypeStruct(bins_shape, bf16), jax.ShapeDtypeStruct(q_long.shape, bf16)],
        in_specs=[HBM] * 11,
        out_specs=[HBM, HBM],
        scratch_shapes=[
            pltpu.SMEM((NZ * NX * ROUTE,), i32),
            pltpu.SMEM(dest.shape, i32),
            pltpu.VMEM(inverse.shape, f32),
            pltpu.VMEM(lengths.shape, i32),
            pltpu.VMEM(long_lengths.shape, i32),
            *[pltpu.VMEM(a.shape, bf16) for a in inputs],
            [pltpu.VMEM((POOL, ROWS, CUTS[-1]), bf16)] * (BINS * HALVES),
            pltpu.VMEM((slots, DIRS, ROWS, CUTS[-1]), bf16),
            pltpu.VMEM((slots, DIRS, ROWS, CUTS[-1]), bf16),
            pltpu.VMEM((NY, KVHEADS, span, 2 * HEAD_DIM), bf16),
            pltpu.VMEM((KVHEADS, GROUP * span, HEAD_DIM), bf16),
            pltpu.VMEM((KVHEADS, GROUP * span, HEAD_DIM), f32),
            pltpu.VMEM((KVHEADS, GROUP * span, 2 * HEAD_DIM), f32),
            pltpu.VMEM((NY, span, span), f32),
            pltpu.VMEM(bins_shape, bf16),
            pltpu.VMEM(q_long.shape, bf16),
            dma((11,)),
            dma((BINS * CHUNKS + KVHEADS,)),
            dma((BINS * HALVES,)),
            dma((BINS * HALVES,)),
            dma((slots,)),
            dma((slots,)),
            dma((2, Y_SENDS)),
            dma((2, Y_SENDS)),
        ],
        compiler_params=pltpu.CompilerParams(
            collective_id=0, has_side_effects=True, vmem_limit_bytes=56 * 2**20
        ),
    )(table, inverse, lengths, dest, long_lengths, *inputs)
    return pl.pallas_call(
        finish,
        out_shape=[jax.ShapeDtypeStruct(q_short.shape, bf16), jax.ShapeDtypeStruct(q_long.shape, bf16)],
        in_specs=[HBM, HBM],
        out_specs=[HBM, HBM],
        scratch_shapes=[
            pltpu.VMEM(bins_shape, bf16),
            pltpu.VMEM(q_short.shape, bf16),
            pltpu.VMEM(q_long.shape, bf16),
            dma((BINS + PIECES,)),
            dma((BINS + PIECES,)),
        ],
        compiler_params=pltpu.CompilerParams(vmem_limit_bytes=56 * 2**20),
    )(bins, long)


def solution(mesh):
    in_specs = (
        P(("dp", "ctx"), None),
        P(("dp", "ctx"), None),
        P(("dp", "ctx"), None),
        P(None, "ctx", None, None),
        P(None, "ctx", None),
        P(("dp", "ctx"), None),
        P(("dp", "ctx"), None),
        P(("dp", "ctx"), None),
        P("dp", None),
    )
    out_specs = (P(("dp", "ctx"), None), P(("dp", "ctx"), None))
    return jax.shard_map(local, mesh=mesh, in_specs=in_specs, out_specs=out_specs, check_vma=False)
```

```python
import functools
import math

import jax
import jax.numpy as jnp
import numpy as np
from jax import lax
from jax.experimental import pallas as pl
from jax.experimental.pallas import tpu as pltpu
from jax.sharding import PartitionSpec as P

QHEADS = 16
KVHEADS = 4
GROUP = QHEADS // KVHEADS
HEAD_DIM = 128
HALF = HEAD_DIM // 2
WIDE = GROUP * HEAD_DIM
BIN_LEN = 64
BINS = 2
THETA = 500000.0
NEGATIVE = -1e30
SCALE = math.log2(math.e) / math.sqrt(HEAD_DIM)

NZ, NX, NY = 8, 4, 8
EARLY = BIN_LEN // 2
CUTS = (0, HEAD_DIM, 2 * HEAD_DIM, 4 * HEAD_DIM, 5 * HEAD_DIM)
CHUNKS = KVHEADS
STEPS = 8
DIRS = 4
OWN = 2 * CHUNKS
POOL = OWN + DIRS * STEPS
PIECES = 4
ROUTE = 64
HOPS = NY // 2
Y_SENDS = 3 * KVHEADS + KVHEADS // 2
MESH = pl.DeviceIdType.MESH


def moved(place, direction):
    z, x = divmod(place, NX)
    if direction < 2:
        x = (x + (1, -1)[direction]) % NX
    else:
        z = (z + (1, -1)[direction - 2]) % NZ
    return z * NX + x


@functools.cache
def route_table():
    table = np.zeros((NZ * NX, NZ * NX, ROUTE), np.int32)
    for mask in range(NZ * NX):
        packets = []
        for place in range(NZ * NX):
            z, x = divmod(place, NX)
            goal_z, goal_x = divmod(place ^ mask, NX)
            for chunk in range(CHUNKS):
                dz, dx = (goal_z - z) % NZ, (goal_x - x) % NX
                if dz > NZ // 2 or (dz == NZ // 2 and chunk % 2):
                    dz -= NZ
                if dx > NX // 2 or (dx == NX // 2 and (chunk // (2 if mask // NX == NZ // 2 else 1)) % 2):
                    dx -= NX
                packets.append([place, dz, dx, chunk, chunk])
        step = 0
        while any(p[1] or p[2] for p in packets):
            order = sorted(packets, key=lambda p: (-abs(p[1]) - abs(p[2]), -abs(p[1]), p[4]))
            taken, moves = set(), []
            for p in order:
                options = []
                if p[1]:
                    options.append(2 if p[1] > 0 else 3)
                if p[2]:
                    options.append(0 if p[2] > 0 else 1)
                for d in options:
                    if (p[0], d) not in taken:
                        taken.add((p[0], d))
                        moves.append((p, d))
                        break
            for p, d in moves:
                table[mask, p[0], step * DIRS + d] = p[3]
                p[0] = moved(p[0], d)
                p[2 if d < 2 else 1] -= (1, -1)[d % 2]
                p[3] = OWN + DIRS * step + d
            step += 1
        assert step <= STEPS
        for p in packets:
            table[mask, p[0], DIRS * STEPS + p[4]] = p[3]
    return np.ascontiguousarray(table.transpose(1, 0, 2)).reshape(-1)


INVERSE = np.power(THETA, -np.arange(HALF, dtype=np.float64) * (2.0 / HEAD_DIM)).astype(np.float32)
QUARTER1 = float(np.float32(1.5703125))
QUARTER2 = float(np.float32(math.floor((math.pi / 2 - QUARTER1) * 2**23) / 2**23))
QUARTER3 = float(np.float32(math.pi / 2 - QUARTER1 - QUARTER2))


def turns(angle):
    quarters = jnp.floor(angle * (2.0 / math.pi) + 0.5)
    r = ((angle - quarters * QUARTER1) - quarters * QUARTER2) - quarters * QUARTER3
    s = r * r
    sine = 1.0 / 362880
    for k in (-1.0 / 5040, 1.0 / 120, -1.0 / 6):
        sine = sine * s + k
    sine = r + r * s * sine
    cosine = 1.0 / 40320
    for k in (-1.0 / 720, 1.0 / 24, -0.5, 1.0):
        cosine = cosine * s + k
    count = quarters.astype(jnp.int32)
    odd, turned = (count & 1) == 1, (count & 2) == 2
    first, second = jnp.where(odd, sine, cosine), jnp.where(odd, cosine, sine)
    flip = turned != odd
    return jnp.where(flip, -first, first), jnp.where(turned, -second, second)


def doc_start(first, second, index):
    return jnp.where(index >= second, second, jnp.where(index >= first, first, 0))


def rotated(block, cosine, sine):
    wide = block.astype(jnp.float32)
    return (wide * cosine + pltpu.roll(wide, HALF, 1) * sine).astype(jnp.bfloat16)


def lanes(i, width):
    return slice(i * width, (i + 1) * width)


def lanes_at(i, width):
    return pl.ds(pl.multiple_of(i * width, width), width)


def stacked_heads(q_ref, g, cosine, sine):
    parts = [q_ref[:, lanes_at(g * GROUP + i, HEAD_DIM)] for i in range(GROUP)]
    return jnp.concatenate([rotated(part, cosine, sine) for part in parts], 0)


def score(query, key):
    return SCALE * lax.dot_general(
        query, key, (((1,), (1,)), ((), ())), preferred_element_type=jnp.float32
    )


def blend(weight, values):
    wide = jnp.concatenate([values, jnp.ones_like(values)], 1)
    return jnp.dot(weight.astype(jnp.bfloat16), wide, preferred_element_type=jnp.float32)


def kernel(
    table_any, inverse_any, lengths_any, dest_any, long_lengths_any,
    k_long_any, v_long_any, q_short_any, k_short_any, v_short_any, q_long_any,
    bin_out, long_out,
    table, dest, inverse, lengths, long_lengths,
    k_long, v_long, q_short, k_short, v_short, q_long,
    pool, stage, landing, kv, query, top, acc, bias_ref, short_bias, short_turn, long_turn,
    bin_result, long_result,
    load_sem, out_sem, mate_send, mate_recv, route_send, route_recv, y_send, y_recv,
):
    dp, ctx = lax.axis_index("dp"), lax.axis_index("ctx")
    core, x, z = dp % 2, (dp // 2) % NX, dp // (2 * NX)
    span = q_long.shape[0]

    loads = [
        (table_any.at[pl.ds(pl.multiple_of((dp // 2) * (NZ * NX * ROUTE), NZ * NX * ROUTE), NZ * NX * ROUTE)], table),
        (dest_any, dest),
        (inverse_any, inverse),
        (lengths_any, lengths),
        (long_lengths_any, long_lengths),
        (k_long_any, k_long),
        (v_long_any, v_long),
        (q_short_any, q_short),
        (k_short_any, k_short),
        (v_short_any, v_short),
        (q_long_any, q_long),
    ]
    loads = [pltpu.make_async_copy(a, b, load_sem.at[i]) for i, (a, b) in enumerate(loads)]
    for load in loads[2:] + loads[:2]:
        load.start()

    def at(z_to, x_to):
        return (((z_to + NZ) % NZ * NX + (x_to + NX) % NX) * 2 + core, ctx)

    mate = (dp + 1 - 2 * core, ctx)
    routes = [at(z, x + 1), at(z, x - 1), at(z + 1, x), at(z - 1, x)]
    rings = [(dp, (ctx + 1) % NY), (dp, (ctx + NY - 1) % NY)]

    barrier = pltpu.get_barrier_semaphore()
    for other in [mate, *routes, *rings]:
        pl.semaphore_signal(barrier, inc=1, device_id=other, device_id_type=MESH)

    def copy(source, target, send, recv, other):
        return pltpu.make_async_remote_copy(
            src_ref=source, dst_ref=target, send_sem=send, recv_sem=recv,
            device_id=other, device_id_type=MESH,
        )

    def ring_copy(n, way):
        hop = n // KVHEADS
        g = (n + way * (KVHEADS // 2)) % KVHEADS
        if way == 0:
            source, target = hop, hop + 1
        else:
            source = jnp.where(hop == 0, 0, hop + HOPS)
            target = jnp.where(hop == HOPS - 1, HOPS, hop + HOPS + 1)
        return copy(
            kv.at[source, g], kv.at[target, g], y_send.at[way, n], y_recv.at[way, n], rings[way]
        )

    for load in loads[2:5]:
        load.wait()
    row = lax.broadcasted_iota(jnp.int32, (span, HEAD_DIM), 0)
    lane = lax.broadcasted_iota(jnp.int32, (span, HEAD_DIM), 1)
    mine = lax.broadcasted_iota(jnp.int32, lengths.shape[2:], 1) == dp
    home = [jnp.sum(jnp.where(mine, lengths[0, d], 0), axis=1, keepdims=True) for d in range(2)]
    first = jnp.where(row < BIN_LEN, home[0][0:1], home[0][1:2])
    second = first + jnp.where(row < BIN_LEN, home[1][0:1], home[1][1:2])
    token = row % BIN_LEN
    short_start = doc_start(first, second, token)
    my_row = row + ctx * span
    first = long_lengths[:, 0:1]
    long_start = doc_start(first, first + long_lengths[:, 1:2], my_row)
    position = jnp.where(lane < HALF, token - short_start, my_row - long_start)
    cosine, sine = turns(position.astype(jnp.float32) * inverse[...])
    cosine_swap, sine_swap = pltpu.roll(cosine, HALF, 1), pltpu.roll(sine, HALF, 1)
    low = lane < HALF
    short_cos, short_sin = jnp.where(low, cosine, cosine_swap), jnp.where(low, -sine, sine_swap)
    long_cos, long_sin = jnp.where(low, cosine_swap, cosine), jnp.where(low, -sine_swap, sine)

    for load in loads[5:7]:
        load.wait()
    short_turn[0], short_turn[1] = short_cos, short_sin
    long_turn[0], long_turn[1] = long_cos, long_sin

    @pl.loop(0, KVHEADS)
    def _(g):
        kv[0, g, :, :HEAD_DIM] = rotated(k_long[:, lanes_at(g, HEAD_DIM)], long_turn[0], long_turn[1])
        kv[0, g, :, HEAD_DIM:] = v_long[:, lanes_at(g, HEAD_DIM)]

    pl.semaphore_wait(barrier, 3 + DIRS)

    @pl.loop(0, KVHEADS)
    def _(n):
        for way in range(2):
            ring_copy(n, way).start()

    def mate_copy(j):
        return copy(
            pool.at[j, pl.ds(0, CHUNKS)], pool.at[j, pl.ds(CHUNKS, CHUNKS)],
            mate_send.at[j], mate_recv.at[j], mate,
        )

    for load in loads[7:10]:
        load.wait()

    def bias_of(rows, reach):
        index = lane[rows] % reach
        allowed = (index >= short_start[rows]) & (index <= token[rows])
        return jnp.where(allowed, 0.0, NEGATIVE)

    spot = lane[:EARLY]
    spans = [slice(i * EARLY, (i + 1) * EARLY) for i in range(2 * BINS)]
    for i, rows in enumerate(spans):
        short_bias[i] = bias_of(rows, (EARLY, BIN_LEN)[i % 2])

    @pl.loop(0, CHUNKS)
    def _(g):
        cosine, sine = short_turn[0], short_turn[1]
        heads = [
            rotated(q_short[:, lanes_at(g * GROUP + i, HEAD_DIM)], cosine, sine) for i in range(GROUP)
        ]
        key = rotated(k_short[:, lanes_at(g, HEAD_DIM)], cosine, sine)
        values = v_short[:, lanes_at(g, HEAD_DIM)]
        scores = []
        for i, rows in enumerate(spans):
            queries = jnp.concatenate([q[rows] for q in heads], 0)
            if i % 2:
                keys = jnp.concatenate([key[spans[i - 1]], key[rows]] * 2, 0)
            else:
                keys = jnp.concatenate([key[rows]] * GROUP, 0)
            scores.append(score(queries, keys) + jnp.concatenate([short_bias[i]] * GROUP, 0))
        scores = jnp.concatenate(scores, 0)
        weight = jnp.exp2(scores - jnp.max(scores, axis=1, keepdims=True))
        for j in range(BINS):
            w = [weight[(2 * j * GROUP + i) * EARLY :][:EARLY] for i in range(2 * GROUP)]
            packed = w[0]
            for i in range(1, GROUP):
                packed = jnp.where(spot // EARLY == i, w[i], packed)
            left = jnp.where(spot < BIN_LEN, w[GROUP], w[GROUP + 1])
            right = jnp.where(spot < BIN_LEN, w[GROUP + 2], w[GROUP + 3])
            pool[j, g, :, CUTS[0] : CUTS[1]] = packed.astype(jnp.bfloat16)
            pool[j, g, :, CUTS[1] : CUTS[2]] = values[spans[2 * j]]
            pool[j, g, :, CUTS[2] : CUTS[3]] = jnp.concatenate([left, right], 1).astype(jnp.bfloat16)
            pool[j, g, :, CUTS[3] : CUTS[4]] = values[spans[2 * j + 1]]

    for j in range(BINS):
        mate_copy(j).start()

    for load in loads[:2]:
        load.wait()
    def entry(j, place):
        mask = dest[0, j, 0]
        index = table[(mask >> 1) * ROUTE + place]
        return index + jnp.where(index < CHUNKS, (mask & 1) * CHUNKS, 0)

    def route_copy(slot, d):
        return copy(
            stage.at[slot, d], landing.at[slot, d], route_send.at[slot], route_recv.at[slot], routes[d]
        )

    def all_of(slot):
        return copy(stage.at[slot], landing.at[slot], route_send.at[slot], route_recv.at[slot], routes[0])

    def collect(slot):
        all_of(slot).wait_recv()
        for d in range(DIRS):
            pool[slot % BINS, OWN + DIRS * (slot // BINS) + d] = landing[slot, d]

    def send(slot):
        for d in range(DIRS):
            stage[slot, d] = pool[slot % BINS, entry(slot % BINS, slot // BINS * DIRS + d)]
            route_copy(slot, d).start()

    def ring(n):
        for way in range(2):
            ring_copy(n, way).wait_recv()

        @pl.when(n + KVHEADS < Y_SENDS)
        def _():
            for way in range(2):
                ring_copy(n + KVHEADS, way).start()

    loads[10].wait()

    @pl.loop(0, KVHEADS)
    def _(g):
        query[g] = stacked_heads(q_long, g, long_turn[0], long_turn[1])
        top[g] = jnp.full(top.shape[1:], NEGATIVE)
        acc[g] = jnp.zeros(acc.shape[1:])
        for i in (2 * g, 2 * g + 1):
            shift = jnp.where(i <= HOPS, NY - i, i - HOPS)
            key_index = lane + (ctx + shift) % NY * span
            allowed = (key_index >= long_start) & (key_index <= my_row)
            bias_ref[i] = jnp.where(allowed, 0.0, NEGATIVE)

    def attend(u):
        turn = u // KVHEADS
        g = jnp.where(turn == HOPS - 1, u % 2 * 2 + u // 2 % 2, u % KVHEADS)
        blocks = [jnp.where(turn == 0, 0, turn + HOPS), turn + 1]
        bias = jnp.concatenate([bias_ref[i] for i in blocks], 1)
        keys = jnp.concatenate([kv[i, g, :, :HEAD_DIM] for i in blocks], 0)
        values = jnp.concatenate([kv[i, g, :, HEAD_DIM:] for i in blocks], 0)
        scores = score(query[g], keys) + jnp.concatenate([bias] * GROUP, 0)
        old = top[g]
        peak = jnp.maximum(jnp.max(scores, axis=1, keepdims=True), old[:, :1])
        blended = blend(jnp.exp2(scores - peak), values)
        acc[g] = blended + acc[g] * jnp.exp2(old[:, :1] - peak)
        top[g] = jnp.broadcast_to(peak, old.shape)

    def long_copy(g):
        part = lanes_at(g, WIDE)
        return pltpu.make_async_copy(
            long_result.at[:, part], long_out.at[:, part], out_sem.at[BINS * CHUNKS + g]
        )

    def bin_copy(m, g):
        return pltpu.make_async_copy(bin_result.at[m, g], bin_out.at[m, g], out_sem.at[m * CHUNKS + g])

    slots = BINS * STEPS
    for j in range(BINS):
        mate_copy(j).wait()

    @pl.loop(0, slots)
    def _(slot):
        @pl.when(slot >= BINS)
        def _():
            collect(slot - BINS)

        send(slot)

        @pl.when((slot >= 1) & (slot <= Y_SENDS))
        def _():
            ring(slot - 1)

        full = (HOPS - 1) * KVHEADS
        begin = jnp.where(slot <= full + 1, jnp.maximum(slot - 1, 0), jnp.minimum(2 * slot - 2 - full, 4 * HOPS))
        end = jnp.where(slot <= full, slot, jnp.minimum(2 * slot - full, 4 * HOPS))

        @pl.loop(begin, end)
        def _(u):
            attend(u)

        @pl.when(slot >= BINS)
        def _():
            all_of(slot - BINS).wait_send()

    @pl.loop(0, KVHEADS)
    def _(g):
        both = acc[g]
        result = (both[:, :HEAD_DIM] / both[:, HEAD_DIM:]).astype(jnp.bfloat16)
        for i in range(GROUP):
            long_result[:, lanes_at(g * GROUP + i, HEAD_DIM)] = result[i * span : (i + 1) * span]
        long_copy(g).start()

    for slot in range(slots - BINS, slots):
        collect(slot)

    swap = (dp ^ dest[0, 0, 0]) > (dp ^ dest[0, 1, 0])

    @pl.loop(0, CHUNKS)
    def _(g):
        chunks = [pool[j, entry(j, DIRS * STEPS + g)] for j in range(BINS)]
        bin_result[0, g] = jnp.where(swap, chunks[1], chunks[0])
        bin_result[1, g] = jnp.where(swap, chunks[0], chunks[1])
        for m in range(BINS):
            bin_copy(m, g).start()

    for slot in range(slots - BINS, slots):
        all_of(slot).wait_send()

    @pl.loop(0, Y_SENDS)
    def _(n):
        for way in range(2):
            ring_copy(n, way).wait_send()

    @pl.loop(0, CHUNKS)
    def _(g):
        long_copy(g).wait()
        for m in range(BINS):
            bin_copy(m, g).wait()


def finish(bins_any, long_any, out_short, out_long, bins, short, long, sem_in, sem_out):
    rows = long.shape[0] // PIECES

    def long_copies(p):
        part = pl.ds(p * rows, rows)
        return (
            pltpu.make_async_copy(long_any.at[part], long.at[part], sem_in.at[BINS + p]),
            pltpu.make_async_copy(long.at[part], out_long.at[part], sem_out.at[BINS + p]),
        )

    def short_copies(m):
        part = pl.ds(m * BIN_LEN, BIN_LEN)
        return (
            pltpu.make_async_copy(bins_any.at[m], bins.at[m], sem_in.at[m]),
            pltpu.make_async_copy(short.at[part], out_short.at[part], sem_out.at[m]),
        )

    pieces = [short_copies(m) for m in range(BINS)] + [long_copies(p) for p in range(PIECES)]
    for load, _ in pieces:
        load.start()

    spot = lax.broadcasted_iota(jnp.int32, (EARLY, HEAD_DIM), 1)

    def chosen(test):
        return jnp.where(test, 1.0, 0.0).astype(jnp.bfloat16)

    quarter = [chosen(spot // EARLY == i) for i in range(GROUP)]
    side = [chosen(spot < BIN_LEN), chosen(spot >= BIN_LEN)]

    def finished(weight, values):
        blended = blend(weight, values)
        result = (blended[:, :HEAD_DIM] / blended[:, HEAD_DIM:]).astype(jnp.bfloat16)
        return jnp.concatenate([result[i * EARLY : (i + 1) * EARLY] for i in range(GROUP)], 1)

    for m in range(BINS):
        pieces[m][0].wait()

    @pl.loop(0, BINS * CHUNKS)
    def _(n):
        m, g = n // CHUNKS, n % CHUNKS
        first, first_v, second, second_v = [bins[m, g, :, CUTS[i] : CUTS[i + 1]] for i in range(4)]
        early = jnp.concatenate([first * q for q in quarter], 0)
        late = [second[:, lanes(i // 2, HEAD_DIM)] * side[i % 2] for i in range(GROUP)]
        late = jnp.concatenate(late, 0)
        parts = [
            finished(early, jnp.concatenate([first_v] * GROUP, 0)),
            finished(late, jnp.concatenate([first_v, second_v] * 2, 0)),
        ]
        for i, part in enumerate(parts):
            rows = pl.ds(pl.multiple_of(m * BIN_LEN + i * EARLY, EARLY), EARLY)
            short[rows, lanes_at(g, WIDE)] = part

    for load, store in pieces[BINS:]:
        load.wait()
        store.start()
    for m in range(BINS):
        pieces[m][1].start()
    for _, store in pieces:
        store.wait()


HBM = pl.BlockSpec(memory_space=pltpu.HBM)


def local(q_short, k_short, v_short, short_lengths, bin_dest, q_long, k_long, v_long, long_lengths):
    span = q_long.shape[0]
    table = jnp.asarray(route_table())
    inverse = jnp.asarray(np.concatenate([INVERSE, INVERSE])[None, :])
    lengths = jnp.transpose(short_lengths, (1, 3, 2, 0))
    dest = jnp.transpose(bin_dest, (1, 2, 0))

    bf16, f32, i32 = jnp.bfloat16, jnp.float32, jnp.int32
    slots = BINS * STEPS
    dma = pltpu.SemaphoreType.DMA
    inputs = [k_long, v_long, q_short, k_short, v_short, q_long]
    bins_shape = (BINS, CHUNKS, EARLY, CUTS[-1])
    bins, long = pl.pallas_call(
        kernel,
        out_shape=[jax.ShapeDtypeStruct(bins_shape, bf16), jax.ShapeDtypeStruct(q_long.shape, bf16)],
        in_specs=[HBM] * 11,
        out_specs=[HBM, HBM],
        scratch_shapes=[
            pltpu.SMEM((NZ * NX * ROUTE,), i32),
            pltpu.SMEM(dest.shape, i32),
            pltpu.VMEM(inverse.shape, f32),
            pltpu.VMEM(lengths.shape, i32),
            pltpu.VMEM(long_lengths.shape, i32),
            *[pltpu.VMEM(a.shape, bf16) for a in inputs],
            pltpu.VMEM((BINS, POOL, EARLY, CUTS[-1]), bf16),
            pltpu.VMEM((slots, DIRS, EARLY, CUTS[-1]), bf16),
            pltpu.VMEM((slots, DIRS, EARLY, CUTS[-1]), bf16),
            pltpu.VMEM((NY, KVHEADS, span, 2 * HEAD_DIM), bf16),
            pltpu.VMEM((KVHEADS, GROUP * span, HEAD_DIM), bf16),
            pltpu.VMEM((KVHEADS, GROUP * span, HEAD_DIM), f32),
            pltpu.VMEM((KVHEADS, GROUP * span, 2 * HEAD_DIM), f32),
            pltpu.VMEM((NY, span, span), f32),
            pltpu.VMEM((2 * BINS, EARLY, HEAD_DIM), f32),
            pltpu.VMEM((2, span, HEAD_DIM), f32),
            pltpu.VMEM((2, span, HEAD_DIM), f32),
            pltpu.VMEM(bins_shape, bf16),
            pltpu.VMEM(q_long.shape, bf16),
            dma((11,)),
            dma((BINS * CHUNKS + KVHEADS,)),
            dma((BINS,)),
            dma((BINS,)),
            dma((slots,)),
            dma((slots,)),
            dma((2, Y_SENDS)),
            dma((2, Y_SENDS)),
        ],
        compiler_params=pltpu.CompilerParams(
            collective_id=0, has_side_effects=True, vmem_limit_bytes=56 * 2**20
        ),
    )(table, inverse, lengths, dest, long_lengths, *inputs)
    return pl.pallas_call(
        finish,
        out_shape=[jax.ShapeDtypeStruct(q_short.shape, bf16), jax.ShapeDtypeStruct(q_long.shape, bf16)],
        in_specs=[HBM, HBM],
        out_specs=[HBM, HBM],
        scratch_shapes=[
            pltpu.VMEM(bins_shape, bf16),
            pltpu.VMEM(q_short.shape, bf16),
            pltpu.VMEM(q_long.shape, bf16),
            dma((BINS + PIECES,)),
            dma((BINS + PIECES,)),
        ],
        compiler_params=pltpu.CompilerParams(vmem_limit_bytes=56 * 2**20),
    )(bins, long)


def solution(mesh):
    in_specs = (
        P(("dp", "ctx"), None),
        P(("dp", "ctx"), None),
        P(("dp", "ctx"), None),
        P(None, "ctx", None, None),
        P(None, "ctx", None),
        P(("dp", "ctx"), None),
        P(("dp", "ctx"), None),
        P(("dp", "ctx"), None),
        P("dp", None),
    )
    out_specs = (P(("dp", "ctx"), None), P(("dp", "ctx"), None))
    return jax.shard_map(local, mesh=mesh, in_specs=in_specs, out_specs=out_specs, check_vma=False)
```

```python
import functools
import math

import jax
import jax.numpy as jnp
import numpy as np
from jax import lax
from jax.experimental import pallas as pl
from jax.experimental.pallas import tpu as pltpu
from jax.sharding import PartitionSpec as P

QHEADS = 16
KVHEADS = 4
GROUP = QHEADS // KVHEADS
HEAD_DIM = 128
HALF = HEAD_DIM // 2
WIDE = GROUP * HEAD_DIM
BIN_LEN = 64
BINS = 2
THETA = 500000.0
NEGATIVE = -1e30
SCALE = math.log2(math.e) / math.sqrt(HEAD_DIM)

NZ, NX, NY = 8, 4, 8
HALVES = 1
EARLY = BIN_LEN // 2
ROWS = EARLY // HALVES
CUTS = (0, HEAD_DIM, 2 * HEAD_DIM, 4 * HEAD_DIM, 5 * HEAD_DIM)
CHUNKS = KVHEADS
STEPS = 8
DIRS = 4
OWN = 2 * CHUNKS
POOL = OWN + DIRS * STEPS
PIECES = 4
ROUTE = 64
HOPS = NY // 2
Y_SENDS = 3 * KVHEADS + KVHEADS // 2
MESH = pl.DeviceIdType.MESH


def moved(place, direction):
    z, x = divmod(place, NX)
    if direction < 2:
        x = (x + (1, -1)[direction]) % NX
    else:
        z = (z + (1, -1)[direction - 2]) % NZ
    return z * NX + x


@functools.cache
def route_table():
    table = np.zeros((NZ * NX, NZ * NX, ROUTE), np.int32)
    for mask in range(NZ * NX):
        packets = []
        for place in range(NZ * NX):
            z, x = divmod(place, NX)
            goal_z, goal_x = divmod(place ^ mask, NX)
            for chunk in range(CHUNKS):
                dz, dx = (goal_z - z) % NZ, (goal_x - x) % NX
                if dz > NZ // 2 or (dz == NZ // 2 and chunk % 2):
                    dz -= NZ
                if dx > NX // 2 or (dx == NX // 2 and (chunk // (2 if mask // NX == NZ // 2 else 1)) % 2):
                    dx -= NX
                packets.append([place, dz, dx, chunk, chunk])
        step = 0
        while any(p[1] or p[2] for p in packets):
            order = sorted(packets, key=lambda p: (-abs(p[1]) - abs(p[2]), -abs(p[1]), p[4]))
            taken, moves = set(), []
            for p in order:
                options = []
                if p[1]:
                    options.append(2 if p[1] > 0 else 3)
                if p[2]:
                    options.append(0 if p[2] > 0 else 1)
                for d in options:
                    if (p[0], d) not in taken:
                        taken.add((p[0], d))
                        moves.append((p, d))
                        break
            for p, d in moves:
                table[mask, p[0], step * DIRS + d] = p[3]
                p[0] = moved(p[0], d)
                p[2 if d < 2 else 1] -= (1, -1)[d % 2]
                p[3] = OWN + DIRS * step + d
            step += 1
        assert step <= STEPS
        for p in packets:
            table[mask, p[0], DIRS * STEPS + p[4]] = p[3]
    return np.ascontiguousarray(table.transpose(1, 0, 2)).reshape(-1)


INVERSE = np.power(THETA, -np.arange(HALF, dtype=np.float64) * (2.0 / HEAD_DIM)).astype(np.float32)
QUARTER1 = float(np.float32(1.5703125))
QUARTER2 = float(np.float32(math.floor((math.pi / 2 - QUARTER1) * 2**23) / 2**23))
QUARTER3 = float(np.float32(math.pi / 2 - QUARTER1 - QUARTER2))


def turns(angle):
    quarters = jnp.floor(angle * (2.0 / math.pi) + 0.5)
    r = ((angle - quarters * QUARTER1) - quarters * QUARTER2) - quarters * QUARTER3
    s = r * r
    sine = 1.0 / 362880
    for k in (-1.0 / 5040, 1.0 / 120, -1.0 / 6):
        sine = sine * s + k
    sine = r + r * s * sine
    cosine = 1.0 / 40320
    for k in (-1.0 / 720, 1.0 / 24, -0.5, 1.0):
        cosine = cosine * s + k
    count = quarters.astype(jnp.int32)
    odd, turned = (count & 1) == 1, (count & 2) == 2
    first, second = jnp.where(odd, sine, cosine), jnp.where(odd, cosine, sine)
    flip = turned != odd
    return jnp.where(flip, -first, first), jnp.where(turned, -second, second)


def doc_start(first, second, index):
    return jnp.where(index >= second, second, jnp.where(index >= first, first, 0))


def rotated(block, cosine, sine):
    wide = block.astype(jnp.float32)
    return (wide * cosine + pltpu.roll(wide, HALF, 1) * sine).astype(jnp.bfloat16)


def lanes(i, width):
    return slice(i * width, (i + 1) * width)


def lanes_at(i, width):
    return pl.ds(i * width, width)


def stacked_heads(q_ref, g, cosine, sine):
    heads = range(g * GROUP, (g + 1) * GROUP)
    return jnp.concatenate([rotated(q_ref[:, lanes(h, HEAD_DIM)], cosine, sine) for h in heads], 0)


def score(query, key):
    return SCALE * lax.dot_general(
        query, key, (((1,), (1,)), ((), ())), preferred_element_type=jnp.float32
    )


def blend(weight, values):
    wide = jnp.concatenate([values, jnp.ones_like(values)], 1)
    return jnp.dot(weight.astype(jnp.bfloat16), wide, preferred_element_type=jnp.float32)


def kernel(
    table_any, inverse_any, lengths_any, dest_any, long_lengths_any,
    k_long_any, v_long_any, q_short_any, k_short_any, v_short_any, q_long_any,
    bin_out, long_out,
    table, dest, inverse, lengths, long_lengths,
    k_long, v_long, q_short, k_short, v_short, q_long,
    pool_refs, stage, landing, kv, query, top, acc, bias_ref, bin_result, long_result,
    load_sem, out_sem, mate_send, mate_recv, route_send, route_recv, y_send, y_recv,
):
    dp, ctx = lax.axis_index("dp"), lax.axis_index("ctx")
    core, x, z = dp % 2, (dp // 2) % NX, dp // (2 * NX)
    span = q_long.shape[0]

    loads = [
        (table_any.at[pl.ds(pl.multiple_of((dp // 2) * (NZ * NX * ROUTE), NZ * NX * ROUTE), NZ * NX * ROUTE)], table),
        (dest_any, dest),
        (inverse_any, inverse),
        (lengths_any, lengths),
        (long_lengths_any, long_lengths),
        (k_long_any, k_long),
        (v_long_any, v_long),
        (q_short_any, q_short),
        (k_short_any, k_short),
        (v_short_any, v_short),
        (q_long_any, q_long),
    ]
    loads = [pltpu.make_async_copy(a, b, load_sem.at[i]) for i, (a, b) in enumerate(loads)]
    for load in loads[2:] + loads[:2]:
        load.start()

    def at(z_to, x_to):
        return (((z_to + NZ) % NZ * NX + (x_to + NX) % NX) * 2 + core, ctx)

    mate = (dp + 1 - 2 * core, ctx)
    routes = [at(z, x + 1), at(z, x - 1), at(z + 1, x), at(z - 1, x)]
    rings = [(dp, (ctx + 1) % NY), (dp, (ctx + NY - 1) % NY)]

    barrier = pltpu.get_barrier_semaphore()
    for other in [mate, *routes, *rings]:
        pl.semaphore_signal(barrier, inc=1, device_id=other, device_id_type=MESH)

    def copy(source, target, send, recv, other):
        return pltpu.make_async_remote_copy(
            src_ref=source, dst_ref=target, send_sem=send, recv_sem=recv,
            device_id=other, device_id_type=MESH,
        )

    def ring_copy(n, way):
        hop = n // KVHEADS
        g = (n + way * (KVHEADS // 2)) % KVHEADS
        if way == 0:
            source, target = hop, hop + 1
        else:
            source = jnp.where(hop == 0, 0, hop + HOPS)
            target = jnp.where(hop == HOPS - 1, HOPS, hop + HOPS + 1)
        return copy(
            kv.at[source, g], kv.at[target, g], y_send.at[way, n], y_recv.at[way, n], rings[way]
        )

    for load in loads[2:5]:
        load.wait()
    row = lax.broadcasted_iota(jnp.int32, (span, HEAD_DIM), 0)
    lane = lax.broadcasted_iota(jnp.int32, (span, HEAD_DIM), 1)
    mine = lax.broadcasted_iota(jnp.int32, lengths.shape[2:], 1) == dp
    home = [jnp.sum(jnp.where(mine, lengths[0, d], 0), axis=1, keepdims=True) for d in range(2)]
    first = jnp.where(row < BIN_LEN, home[0][0:1], home[0][1:2])
    second = first + jnp.where(row < BIN_LEN, home[1][0:1], home[1][1:2])
    token = row % BIN_LEN
    short_start = doc_start(first, second, token)
    my_row = row + ctx * span
    first = long_lengths[:, 0:1]
    long_start = doc_start(first, first + long_lengths[:, 1:2], my_row)
    position = jnp.where(lane < HALF, token - short_start, my_row - long_start)
    cosine, sine = turns(position.astype(jnp.float32) * inverse[...])
    cosine_swap, sine_swap = pltpu.roll(cosine, HALF, 1), pltpu.roll(sine, HALF, 1)
    low = lane < HALF
    short_cos, short_sin = jnp.where(low, cosine, cosine_swap), jnp.where(low, -sine, sine_swap)
    long_cos, long_sin = jnp.where(low, cosine_swap, cosine), jnp.where(low, -sine_swap, sine)

    for load in loads[5:7]:
        load.wait()
    for g in range(KVHEADS):
        kv[0, g, :, :HEAD_DIM] = rotated(k_long[:, lanes(g, HEAD_DIM)], long_cos, long_sin)
        kv[0, g, :, HEAD_DIM:] = v_long[:, lanes(g, HEAD_DIM)]
    pl.semaphore_wait(barrier, 3 + DIRS)
    for n in range(KVHEADS):
        for way in range(2):
            ring_copy(n, way).start()

    pools = [*pool_refs]
    streams = range(BINS * HALVES)

    def mate_copy(t):
        return copy(
            pools[t].at[pl.ds(0, CHUNKS)], pools[t].at[pl.ds(CHUNKS, CHUNKS)],
            mate_send.at[t], mate_recv.at[t], mate,
        )

    for load in loads[7:10]:
        load.wait()

    def bias_of(rows, reach):
        index = lane[rows] % reach
        allowed = (index >= short_start[rows]) & (index <= token[rows])
        return jnp.concatenate([jnp.where(allowed, 0.0, NEGATIVE)] * GROUP, 0)

    spot = lane[:EARLY]
    for j in range(BINS):
        rows = slice(j * BIN_LEN, (j + 1) * BIN_LEN)
        early = slice(j * BIN_LEN, j * BIN_LEN + EARLY)
        late = slice(j * BIN_LEN + EARLY, (j + 1) * BIN_LEN)
        early_bias, late_bias = bias_of(early, EARLY), bias_of(late, BIN_LEN)
        early_scores, late_scores = [], []
        for g in range(CHUNKS):
            heads = [
                rotated(q_short[rows, lanes(g * GROUP + i, HEAD_DIM)], short_cos[rows], short_sin[rows])
                for i in range(GROUP)
            ]
            key = rotated(k_short[rows, lanes(g, HEAD_DIM)], short_cos[rows], short_sin[rows])
            first = jnp.concatenate([q[:EARLY] for q in heads], 0)
            second = jnp.concatenate([q[EARLY:] for q in heads], 0)
            keys = jnp.concatenate([key[:EARLY]] * GROUP, 0)
            early_scores.append(score(first, keys) + early_bias)
            late_scores.append(score(second, jnp.concatenate([key] * 2, 0)) + late_bias)
        scores = jnp.concatenate(early_scores + late_scores, 0)
        weight = jnp.exp2(scores - jnp.max(scores, axis=1, keepdims=True))
        for g in range(CHUNKS):
            w = [weight[(g * GROUP + i) * EARLY :][:EARLY] for i in range(GROUP)]
            packed = w[0]
            for i in range(1, GROUP):
                packed = jnp.where(spot // EARLY == i, w[i], packed)
            w = [weight[((CHUNKS + g) * GROUP + i) * EARLY :][:EARLY] for i in range(GROUP)]
            left = jnp.where(spot < BIN_LEN, w[0], w[1])
            right = jnp.where(spot < BIN_LEN, w[2], w[3])
            pieces = [
                packed.astype(jnp.bfloat16), v_short[early, lanes(g, HEAD_DIM)],
                jnp.concatenate([left, right], 1).astype(jnp.bfloat16), v_short[late, lanes(g, HEAD_DIM)],
            ]
            for h in range(HALVES):
                for i, piece in enumerate(pieces):
                    part = slice(CUTS[i], CUTS[i + 1])
                    pools[j * HALVES + h][g, :, part] = piece[h * ROWS : (h + 1) * ROWS]
        for h in range(HALVES):
            mate_copy(j * HALVES + h).start()

    for load in loads[:2]:
        load.wait()
    masks = [dest[0, j, 0] for j in range(BINS)]

    def entry(t, place):
        mask = masks[t // HALVES]
        index = table[(mask >> 1) * ROUTE + place]
        return index + jnp.where(index < CHUNKS, (mask & 1) * CHUNKS, 0)

    def route_copy(slot, d):
        return copy(
            stage.at[slot, d], landing.at[slot, d], route_send.at[slot], route_recv.at[slot], routes[d]
        )

    def all_of(slot):
        return copy(stage.at[slot], landing.at[slot], route_send.at[slot], route_recv.at[slot], routes[0])

    def collect(t, step):
        slot = len(streams) * step + t
        all_of(slot).wait_recv()
        for d in range(DIRS):
            pools[t][OWN + DIRS * step + d] = landing[slot, d]

    def send(t, step, entries):
        slot = len(streams) * step + t
        for d in range(DIRS):
            stage[slot, d] = pools[t][entries[d]]
            route_copy(slot, d).start()

    def ring(n):
        for way in range(2):
            ring_copy(n, way).wait()
        if n + KVHEADS < Y_SENDS:
            for way in range(2):
                ring_copy(n + KVHEADS, way).start()

    shift = [0] + [-h for h in range(1, HOPS + 1)] + [h for h in range(1, NY - HOPS)]

    def prepare(t):
        query[t] = stacked_heads(q_long, t, long_cos, long_sin)
        for i in (2 * t, 2 * t + 1):
            key_index = lane + (ctx + NY + shift[i]) % NY * span
            allowed = (key_index >= long_start) & (key_index <= my_row)
            bias_ref[i] = jnp.where(allowed, 0.0, NEGATIVE)

    def attend(heads, blocks):
        begins, ends = 0 in blocks, HOPS in blocks
        bias = jnp.concatenate([bias_ref[i] for i in blocks], 1)
        bias = jnp.concatenate([bias] * GROUP, 0)
        keys = [jnp.concatenate([kv[i, g, :, :HEAD_DIM] for i in blocks], 0) for g in heads]
        values = [jnp.concatenate([kv[i, g, :, HEAD_DIM:] for i in blocks], 0) for g in heads]
        scores = [score(query[g], k) + bias for g, k in zip(heads, keys)]
        peaks = [jnp.max(s, axis=1, keepdims=True) for s in scores]
        if not begins:
            olds = [top[g][:, :1] for g in heads]
            peaks = [jnp.maximum(peak, old) for peak, old in zip(peaks, olds)]
        weights = [jnp.exp2(s - peak) for s, peak in zip(scores, peaks)]
        blended = [blend(w, v) for w, v in zip(weights, values)]
        for n, g in enumerate(heads):
            both = blended[n]
            if not begins:
                both = both + acc[g] * jnp.exp2(olds[n] - peaks[n])
            if ends:
                result = (both[:, :HEAD_DIM] / both[:, HEAD_DIM:]).astype(jnp.bfloat16)
                for i in range(GROUP):
                    long_result[:, lanes(g * GROUP + i, HEAD_DIM)] = result[i * span : (i + 1) * span]
                long_copy(g).start()
            else:
                top[g] = jnp.broadcast_to(peaks[n], top.shape[1:])
                acc[g] = both

    def long_copy(g):
        return pltpu.make_async_copy(
            long_result.at[:, lanes_at(g, WIDE)], long_out.at[:, lanes_at(g, WIDE)], out_sem.at[BINS * CHUNKS + g]
        )

    def bin_copy(m, g):
        return pltpu.make_async_copy(bin_result.at[m, g], bin_out.at[m, g], out_sem.at[m * CHUNKS + g])

    near = [0, 1, HOPS + 1]
    middle = [2, HOPS + 2]
    third = [3, HOPS + 3]
    far = [HOPS]

    plan = [
        [(prepare, 0)],
        [(ring, 0), (prepare, 1)],
        [(ring, 1), (prepare, 2)],
        [(ring, 2), (prepare, 3)],
        [(ring, 3), (attend, [0, 1], near)],
        [(ring, 4)],
        [(ring, 5), (attend, [2, 3], near)],
        [(ring, 6)],
        [(ring, 7)],
        [(ring, 8), (attend, [0, 1], middle)],
        [(ring, 9)],
        [(ring, 10), (attend, [2, 3], middle)],
        [(ring, 11)],
        [(ring, 12)],
        [(attend, [0, 2], third + far)],
        [(ring, 13), (attend, [1, 3], third + far)],
    ]

    def work(tasks):
        for task, *arguments in tasks:
            task(*arguments)

    loads[10].wait()
    for step in range(STEPS):
        for t in streams:
            entries = [entry(t, step * DIRS + d) for d in range(DIRS)]
            if step == 0:
                mate_copy(t).wait()
            else:
                collect(t, step - 1)
            send(t, step, entries)
            if t % HALVES == 0:
                work(plan[2 * step + t // HALVES])
            if step > 0:
                all_of(len(streams) * (step - 1) + t).wait_send()

    for t in streams:
        collect(t, STEPS - 1)

    swap = (dp ^ masks[0]) > (dp ^ masks[1])
    for g in range(CHUNKS):
        chunks = [
            jnp.concatenate(
                [pools[t][entry(t, DIRS * STEPS + g)] for t in range(j * HALVES, (j + 1) * HALVES)], 0
            )
            for j in range(BINS)
        ]
        bin_result[0, g] = jnp.where(swap, chunks[1], chunks[0])
        bin_result[1, g] = jnp.where(swap, chunks[0], chunks[1])
        for m in range(BINS):
            bin_copy(m, g).start()
    for t in streams:
        all_of(len(streams) * (STEPS - 1) + t).wait_send()

    for g in range(CHUNKS):
        long_copy(g).wait()
        for m in range(BINS):
            bin_copy(m, g).wait()


def finish(bins_any, long_any, out_short, out_long, bins, short, long, sem_in, sem_out):
    rows = long.shape[0] // PIECES

    def long_copies(p):
        part = pl.ds(p * rows, rows)
        return (
            pltpu.make_async_copy(long_any.at[part], long.at[part], sem_in.at[BINS + p]),
            pltpu.make_async_copy(long.at[part], out_long.at[part], sem_out.at[BINS + p]),
        )

    def short_copies(m):
        part = pl.ds(m * BIN_LEN, BIN_LEN)
        return (
            pltpu.make_async_copy(bins_any.at[m], bins.at[m], sem_in.at[m]),
            pltpu.make_async_copy(short.at[part], out_short.at[part], sem_out.at[m]),
        )

    pieces = [short_copies(m) for m in range(BINS)] + [long_copies(p) for p in range(PIECES)]
    for load, _ in pieces:
        load.start()

    spot = lax.broadcasted_iota(jnp.int32, (EARLY, HEAD_DIM), 1)

    def chosen(test):
        return jnp.where(test, 1.0, 0.0).astype(jnp.bfloat16)

    quarter = [chosen(spot // EARLY == i) for i in range(GROUP)]
    side = [chosen(spot < BIN_LEN), chosen(spot >= BIN_LEN)]

    def finished(weight, values):
        blended = blend(weight, values)
        result = (blended[:, :HEAD_DIM] / blended[:, HEAD_DIM:]).astype(jnp.bfloat16)
        return jnp.concatenate([result[i * EARLY : (i + 1) * EARLY] for i in range(GROUP)], 1)

    for m in range(BINS):
        pieces[m][0].wait()
        for g in range(CHUNKS):
            chunk = bins[m, g]
            first, first_v, second, second_v = [chunk[:, CUTS[i] : CUTS[i + 1]] for i in range(4)]
            early = jnp.concatenate([first * q for q in quarter], 0)
            late = [second[:, lanes(i // 2, HEAD_DIM)] * side[i % 2] for i in range(GROUP)]
            late = jnp.concatenate(late, 0)
            start = m * BIN_LEN
            short[start : start + EARLY, lanes(g, WIDE)] = finished(
                early, jnp.concatenate([first_v] * GROUP, 0)
            )
            short[start + EARLY : start + BIN_LEN, lanes(g, WIDE)] = finished(
                late, jnp.concatenate([first_v, second_v] * 2, 0)
            )
        if m == 0:
            for load, store in pieces[BINS:]:
                load.wait()
                store.start()
        pieces[m][1].start()
    for _, store in pieces:
        store.wait()


HBM = pl.BlockSpec(memory_space=pltpu.HBM)


def local(q_short, k_short, v_short, short_lengths, bin_dest, q_long, k_long, v_long, long_lengths):
    span = q_long.shape[0]
    table = jnp.asarray(route_table())
    inverse = jnp.asarray(np.concatenate([INVERSE, INVERSE])[None, :])
    lengths = jnp.transpose(short_lengths, (1, 3, 2, 0))
    dest = jnp.transpose(bin_dest, (1, 2, 0))

    bf16, f32, i32 = jnp.bfloat16, jnp.float32, jnp.int32
    slots = BINS * HALVES * STEPS
    dma = pltpu.SemaphoreType.DMA
    inputs = [k_long, v_long, q_short, k_short, v_short, q_long]
    bins_shape = (BINS, CHUNKS, EARLY, CUTS[-1])
    bins, long = pl.pallas_call(
        kernel,
        out_shape=[jax.ShapeDtypeStruct(bins_shape, bf16), jax.ShapeDtypeStruct(q_long.shape, bf16)],
        in_specs=[HBM] * 11,
        out_specs=[HBM, HBM],
        scratch_shapes=[
            pltpu.SMEM((NZ * NX * ROUTE,), i32),
            pltpu.SMEM(dest.shape, i32),
            pltpu.VMEM(inverse.shape, f32),
            pltpu.VMEM(lengths.shape, i32),
            pltpu.VMEM(long_lengths.shape, i32),
            *[pltpu.VMEM(a.shape, bf16) for a in inputs],
            [pltpu.VMEM((POOL, ROWS, CUTS[-1]), bf16)] * (BINS * HALVES),
            pltpu.VMEM((slots, DIRS, ROWS, CUTS[-1]), bf16),
            pltpu.VMEM((slots, DIRS, ROWS, CUTS[-1]), bf16),
            pltpu.VMEM((NY, KVHEADS, span, 2 * HEAD_DIM), bf16),
            pltpu.VMEM((KVHEADS, GROUP * span, HEAD_DIM), bf16),
            pltpu.VMEM((KVHEADS, GROUP * span, HEAD_DIM), f32),
            pltpu.VMEM((KVHEADS, GROUP * span, 2 * HEAD_DIM), f32),
            pltpu.VMEM((NY, span, span), f32),
            pltpu.VMEM(bins_shape, bf16),
            pltpu.VMEM(q_long.shape, bf16),
            dma((11,)),
            dma((BINS * CHUNKS + KVHEADS,)),
            dma((BINS * HALVES,)),
            dma((BINS * HALVES,)),
            dma((slots,)),
            dma((slots,)),
            dma((2, Y_SENDS)),
            dma((2, Y_SENDS)),
        ],
        compiler_params=pltpu.CompilerParams(
            collective_id=0, has_side_effects=True, vmem_limit_bytes=56 * 2**20
        ),
    )(table, inverse, lengths, dest, long_lengths, *inputs)
    return pl.pallas_call(
        finish,
        out_shape=[jax.ShapeDtypeStruct(q_short.shape, bf16), jax.ShapeDtypeStruct(q_long.shape, bf16)],
        in_specs=[HBM, HBM],
        out_specs=[HBM, HBM],
        scratch_shapes=[
            pltpu.VMEM(bins_shape, bf16),
            pltpu.VMEM(q_short.shape, bf16),
            pltpu.VMEM(q_long.shape, bf16),
            dma((BINS + PIECES,)),
            dma((BINS + PIECES,)),
        ],
        compiler_params=pltpu.CompilerParams(vmem_limit_bytes=56 * 2**20),
    )(bins, long)


def solution(mesh):
    in_specs = (
        P(("dp", "ctx"), None),
        P(("dp", "ctx"), None),
        P(("dp", "ctx"), None),
        P(None, "ctx", None, None),
        P(None, "ctx", None),
        P(("dp", "ctx"), None),
        P(("dp", "ctx"), None),
        P(("dp", "ctx"), None),
        P("dp", None),
    )
    out_specs = (P(("dp", "ctx"), None), P(("dp", "ctx"), None))
    return jax.shard_map(local, mesh=mesh, in_specs=in_specs, out_specs=out_specs, check_vma=False)
```

```python
import functools
import math

import jax
import jax.numpy as jnp
import numpy as np
from jax import lax
from jax.experimental import pallas as pl
from jax.experimental.pallas import tpu as pltpu
from jax.sharding import PartitionSpec as P

QHEADS = 16
KVHEADS = 4
GROUP = QHEADS // KVHEADS
HEAD_DIM = 128
HALF = HEAD_DIM // 2
WIDE = GROUP * HEAD_DIM
BIN_LEN = 64
BINS = 2
THETA = 500000.0
NEGATIVE = -1e30
SCALE = math.log2(math.e) / math.sqrt(HEAD_DIM)

NZ, NX, NY = 8, 4, 8
HALVES = 1
EARLY = BIN_LEN // 2
ROWS = EARLY // HALVES
CUTS = (0, HEAD_DIM, 2 * HEAD_DIM, 4 * HEAD_DIM, 5 * HEAD_DIM)
CHUNKS = KVHEADS
STEPS = 8
DIRS = 4
OWN = CHUNKS
POOL = OWN + DIRS * STEPS
PIECES = 4
ROUTE = 64
HOPS = NY // 2
Y_SENDS = 3 * KVHEADS + KVHEADS // 2
MESH = pl.DeviceIdType.MESH


def moved(place, direction):
    z, x = divmod(place, NX)
    if direction < 2:
        x = (x + (1, -1)[direction]) % NX
    else:
        z = (z + (1, -1)[direction - 2]) % NZ
    return z * NX + x


@functools.cache
def route_table():
    table = np.zeros((NZ * NX, NZ * NX, ROUTE), np.int32)
    for mask in range(NZ * NX):
        packets = []
        for place in range(NZ * NX):
            z, x = divmod(place, NX)
            goal_z, goal_x = divmod(place ^ mask, NX)
            for chunk in range(CHUNKS):
                dz, dx = (goal_z - z) % NZ, (goal_x - x) % NX
                if dz > NZ // 2 or (dz == NZ // 2 and chunk % 2):
                    dz -= NZ
                if dx > NX // 2 or (dx == NX // 2 and (chunk // (2 if mask // NX == NZ // 2 else 1)) % 2):
                    dx -= NX
                packets.append([place, dz, dx, chunk, chunk])
        step = 0
        while any(p[1] or p[2] for p in packets):
            order = sorted(packets, key=lambda p: (-abs(p[1]) - abs(p[2]), -abs(p[1]), p[4]))
            taken, moves = set(), []
            for p in order:
                options = []
                if p[1]:
                    options.append(2 if p[1] > 0 else 3)
                if p[2]:
                    options.append(0 if p[2] > 0 else 1)
                for d in options:
                    if (p[0], d) not in taken:
                        taken.add((p[0], d))
                        moves.append((p, d))
                        break
            for p, d in moves:
                table[mask, p[0], step * DIRS + d] = p[3]
                p[0] = moved(p[0], d)
                p[2 if d < 2 else 1] -= (1, -1)[d % 2]
                p[3] = OWN + DIRS * step + d
            step += 1
        assert step <= STEPS
        for p in packets:
            table[mask, p[0], DIRS * STEPS + p[4]] = p[3]
    return np.ascontiguousarray(table.transpose(1, 0, 2)).reshape(-1)


INVERSE = np.power(THETA, -np.arange(HALF, dtype=np.float64) * (2.0 / HEAD_DIM)).astype(np.float32)
QUARTER1 = float(np.float32(1.5703125))
QUARTER2 = float(np.float32(math.floor((math.pi / 2 - QUARTER1) * 2**23) / 2**23))
QUARTER3 = float(np.float32(math.pi / 2 - QUARTER1 - QUARTER2))


def turns(angle):
    quarters = jnp.floor(angle * (2.0 / math.pi) + 0.5)
    r = ((angle - quarters * QUARTER1) - quarters * QUARTER2) - quarters * QUARTER3
    s = r * r
    sine = 1.0 / 362880
    for k in (-1.0 / 5040, 1.0 / 120, -1.0 / 6):
        sine = sine * s + k
    sine = r + r * s * sine
    cosine = 1.0 / 40320
    for k in (-1.0 / 720, 1.0 / 24, -0.5, 1.0):
        cosine = cosine * s + k
    count = quarters.astype(jnp.int32)
    odd, turned = (count & 1) == 1, (count & 2) == 2
    first, second = jnp.where(odd, sine, cosine), jnp.where(odd, cosine, sine)
    flip = turned != odd
    return jnp.where(flip, -first, first), jnp.where(turned, -second, second)


def doc_start(first, second, index):
    return jnp.where(index >= second, second, jnp.where(index >= first, first, 0))


def rotated(block, cosine, sine):
    wide = block.astype(jnp.float32)
    return (wide * cosine + pltpu.roll(wide, HALF, 1) * sine).astype(jnp.bfloat16)


def lanes(i, width):
    return slice(i * width, (i + 1) * width)


def lanes_at(i, width):
    return pl.ds(i * width, width)


def stacked_heads(q_ref, g, cosine, sine):
    heads = range(g * GROUP, (g + 1) * GROUP)
    return jnp.concatenate([rotated(q_ref[:, lanes(h, HEAD_DIM)], cosine, sine) for h in heads], 0)


def score(query, key):
    return SCALE * lax.dot_general(
        query, key, (((1,), (1,)), ((), ())), preferred_element_type=jnp.float32
    )


def blend(weight, values):
    wide = jnp.concatenate([values, jnp.ones_like(values)], 1)
    return jnp.dot(weight.astype(jnp.bfloat16), wide, preferred_element_type=jnp.float32)


def kernel(
    table_any, inverse_any, lengths_any, dest_any, long_lengths_any,
    k_long_any, v_long_any, q_short_any, k_short_any, v_short_any, q_long_any,
    bin_out, long_out,
    table, dest, inverse, lengths, long_lengths,
    k_long, v_long, q_short, k_short, v_short, q_long,
    pool_refs, stage, landing, kv, query, top, acc, bias_ref, bin_result, long_result,
    load_sem, out_sem, route_send, route_recv, y_send, y_recv,
):
    dp, ctx = lax.axis_index("dp"), lax.axis_index("ctx")
    core, x, z = dp % 2, (dp // 2) % NX, dp // (2 * NX)
    span = q_long.shape[0]

    loads = [
        (table_any.at[pl.ds(pl.multiple_of((dp // 2) * (NZ * NX * ROUTE), NZ * NX * ROUTE), NZ * NX * ROUTE)], table),
        (dest_any, dest),
        (inverse_any, inverse),
        (lengths_any, lengths),
        (long_lengths_any, long_lengths),
        (k_long_any, k_long),
        (v_long_any, v_long),
        (q_short_any, q_short),
        (k_short_any, k_short),
        (v_short_any, v_short),
        (q_long_any, q_long),
    ]
    loads = [pltpu.make_async_copy(a, b, load_sem.at[i]) for i, (a, b) in enumerate(loads)]
    for load in loads[2:] + loads[:2]:
        load.start()

    def at(z_to, x_to):
        return (((z_to + NZ) % NZ * NX + (x_to + NX) % NX) * 2 + core, ctx)

    routes = [at(z, x + 1), at(z, x - 1), at(z + 1, x), at(z - 1, x)]
    rings = [(dp, (ctx + 1) % NY), (dp, (ctx + NY - 1) % NY)]

    barrier = pltpu.get_barrier_semaphore()
    for other in [*routes, *rings]:
        pl.semaphore_signal(barrier, inc=1, device_id=other, device_id_type=MESH)

    def copy(source, target, send, recv, other):
        return pltpu.make_async_remote_copy(
            src_ref=source, dst_ref=target, send_sem=send, recv_sem=recv,
            device_id=other, device_id_type=MESH,
        )

    def ring_copy(n, way):
        hop = n // KVHEADS
        g = (n + way * (KVHEADS // 2)) % KVHEADS
        if way == 0:
            source, target = hop, hop + 1
        else:
            source = jnp.where(hop == 0, 0, hop + HOPS)
            target = jnp.where(hop == HOPS - 1, HOPS, hop + HOPS + 1)
        return copy(
            kv.at[source, g], kv.at[target, g], y_send.at[way, n], y_recv.at[way, n], rings[way]
        )

    for load in loads[2:5]:
        load.wait()
    row = lax.broadcasted_iota(jnp.int32, (span, HEAD_DIM), 0)
    lane = lax.broadcasted_iota(jnp.int32, (span, HEAD_DIM), 1)
    mine = lax.broadcasted_iota(jnp.int32, lengths.shape[2:], 1) == dp
    home = [jnp.sum(jnp.where(mine, lengths[0, d], 0), axis=1, keepdims=True) for d in range(2)]
    first = jnp.where(row < BIN_LEN, home[0][0:1], home[0][1:2])
    second = first + jnp.where(row < BIN_LEN, home[1][0:1], home[1][1:2])
    token = row % BIN_LEN
    short_start = doc_start(first, second, token)
    my_row = row + ctx * span
    first = long_lengths[:, 0:1]
    long_start = doc_start(first, first + long_lengths[:, 1:2], my_row)
    position = jnp.where(lane < HALF, token - short_start, my_row - long_start)
    cosine, sine = turns(position.astype(jnp.float32) * inverse[...])
    cosine_swap, sine_swap = pltpu.roll(cosine, HALF, 1), pltpu.roll(sine, HALF, 1)
    low = lane < HALF
    short_cos, short_sin = jnp.where(low, cosine, cosine_swap), jnp.where(low, -sine, sine_swap)
    long_cos, long_sin = jnp.where(low, cosine_swap, cosine), jnp.where(low, -sine_swap, sine)

    for load in loads[5:7]:
        load.wait()
    for g in range(KVHEADS):
        kv[0, g, :, :HEAD_DIM] = rotated(k_long[:, lanes(g, HEAD_DIM)], long_cos, long_sin)
        kv[0, g, :, HEAD_DIM:] = v_long[:, lanes(g, HEAD_DIM)]
    pl.semaphore_wait(barrier, 2 + DIRS)
    for n in range(KVHEADS):
        for way in range(2):
            ring_copy(n, way).start()

    pools = [*pool_refs]
    streams = range(BINS * HALVES)

    for load in loads[7:10]:
        load.wait()

    def bias_of(rows, reach):
        index = lane[rows] % reach
        allowed = (index >= short_start[rows]) & (index <= token[rows])
        return jnp.concatenate([jnp.where(allowed, 0.0, NEGATIVE)] * GROUP, 0)

    spot = lane[:EARLY]
    for j in range(BINS):
        rows = slice(j * BIN_LEN, (j + 1) * BIN_LEN)
        early = slice(j * BIN_LEN, j * BIN_LEN + EARLY)
        late = slice(j * BIN_LEN + EARLY, (j + 1) * BIN_LEN)
        early_bias, late_bias = bias_of(early, EARLY), bias_of(late, BIN_LEN)
        early_scores, late_scores = [], []
        for g in range(CHUNKS):
            heads = [
                rotated(q_short[rows, lanes(g * GROUP + i, HEAD_DIM)], short_cos[rows], short_sin[rows])
                for i in range(GROUP)
            ]
            key = rotated(k_short[rows, lanes(g, HEAD_DIM)], short_cos[rows], short_sin[rows])
            first = jnp.concatenate([q[:EARLY] for q in heads], 0)
            second = jnp.concatenate([q[EARLY:] for q in heads], 0)
            keys = jnp.concatenate([key[:EARLY]] * GROUP, 0)
            early_scores.append(score(first, keys) + early_bias)
            late_scores.append(score(second, jnp.concatenate([key] * 2, 0)) + late_bias)
        scores = jnp.concatenate(early_scores + late_scores, 0)
        weight = jnp.exp2(scores - jnp.max(scores, axis=1, keepdims=True))
        for g in range(CHUNKS):
            w = [weight[(g * GROUP + i) * EARLY :][:EARLY] for i in range(GROUP)]
            packed = w[0]
            for i in range(1, GROUP):
                packed = jnp.where(spot // EARLY == i, w[i], packed)
            w = [weight[((CHUNKS + g) * GROUP + i) * EARLY :][:EARLY] for i in range(GROUP)]
            left = jnp.where(spot < BIN_LEN, w[0], w[1])
            right = jnp.where(spot < BIN_LEN, w[2], w[3])
            pieces = [
                packed.astype(jnp.bfloat16), v_short[early, lanes(g, HEAD_DIM)],
                jnp.concatenate([left, right], 1).astype(jnp.bfloat16), v_short[late, lanes(g, HEAD_DIM)],
            ]
            for h in range(HALVES):
                for i, piece in enumerate(pieces):
                    part = slice(CUTS[i], CUTS[i + 1])
                    pools[j * HALVES + h][g, :, part] = piece[h * ROWS : (h + 1) * ROWS]
    for load in loads[:2]:
        load.wait()
    masks = [dest[0, j, 0] for j in range(BINS)]

    def entry(t, place):
        return table[(masks[t // HALVES] >> 1) * ROUTE + place]

    def route_copy(slot, d):
        return copy(
            stage.at[slot, d], landing.at[slot, d], route_send.at[slot], route_recv.at[slot], routes[d]
        )

    def all_of(slot):
        return copy(stage.at[slot], landing.at[slot], route_send.at[slot], route_recv.at[slot], routes[0])

    def collect(t, step):
        slot = len(streams) * step + t
        all_of(slot).wait_recv()
        for d in range(DIRS):
            pools[t][OWN + DIRS * step + d] = landing[slot, d]

    def send(t, step, entries):
        slot = len(streams) * step + t
        for d in range(DIRS):
            stage[slot, d] = pools[t][entries[d]]
            route_copy(slot, d).start()

    def ring(n):
        for way in range(2):
            ring_copy(n, way).wait()
        if n + KVHEADS < Y_SENDS:
            for way in range(2):
                ring_copy(n + KVHEADS, way).start()

    shift = [0] + [-h for h in range(1, HOPS + 1)] + [h for h in range(1, NY - HOPS)]

    def prepare(t):
        query[t] = stacked_heads(q_long, t, long_cos, long_sin)
        for i in (2 * t, 2 * t + 1):
            key_index = lane + (ctx + NY + shift[i]) % NY * span
            allowed = (key_index >= long_start) & (key_index <= my_row)
            bias_ref[i] = jnp.where(allowed, 0.0, NEGATIVE)

    def attend(heads, blocks):
        begins, ends = 0 in blocks, HOPS in blocks
        bias = jnp.concatenate([bias_ref[i] for i in blocks], 1)
        bias = jnp.concatenate([bias] * GROUP, 0)
        keys = [jnp.concatenate([kv[i, g, :, :HEAD_DIM] for i in blocks], 0) for g in heads]
        values = [jnp.concatenate([kv[i, g, :, HEAD_DIM:] for i in blocks], 0) for g in heads]
        scores = [score(query[g], k) + bias for g, k in zip(heads, keys)]
        peaks = [jnp.max(s, axis=1, keepdims=True) for s in scores]
        if not begins:
            olds = [top[g][:, :1] for g in heads]
            peaks = [jnp.maximum(peak, old) for peak, old in zip(peaks, olds)]
        weights = [jnp.exp2(s - peak) for s, peak in zip(scores, peaks)]
        blended = [blend(w, v) for w, v in zip(weights, values)]
        for n, g in enumerate(heads):
            both = blended[n]
            if not begins:
                both = both + acc[g] * jnp.exp2(olds[n] - peaks[n])
            if ends:
                result = (both[:, :HEAD_DIM] / both[:, HEAD_DIM:]).astype(jnp.bfloat16)
                for i in range(GROUP):
                    long_result[:, lanes(g * GROUP + i, HEAD_DIM)] = result[i * span : (i + 1) * span]
                long_copy(g).start()
            else:
                top[g] = jnp.broadcast_to(peaks[n], top.shape[1:])
                acc[g] = both

    def long_copy(g):
        return pltpu.make_async_copy(
            long_result.at[:, lanes_at(g, WIDE)], long_out.at[:, lanes_at(g, WIDE)], out_sem.at[BINS * CHUNKS + g]
        )

    def bin_copy(m, g):
        return pltpu.make_async_copy(bin_result.at[m, g], bin_out.at[m, g], out_sem.at[m * CHUNKS + g])

    near = [0, 1, HOPS + 1]
    middle = [2, HOPS + 2]
    third = [3, HOPS + 3]
    far = [HOPS]

    plan = [
        [(prepare, 0)],
        [(ring, 0), (prepare, 1)],
        [(ring, 1), (prepare, 2)],
        [(ring, 2), (prepare, 3)],
        [(ring, 3), (attend, [0, 1], near)],
        [(ring, 4)],
        [(ring, 5), (attend, [2, 3], near)],
        [(ring, 6)],
        [(ring, 7)],
        [(ring, 8), (attend, [0, 1], middle)],
        [(ring, 9)],
        [(ring, 10), (attend, [2, 3], middle)],
        [(ring, 11)],
        [(ring, 12)],
        [(attend, [0, 2], third + far)],
        [(ring, 13), (attend, [1, 3], third + far)],
    ]

    def work(tasks):
        for task, *arguments in tasks:
            task(*arguments)

    loads[10].wait()
    for step in range(STEPS):
        for t in streams:
            entries = [entry(t, step * DIRS + d) for d in range(DIRS)]
            if step > 0:
                collect(t, step - 1)
            send(t, step, entries)
            if t % HALVES == 0:
                work(plan[2 * step + t // HALVES])
            if step > 0:
                all_of(len(streams) * (step - 1) + t).wait_send()

    for t in streams:
        collect(t, STEPS - 1)

    for j in range(BINS):
        for g in range(CHUNKS):
            bin_result[j, g] = jnp.concatenate(
                [pools[t][entry(t, DIRS * STEPS + g)] for t in range(j * HALVES, (j + 1) * HALVES)], 0
            )
            bin_copy(j, g).start()

    for t in streams:
        all_of(len(streams) * (STEPS - 1) + t).wait_send()

    for g in range(CHUNKS):
        long_copy(g).wait()
        for m in range(BINS):
            bin_copy(m, g).wait()


def hand_over(long_any, out_long, long, sem_in, sem_out):
    rows = long.shape[0] // PIECES
    pieces = []
    for p in range(PIECES):
        part = pl.ds(p * rows, rows)
        load = pltpu.make_async_copy(long_any.at[part], long.at[part], sem_in.at[p])
        load.start()
        pieces.append((load, pltpu.make_async_copy(long.at[part], out_long.at[part], sem_out.at[p])))
    for load, store in pieces:
        load.wait()
        store.start()
    for _, store in pieces:
        store.wait()


def finish(dest_any, bins_any, mate_any, out_short, dest, bins, short, dest_sem, sem_in, sem_out):
    pieces = []
    for m in range(BINS):
        part = pl.ds(m * BIN_LEN, BIN_LEN)
        load = pltpu.make_async_copy((bins_any, mate_any)[m], bins.at[m], sem_in.at[m])
        load.start()
        pieces.append((load, pltpu.make_async_copy(short.at[part], out_short.at[part], sem_out.at[m])))

    dest_copy = pltpu.make_async_copy(dest_any, dest, dest_sem)
    dest_copy.start()

    spot = lax.broadcasted_iota(jnp.int32, (EARLY, HEAD_DIM), 1)

    def chosen(test):
        return jnp.where(test, 1.0, 0.0).astype(jnp.bfloat16)

    quarter = [chosen(spot // EARLY == i) for i in range(GROUP)]
    side = [chosen(spot < BIN_LEN), chosen(spot >= BIN_LEN)]

    def finished(weight, values):
        blended = blend(weight, values)
        result = (blended[:, :HEAD_DIM] / blended[:, HEAD_DIM:]).astype(jnp.bfloat16)
        return jnp.concatenate([result[i * EARLY : (i + 1) * EARLY] for i in range(GROUP)], 1)

    dest_copy.wait()
    for m in range(2):
        pieces[m][0].wait()
    dp = lax.axis_index("dp")
    masks = [dest[0, j, 0] for j in range(BINS)]
    swap = jnp.where((dp ^ masks[0]) > (dp ^ masks[1]), 1, 0)
    for m in range(BINS):
        j = m ^ swap
        crossed = jnp.where(j == 0, masks[0], masks[1]) & 1
        for g in range(CHUNKS):
            chunk = bins[crossed, j, g]
            first, first_v, second, second_v = [chunk[:, CUTS[i] : CUTS[i + 1]] for i in range(4)]
            early = jnp.concatenate([first * q for q in quarter], 0)
            late = [second[:, lanes(i // 2, HEAD_DIM)] * side[i % 2] for i in range(GROUP)]
            late = jnp.concatenate(late, 0)
            start = m * BIN_LEN
            short[start : start + EARLY, lanes(g, WIDE)] = finished(
                early, jnp.concatenate([first_v] * GROUP, 0)
            )
            short[start + EARLY : start + BIN_LEN, lanes(g, WIDE)] = finished(
                late, jnp.concatenate([first_v, second_v] * 2, 0)
            )
        pieces[m][1].start()
    for _, store in pieces:
        store.wait()


HBM = pl.BlockSpec(memory_space=pltpu.HBM)
ANY = pl.BlockSpec(memory_space=pl.ANY)


def local(q_short, k_short, v_short, short_lengths, bin_dest, q_long, k_long, v_long, long_lengths):
    span = q_long.shape[0]
    table = jnp.asarray(route_table())
    inverse = jnp.asarray(np.concatenate([INVERSE, INVERSE])[None, :])
    lengths = jnp.transpose(short_lengths, (1, 3, 2, 0))
    dest = jnp.transpose(bin_dest, (1, 2, 0))

    bf16, f32, i32 = jnp.bfloat16, jnp.float32, jnp.int32
    slots = BINS * HALVES * STEPS
    dma = pltpu.SemaphoreType.DMA
    inputs = [k_long, v_long, q_short, k_short, v_short, q_long]
    bins_shape = (BINS, CHUNKS, EARLY, CUTS[-1])
    bins, long = pl.pallas_call(
        kernel,
        out_shape=[jax.ShapeDtypeStruct(bins_shape, bf16), jax.ShapeDtypeStruct(q_long.shape, bf16)],
        in_specs=[HBM] * 11,
        out_specs=[HBM, HBM],
        scratch_shapes=[
            pltpu.SMEM((NZ * NX * ROUTE,), i32),
            pltpu.SMEM(dest.shape, i32),
            pltpu.VMEM(inverse.shape, f32),
            pltpu.VMEM(lengths.shape, i32),
            pltpu.VMEM(long_lengths.shape, i32),
            *[pltpu.VMEM(a.shape, bf16) for a in inputs],
            [pltpu.VMEM((POOL, ROWS, CUTS[-1]), bf16)] * (BINS * HALVES),
            pltpu.VMEM((slots, DIRS, ROWS, CUTS[-1]), bf16),
            pltpu.VMEM((slots, DIRS, ROWS, CUTS[-1]), bf16),
            pltpu.VMEM((NY, KVHEADS, span, 2 * HEAD_DIM), bf16),
            pltpu.VMEM((KVHEADS, GROUP * span, HEAD_DIM), bf16),
            pltpu.VMEM((KVHEADS, GROUP * span, HEAD_DIM), f32),
            pltpu.VMEM((KVHEADS, GROUP * span, 2 * HEAD_DIM), f32),
            pltpu.VMEM((NY, span, span), f32),
            pltpu.VMEM(bins_shape, bf16),
            pltpu.VMEM(q_long.shape, bf16),
            dma((11,)),
            dma((BINS * CHUNKS + KVHEADS,)),
            dma((slots,)),
            dma((slots,)),
            dma((2, Y_SENDS)),
            dma((2, Y_SENDS)),
        ],
        compiler_params=pltpu.CompilerParams(
            collective_id=0, has_side_effects=True, vmem_limit_bytes=56 * 2**20
        ),
    )(table, inverse, lengths, dest, long_lengths, *inputs)
    mate_bins = lax.ppermute(bins, "dp", [(i, i ^ 1) for i in range(lax.axis_size("dp"))])
    out_long = pl.pallas_call(
        hand_over,
        out_shape=jax.ShapeDtypeStruct(q_long.shape, bf16),
        in_specs=[ANY],
        out_specs=HBM,
        scratch_shapes=[pltpu.VMEM(q_long.shape, bf16), dma((PIECES,)), dma((PIECES,))],
        compiler_params=pltpu.CompilerParams(vmem_limit_bytes=56 * 2**20),
        cost_estimate=pl.CostEstimate(flops=0, bytes_accessed=4 * q_long.size, transcendentals=0),
    )(long)
    out_short = pl.pallas_call(
        finish,
        out_shape=jax.ShapeDtypeStruct(q_short.shape, bf16),
        in_specs=[ANY] * 3,
        out_specs=HBM,
        scratch_shapes=[
            pltpu.SMEM(dest.shape, i32),
            pltpu.VMEM((2, *bins_shape), bf16),
            pltpu.VMEM(q_short.shape, bf16),
            dma,
            dma((2,)),
            dma((BINS,)),
        ],
        compiler_params=pltpu.CompilerParams(vmem_limit_bytes=24 * 2**20),
    )(dest, bins, mate_bins)
    return (out_short, out_long)


def solution(mesh):
    in_specs = (
        P(("dp", "ctx"), None),
        P(("dp", "ctx"), None),
        P(("dp", "ctx"), None),
        P(None, "ctx", None, None),
        P(None, "ctx", None),
        P(("dp", "ctx"), None),
        P(("dp", "ctx"), None),
        P(("dp", "ctx"), None),
        P("dp", None),
    )
    out_specs = (P(("dp", "ctx"), None), P(("dp", "ctx"), None))
    return jax.shard_map(local, mesh=mesh, in_specs=in_specs, out_specs=out_specs, check_vma=False)
```

```python
import functools
import math

import jax
import jax.numpy as jnp
import numpy as np
from jax import lax
from jax.experimental import pallas as pl
from jax.experimental.pallas import tpu as pltpu
from jax.sharding import PartitionSpec as P

QHEADS = 16
KVHEADS = 4
GROUP = QHEADS // KVHEADS
HEAD_DIM = 128
HALF = HEAD_DIM // 2
WIDE = GROUP * HEAD_DIM
BIN_LEN = 64
BINS = 2
THETA = 500000.0
NEGATIVE = -1e30
SCALE = math.log2(math.e) / math.sqrt(HEAD_DIM)

NZ, NX, NY = 8, 4, 8
HALVES = 2
EARLY = BIN_LEN // 2
ROWS = EARLY // HALVES
CUTS = (0, HEAD_DIM, 2 * HEAD_DIM, 4 * HEAD_DIM, 5 * HEAD_DIM)
CHUNKS = KVHEADS
STEPS = 8
DIRS = 4
OWN = 2 * CHUNKS
POOL = OWN + DIRS * STEPS
PIECES = 4
ROUTE = 64
HOPS = NY // 2
Y_SENDS = 3 * KVHEADS + KVHEADS // 2
MESH = pl.DeviceIdType.MESH


def moved(place, direction):
    z, x = divmod(place, NX)
    if direction < 2:
        x = (x + (1, -1)[direction]) % NX
    else:
        z = (z + (1, -1)[direction - 2]) % NZ
    return z * NX + x


@functools.cache
def route_table():
    table = np.zeros((NZ * NX, NZ * NX, ROUTE), np.int32)
    for mask in range(NZ * NX):
        packets = []
        for place in range(NZ * NX):
            z, x = divmod(place, NX)
            goal_z, goal_x = divmod(place ^ mask, NX)
            for chunk in range(CHUNKS):
                dz, dx = (goal_z - z) % NZ, (goal_x - x) % NX
                if dz > NZ // 2 or (dz == NZ // 2 and chunk % 2):
                    dz -= NZ
                if dx > NX // 2 or (dx == NX // 2 and (chunk // (2 if mask // NX == NZ // 2 else 1)) % 2):
                    dx -= NX
                packets.append([place, dz, dx, chunk, chunk])
        step = 0
        while any(p[1] or p[2] for p in packets):
            order = sorted(packets, key=lambda p: (-abs(p[1]) - abs(p[2]), -abs(p[1]), p[4]))
            taken, moves = set(), []
            for p in order:
                options = []
                if p[1]:
                    options.append(2 if p[1] > 0 else 3)
                if p[2]:
                    options.append(0 if p[2] > 0 else 1)
                for d in options:
                    if (p[0], d) not in taken:
                        taken.add((p[0], d))
                        moves.append((p, d))
                        break
            for p, d in moves:
                table[mask, p[0], step * DIRS + d] = p[3]
                p[0] = moved(p[0], d)
                p[2 if d < 2 else 1] -= (1, -1)[d % 2]
                p[3] = OWN + DIRS * step + d
            step += 1
        assert step <= STEPS
        for p in packets:
            table[mask, p[0], DIRS * STEPS + p[4]] = p[3]
    return np.ascontiguousarray(table.transpose(1, 0, 2)).reshape(-1)


INVERSE = np.power(THETA, -np.arange(HALF, dtype=np.float64) * (2.0 / HEAD_DIM)).astype(np.float32)
QUARTER1 = float(np.float32(1.5703125))
QUARTER2 = float(np.float32(math.floor((math.pi / 2 - QUARTER1) * 2**23) / 2**23))
QUARTER3 = float(np.float32(math.pi / 2 - QUARTER1 - QUARTER2))


def turns(angle):
    quarters = jnp.floor(angle * (2.0 / math.pi) + 0.5)
    r = ((angle - quarters * QUARTER1) - quarters * QUARTER2) - quarters * QUARTER3
    s = r * r
    sine = 1.0 / 362880
    for k in (-1.0 / 5040, 1.0 / 120, -1.0 / 6):
        sine = sine * s + k
    sine = r + r * s * sine
    cosine = 1.0 / 40320
    for k in (-1.0 / 720, 1.0 / 24, -0.5, 1.0):
        cosine = cosine * s + k
    count = quarters.astype(jnp.int32)
    odd, turned = (count & 1) == 1, (count & 2) == 2
    first, second = jnp.where(odd, sine, cosine), jnp.where(odd, cosine, sine)
    flip = turned != odd
    return jnp.where(flip, -first, first), jnp.where(turned, -second, second)


def doc_start(first, second, index):
    return jnp.where(index >= second, second, jnp.where(index >= first, first, 0))


def rotated(block, cosine, sine):
    wide = block.astype(jnp.float32)
    return (wide * cosine + pltpu.roll(wide, HALF, 1) * sine).astype(jnp.bfloat16)


def lanes(i, width):
    return slice(i * width, (i + 1) * width)


def lanes_at(i, width):
    return pl.ds(i * width, width)


def stacked_heads(q_ref, g, cosine, sine):
    heads = range(g * GROUP, (g + 1) * GROUP)
    return jnp.concatenate([rotated(q_ref[:, lanes(h, HEAD_DIM)], cosine, sine) for h in heads], 0)


def score(query, key):
    return SCALE * lax.dot_general(
        query, key, (((1,), (1,)), ((), ())), preferred_element_type=jnp.float32
    )


def blend(weight, values):
    wide = jnp.concatenate([values, jnp.ones_like(values)], 1)
    return jnp.dot(weight.astype(jnp.bfloat16), wide, preferred_element_type=jnp.float32)


def kernel(
    table_any, inverse_any, lengths_any, dest_any, long_lengths_any,
    k_long_any, v_long_any, q_short_any, k_short_any, v_short_any, q_long_any,
    bin_out, long_out,
    table, dest, inverse, lengths, long_lengths,
    k_long, v_long, q_short, k_short, v_short, q_long,
    pool_refs, stage, landing, kv, query, top, acc, bias_ref, bin_result, long_result,
    load_sem, out_sem, mate_send, mate_recv, route_send, route_recv, y_send, y_recv,
):
    dp, ctx = lax.axis_index("dp"), lax.axis_index("ctx")
    core, x, z = dp % 2, (dp // 2) % NX, dp // (2 * NX)
    span = q_long.shape[0]

    loads = [
        (table_any.at[pl.ds(pl.multiple_of((dp // 2) * (NZ * NX * ROUTE), NZ * NX * ROUTE), NZ * NX * ROUTE)], table),
        (dest_any, dest),
        (inverse_any, inverse),
        (lengths_any, lengths),
        (long_lengths_any, long_lengths),
        (k_long_any, k_long),
        (v_long_any, v_long),
        (q_short_any, q_short),
        (k_short_any, k_short),
        (v_short_any, v_short),
        (q_long_any, q_long),
    ]
    loads = [pltpu.make_async_copy(a, b, load_sem.at[i]) for i, (a, b) in enumerate(loads)]
    for load in loads[2:] + loads[:2]:
        load.start()

    def at(z_to, x_to):
        return (((z_to + NZ) % NZ * NX + (x_to + NX) % NX) * 2 + core, ctx)

    mate = (dp + 1 - 2 * core, ctx)
    routes = [at(z, x + 1), at(z, x - 1), at(z + 1, x), at(z - 1, x)]
    rings = [(dp, (ctx + 1) % NY), (dp, (ctx + NY - 1) % NY)]

    barrier = pltpu.get_barrier_semaphore()
    for other in [mate, *routes, *rings]:
        pl.semaphore_signal(barrier, inc=1, device_id=other, device_id_type=MESH)

    def copy(source, target, send, recv, other):
        return pltpu.make_async_remote_copy(
            src_ref=source, dst_ref=target, send_sem=send, recv_sem=recv,
            device_id=other, device_id_type=MESH,
        )

    def ring_copy(n, way):
        hop = n // KVHEADS
        g = (n + way * (KVHEADS // 2)) % KVHEADS
        if way == 0:
            source, target = hop, hop + 1
        else:
            source = jnp.where(hop == 0, 0, hop + HOPS)
            target = jnp.where(hop == HOPS - 1, HOPS, hop + HOPS + 1)
        return copy(
            kv.at[source, g], kv.at[target, g], y_send.at[way, n], y_recv.at[way, n], rings[way]
        )

    for load in loads[2:5]:
        load.wait()
    row = lax.broadcasted_iota(jnp.int32, (span, HEAD_DIM), 0)
    lane = lax.broadcasted_iota(jnp.int32, (span, HEAD_DIM), 1)
    mine = lax.broadcasted_iota(jnp.int32, lengths.shape[2:], 1) == dp
    home = [jnp.sum(jnp.where(mine, lengths[0, d], 0), axis=1, keepdims=True) for d in range(2)]
    first = jnp.where(row < BIN_LEN, home[0][0:1], home[0][1:2])
    second = first + jnp.where(row < BIN_LEN, home[1][0:1], home[1][1:2])
    token = row % BIN_LEN
    short_start = doc_start(first, second, token)
    my_row = row + ctx * span
    first = long_lengths[:, 0:1]
    long_start = doc_start(first, first + long_lengths[:, 1:2], my_row)
    position = jnp.where(lane < HALF, token - short_start, my_row - long_start)
    cosine, sine = turns(position.astype(jnp.float32) * inverse[...])
    cosine_swap, sine_swap = pltpu.roll(cosine, HALF, 1), pltpu.roll(sine, HALF, 1)
    low = lane < HALF
    short_cos, short_sin = jnp.where(low, cosine, cosine_swap), jnp.where(low, -sine, sine_swap)
    long_cos, long_sin = jnp.where(low, cosine_swap, cosine), jnp.where(low, -sine_swap, sine)

    for load in loads[5:7]:
        load.wait()
    for g in range(KVHEADS):
        kv[0, g, :, :HEAD_DIM] = rotated(k_long[:, lanes(g, HEAD_DIM)], long_cos, long_sin)
        kv[0, g, :, HEAD_DIM:] = v_long[:, lanes(g, HEAD_DIM)]
    pl.semaphore_wait(barrier, 3 + DIRS)
    for n in range(KVHEADS):
        for way in range(2):
            ring_copy(n, way).start()

    pools = [*pool_refs]
    streams = range(BINS * HALVES)

    def mate_copy(t):
        return copy(
            pools[t].at[pl.ds(0, CHUNKS)], pools[t].at[pl.ds(CHUNKS, CHUNKS)],
            mate_send.at[t], mate_recv.at[t], mate,
        )

    for load in loads[7:10]:
        load.wait()

    def bias_of(rows, reach):
        index = lane[rows] % reach
        allowed = (index >= short_start[rows]) & (index <= token[rows])
        return jnp.concatenate([jnp.where(allowed, 0.0, NEGATIVE)] * GROUP, 0)

    spot = lane[:EARLY]
    for j in range(BINS):
        rows = slice(j * BIN_LEN, (j + 1) * BIN_LEN)
        early = slice(j * BIN_LEN, j * BIN_LEN + EARLY)
        late = slice(j * BIN_LEN + EARLY, (j + 1) * BIN_LEN)
        early_bias, late_bias = bias_of(early, EARLY), bias_of(late, BIN_LEN)
        early_scores, late_scores = [], []
        for g in range(CHUNKS):
            heads = [
                rotated(q_short[rows, lanes(g * GROUP + i, HEAD_DIM)], short_cos[rows], short_sin[rows])
                for i in range(GROUP)
            ]
            key = rotated(k_short[rows, lanes(g, HEAD_DIM)], short_cos[rows], short_sin[rows])
            first = jnp.concatenate([q[:EARLY] for q in heads], 0)
            second = jnp.concatenate([q[EARLY:] for q in heads], 0)
            keys = jnp.concatenate([key[:EARLY]] * GROUP, 0)
            early_scores.append(score(first, keys) + early_bias)
            late_scores.append(score(second, jnp.concatenate([key] * 2, 0)) + late_bias)
        scores = jnp.concatenate(early_scores + late_scores, 0)
        weight = jnp.exp2(scores - jnp.max(scores, axis=1, keepdims=True))
        for g in range(CHUNKS):
            w = [weight[(g * GROUP + i) * EARLY :][:EARLY] for i in range(GROUP)]
            packed = w[0]
            for i in range(1, GROUP):
                packed = jnp.where(spot // EARLY == i, w[i], packed)
            w = [weight[((CHUNKS + g) * GROUP + i) * EARLY :][:EARLY] for i in range(GROUP)]
            left = jnp.where(spot < BIN_LEN, w[0], w[1])
            right = jnp.where(spot < BIN_LEN, w[2], w[3])
            pieces = [
                packed.astype(jnp.bfloat16), v_short[early, lanes(g, HEAD_DIM)],
                jnp.concatenate([left, right], 1).astype(jnp.bfloat16), v_short[late, lanes(g, HEAD_DIM)],
            ]
            for h in range(HALVES):
                for i, piece in enumerate(pieces):
                    part = slice(CUTS[i], CUTS[i + 1])
                    pools[j * HALVES + h][g, :, part] = piece[h * ROWS : (h + 1) * ROWS]
        for h in range(HALVES):
            mate_copy(j * HALVES + h).start()

    for load in loads[:2]:
        load.wait()
    masks = [dest[0, j, 0] for j in range(BINS)]

    def entry(t, place):
        mask = masks[t // HALVES]
        index = table[(mask >> 1) * ROUTE + place]
        return index + jnp.where(index < CHUNKS, (mask & 1) * CHUNKS, 0)

    def route_copy(slot, d):
        return copy(
            stage.at[slot, d], landing.at[slot, d], route_send.at[slot], route_recv.at[slot], routes[d]
        )

    def all_of(slot):
        return copy(stage.at[slot], landing.at[slot], route_send.at[slot], route_recv.at[slot], routes[0])

    def collect(t, step):
        slot = len(streams) * step + t
        all_of(slot).wait_recv()
        for d in range(DIRS):
            pools[t][OWN + DIRS * step + d] = landing[slot, d]

    def send(t, step, entries):
        slot = len(streams) * step + t
        for d in range(DIRS):
            stage[slot, d] = pools[t][entries[d]]
            route_copy(slot, d).start()

    def ring(n):
        for way in range(2):
            ring_copy(n, way).wait()
        if n + KVHEADS < Y_SENDS:
            for way in range(2):
                ring_copy(n + KVHEADS, way).start()

    shift = [0] + [-h for h in range(1, HOPS + 1)] + [h for h in range(1, NY - HOPS)]

    def prepare(t):
        query[t] = stacked_heads(q_long, t, long_cos, long_sin)
        for i in (2 * t, 2 * t + 1):
            key_index = lane + (ctx + NY + shift[i]) % NY * span
            allowed = (key_index >= long_start) & (key_index <= my_row)
            bias_ref[i] = jnp.where(allowed, 0.0, NEGATIVE)

    def attend(heads, blocks):
        begins, ends = 0 in blocks, HOPS in blocks
        bias = jnp.concatenate([bias_ref[i] for i in blocks], 1)
        bias = jnp.concatenate([bias] * GROUP, 0)
        keys = [jnp.concatenate([kv[i, g, :, :HEAD_DIM] for i in blocks], 0) for g in heads]
        values = [jnp.concatenate([kv[i, g, :, HEAD_DIM:] for i in blocks], 0) for g in heads]
        scores = [score(query[g], k) + bias for g, k in zip(heads, keys)]
        peaks = [jnp.max(s, axis=1, keepdims=True) for s in scores]
        if not begins:
            olds = [top[g][:, :1] for g in heads]
            peaks = [jnp.maximum(peak, old) for peak, old in zip(peaks, olds)]
        weights = [jnp.exp2(s - peak) for s, peak in zip(scores, peaks)]
        blended = [blend(w, v) for w, v in zip(weights, values)]
        for n, g in enumerate(heads):
            both = blended[n]
            if not begins:
                both = both + acc[g] * jnp.exp2(olds[n] - peaks[n])
            if ends:
                result = (both[:, :HEAD_DIM] / both[:, HEAD_DIM:]).astype(jnp.bfloat16)
                for i in range(GROUP):
                    long_result[:, lanes(g * GROUP + i, HEAD_DIM)] = result[i * span : (i + 1) * span]
                long_copy(g).start()
            else:
                top[g] = jnp.broadcast_to(peaks[n], top.shape[1:])
                acc[g] = both

    def long_copy(g):
        return pltpu.make_async_copy(
            long_result.at[:, lanes_at(g, WIDE)], long_out.at[:, lanes_at(g, WIDE)], out_sem.at[BINS * CHUNKS + g]
        )

    def bin_copy(m, g):
        return pltpu.make_async_copy(bin_result.at[m, g], bin_out.at[m, g], out_sem.at[m * CHUNKS + g])

    near = [0, 1, HOPS + 1]
    middle = [2, HOPS + 2]
    third = [3, HOPS + 3]
    far = [HOPS]

    nearer, rest = [near, middle], third + far
    plan = [[(prepare, 0)], [(prepare, 1)], [(prepare, 2)], [(prepare, 3)]]
    plan += [[(attend, [g], blocks)] for blocks in nearer for g in range(KVHEADS)]
    plan += [[], [(attend, [0], rest)], [(attend, [2], rest)], [(attend, [1], rest)]]

    def work(tasks):
        for task, *arguments in tasks:
            task(*arguments)

    loads[10].wait()
    for step in range(STEPS):
        for t in streams:
            entries = [entry(t, step * DIRS + d) for d in range(DIRS)]
            if step == 0:
                mate_copy(t).wait()
            else:
                collect(t, step - 1)
            send(t, step, entries)
            phase = 2 * step + t // HALVES
            if t % HALVES == 0 and 0 < phase <= Y_SENDS:
                ring(phase - 1)
            if t % HALVES == HALVES - 1:
                work(plan[phase])
            if step > 0:
                all_of(len(streams) * (step - 1) + t).wait_send()

    attend([3], rest)
    for t in streams:
        collect(t, STEPS - 1)

    swap = (dp ^ masks[0]) > (dp ^ masks[1])
    for g in range(CHUNKS):
        chunks = [
            jnp.concatenate(
                [pools[t][entry(t, DIRS * STEPS + g)] for t in range(j * HALVES, (j + 1) * HALVES)], 0
            )
            for j in range(BINS)
        ]
        bin_result[0, g] = jnp.where(swap, chunks[1], chunks[0])
        bin_result[1, g] = jnp.where(swap, chunks[0], chunks[1])
        for m in range(BINS):
            bin_copy(m, g).start()
    for t in streams:
        all_of(len(streams) * (STEPS - 1) + t).wait_send()

    for g in range(CHUNKS):
        long_copy(g).wait()
        for m in range(BINS):
            bin_copy(m, g).wait()


def finish(bins_any, long_any, out_short, out_long, bins, short, long, sem_in, sem_out):
    rows = long.shape[0] // PIECES

    def long_copies(p):
        part = pl.ds(p * rows, rows)
        return (
            pltpu.make_async_copy(long_any.at[part], long.at[part], sem_in.at[BINS + p]),
            pltpu.make_async_copy(long.at[part], out_long.at[part], sem_out.at[BINS + p]),
        )

    def short_copies(m):
        part = pl.ds(m * BIN_LEN, BIN_LEN)
        return (
            pltpu.make_async_copy(bins_any.at[m], bins.at[m], sem_in.at[m]),
            pltpu.make_async_copy(short.at[part], out_short.at[part], sem_out.at[m]),
        )

    pieces = [short_copies(m) for m in range(BINS)] + [long_copies(p) for p in range(PIECES)]
    for load, _ in pieces:
        load.start()

    spot = lax.broadcasted_iota(jnp.int32, (EARLY, HEAD_DIM), 1)

    def chosen(test):
        return jnp.where(test, 1.0, 0.0).astype(jnp.bfloat16)

    quarter = [chosen(spot // EARLY == i) for i in range(GROUP)]
    side = [chosen(spot < BIN_LEN), chosen(spot >= BIN_LEN)]

    def finished(weight, values):
        blended = blend(weight, values)
        result = (blended[:, :HEAD_DIM] / blended[:, HEAD_DIM:]).astype(jnp.bfloat16)
        return jnp.concatenate([result[i * EARLY : (i + 1) * EARLY] for i in range(GROUP)], 1)

    for m in range(BINS):
        pieces[m][0].wait()
        for g in range(CHUNKS):
            chunk = bins[m, g]
            first, first_v, second, second_v = [chunk[:, CUTS[i] : CUTS[i + 1]] for i in range(4)]
            early = jnp.concatenate([first * q for q in quarter], 0)
            late = [second[:, lanes(i // 2, HEAD_DIM)] * side[i % 2] for i in range(GROUP)]
            late = jnp.concatenate(late, 0)
            start = m * BIN_LEN
            short[start : start + EARLY, lanes(g, WIDE)] = finished(
                early, jnp.concatenate([first_v] * GROUP, 0)
            )
            short[start + EARLY : start + BIN_LEN, lanes(g, WIDE)] = finished(
                late, jnp.concatenate([first_v, second_v] * 2, 0)
            )
        if m == 0:
            for load, store in pieces[BINS:]:
                load.wait()
                store.start()
        pieces[m][1].start()
    for _, store in pieces:
        store.wait()


HBM = pl.BlockSpec(memory_space=pltpu.HBM)


def local(q_short, k_short, v_short, short_lengths, bin_dest, q_long, k_long, v_long, long_lengths):
    span = q_long.shape[0]
    table = jnp.asarray(route_table())
    inverse = jnp.asarray(np.concatenate([INVERSE, INVERSE])[None, :])
    lengths = jnp.transpose(short_lengths, (1, 3, 2, 0))
    dest = jnp.transpose(bin_dest, (1, 2, 0))

    bf16, f32, i32 = jnp.bfloat16, jnp.float32, jnp.int32
    slots = BINS * HALVES * STEPS
    dma = pltpu.SemaphoreType.DMA
    inputs = [k_long, v_long, q_short, k_short, v_short, q_long]
    bins_shape = (BINS, CHUNKS, EARLY, CUTS[-1])
    bins, long = pl.pallas_call(
        kernel,
        out_shape=[jax.ShapeDtypeStruct(bins_shape, bf16), jax.ShapeDtypeStruct(q_long.shape, bf16)],
        in_specs=[HBM] * 11,
        out_specs=[HBM, HBM],
        scratch_shapes=[
            pltpu.SMEM((NZ * NX * ROUTE,), i32),
            pltpu.SMEM(dest.shape, i32),
            pltpu.VMEM(inverse.shape, f32),
            pltpu.VMEM(lengths.shape, i32),
            pltpu.VMEM(long_lengths.shape, i32),
            *[pltpu.VMEM(a.shape, bf16) for a in inputs],
            [pltpu.VMEM((POOL, ROWS, CUTS[-1]), bf16)] * (BINS * HALVES),
            pltpu.VMEM((slots, DIRS, ROWS, CUTS[-1]), bf16),
            pltpu.VMEM((slots, DIRS, ROWS, CUTS[-1]), bf16),
            pltpu.VMEM((NY, KVHEADS, span, 2 * HEAD_DIM), bf16),
            pltpu.VMEM((KVHEADS, GROUP * span, HEAD_DIM), bf16),
            pltpu.VMEM((KVHEADS, GROUP * span, HEAD_DIM), f32),
            pltpu.VMEM((KVHEADS, GROUP * span, 2 * HEAD_DIM), f32),
            pltpu.VMEM((NY, span, span), f32),
            pltpu.VMEM(bins_shape, bf16),
            pltpu.VMEM(q_long.shape, bf16),
            dma((11,)),
            dma((BINS * CHUNKS + KVHEADS,)),
            dma((BINS * HALVES,)),
            dma((BINS * HALVES,)),
            dma((slots,)),
            dma((slots,)),
            dma((2, Y_SENDS)),
            dma((2, Y_SENDS)),
        ],
        compiler_params=pltpu.CompilerParams(
            collective_id=0, has_side_effects=True, vmem_limit_bytes=56 * 2**20
        ),
    )(table, inverse, lengths, dest, long_lengths, *inputs)
    return pl.pallas_call(
        finish,
        out_shape=[jax.ShapeDtypeStruct(q_short.shape, bf16), jax.ShapeDtypeStruct(q_long.shape, bf16)],
        in_specs=[HBM, HBM],
        out_specs=[HBM, HBM],
        scratch_shapes=[
            pltpu.VMEM(bins_shape, bf16),
            pltpu.VMEM(q_short.shape, bf16),
            pltpu.VMEM(q_long.shape, bf16),
            dma((BINS + PIECES,)),
            dma((BINS + PIECES,)),
        ],
        compiler_params=pltpu.CompilerParams(vmem_limit_bytes=56 * 2**20),
    )(bins, long)


def solution(mesh):
    in_specs = (
        P(("dp", "ctx"), None),
        P(("dp", "ctx"), None),
        P(("dp", "ctx"), None),
        P(None, "ctx", None, None),
        P(None, "ctx", None),
        P(("dp", "ctx"), None),
        P(("dp", "ctx"), None),
        P(("dp", "ctx"), None),
        P("dp", None),
    )
    out_specs = (P(("dp", "ctx"), None), P(("dp", "ctx"), None))
    return jax.shard_map(local, mesh=mesh, in_specs=in_specs, out_specs=out_specs, check_vma=False)
```

```python
import functools
import math

import jax
import jax.numpy as jnp
import numpy as np
from jax import lax
from jax.experimental import pallas as pl
from jax.experimental.pallas import tpu as pltpu
from jax.sharding import PartitionSpec as P

QHEADS = 16
KVHEADS = 4
GROUP = QHEADS // KVHEADS
HEAD_DIM = 128
HALF = HEAD_DIM // 2
WIDE = GROUP * HEAD_DIM
BIN_LEN = 64
BINS = 2
THETA = 500000.0
NEGATIVE = -1e30
SCALE = math.log2(math.e) / math.sqrt(HEAD_DIM)

NZ, NX, NY = 8, 4, 8
HALVES = 2
EARLY = BIN_LEN // 2
ROWS = EARLY // HALVES
CUTS = (0, HEAD_DIM, 2 * HEAD_DIM, 4 * HEAD_DIM, 5 * HEAD_DIM)
CHUNKS = KVHEADS
STEPS = 8
X_STEPS = 6
DIRS = 4
OWN = 2 * CHUNKS
POOL = OWN + DIRS * STEPS
PIECES = 4
ROUTE = 64
HOPS = NY // 2
Y_SENDS = 3 * KVHEADS + KVHEADS // 2
MESH = pl.DeviceIdType.MESH


def moved(place, direction):
    z, x = divmod(place, NX)
    if direction < 2:
        x = (x + (1, -1)[direction]) % NX
    else:
        z = (z + (1, -1)[direction - 2]) % NZ
    return z * NX + x


def routed(mask, x_first, spread, key):
    packets = []
    for place in range(NZ * NX):
        z, x = divmod(place, NX)
        goal_z, goal_x = divmod(place ^ mask, NX)
        for chunk in range(CHUNKS):
            dz, dx = (goal_z - z) % NZ, (goal_x - x) % NX
            if dz > NZ // 2 or (dz == NZ // 2 and chunk % 2):
                dz -= NZ
            if dx > NX // 2 or (dx == NX // 2 and (chunk // spread) % 2):
                dx -= NX
            packets.append([place, dz, dx, chunk, chunk])
    sends = []
    for step in range(STEPS):
        taken, moves = set(), []
        for p in sorted(packets, key=key):
            along_z = [2 if p[1] > 0 else 3] if p[1] else []
            along_x = [0 if p[2] > 0 else 1] if p[2] and step < X_STEPS else []
            for d in along_x + along_z if x_first else along_z + along_x:
                if (p[0], d) not in taken:
                    taken.add((p[0], d))
                    moves.append((p, d))
                    break
        for p, d in moves:
            sends.append((p[0], step * DIRS + d, p[3]))
            p[0] = moved(p[0], d)
            p[2 if d < 2 else 1] -= (1, -1)[d % 2]
            p[3] = OWN + DIRS * step + d
    if any(p[1] or p[2] for p in packets):
        return None
    return sends + [(p[0], DIRS * STEPS + p[4], p[3]) for p in packets]


@functools.cache
def route_table():
    keys = [
        lambda p: (-abs(p[1]) - abs(p[2]), -abs(p[1]), p[4]),
        lambda p: (-abs(p[2]), -abs(p[1]), p[4]),
        lambda p: (-abs(p[1]) - abs(p[2]), -abs(p[2]), p[4]),
        lambda p: (-abs(p[1]), -abs(p[2]), p[4]),
    ]
    table = np.zeros((NZ * NX, NZ * NX, ROUTE), np.int32)
    for mask in range(NZ * NX):
        tries = ((x_first, spread, key) for x_first in (0, 1) for spread in (1, 2) for key in keys)
        found = next(r for r in (routed(mask, *t) for t in tries) if r is not None)
        for place, slot, entry in found:
            table[place, mask, slot] = entry
    return table.reshape(-1)


INVERSE = np.power(THETA, -np.arange(HALF, dtype=np.float64) * (2.0 / HEAD_DIM)).astype(np.float32)
QUARTER1 = float(np.float32(1.5703125))
QUARTER2 = float(np.float32(math.floor((math.pi / 2 - QUARTER1) * 2**23) / 2**23))
QUARTER3 = float(np.float32(math.pi / 2 - QUARTER1 - QUARTER2))


def turns(angle):
    quarters = jnp.floor(angle * (2.0 / math.pi) + 0.5)
    r = ((angle - quarters * QUARTER1) - quarters * QUARTER2) - quarters * QUARTER3
    s = r * r
    sine = 1.0 / 362880
    for k in (-1.0 / 5040, 1.0 / 120, -1.0 / 6):
        sine = sine * s + k
    sine = r + r * s * sine
    cosine = 1.0 / 40320
    for k in (-1.0 / 720, 1.0 / 24, -0.5, 1.0):
        cosine = cosine * s + k
    count = quarters.astype(jnp.int32)
    odd, turned = (count & 1) == 1, (count & 2) == 2
    first, second = jnp.where(odd, sine, cosine), jnp.where(odd, cosine, sine)
    flip = turned != odd
    return jnp.where(flip, -first, first), jnp.where(turned, -second, second)


def doc_start(first, second, index):
    return jnp.where(index >= second, second, jnp.where(index >= first, first, 0))


def rotated(block, cosine, sine):
    wide = block.astype(jnp.float32)
    return (wide * cosine + pltpu.roll(wide, HALF, 1) * sine).astype(jnp.bfloat16)


def lanes(i, width):
    return slice(i * width, (i + 1) * width)


def lanes_at(i, width):
    return pl.ds(i * width, width)


def stacked_heads(q_ref, g, cosine, sine):
    heads = range(g * GROUP, (g + 1) * GROUP)
    return jnp.concatenate([rotated(q_ref[:, lanes(h, HEAD_DIM)], cosine, sine) for h in heads], 0)


def score(query, key):
    return SCALE * lax.dot_general(
        query, key, (((1,), (1,)), ((), ())), preferred_element_type=jnp.float32
    )


def blend(weight, values):
    wide = jnp.concatenate([values, jnp.ones_like(values)], 1)
    return jnp.dot(weight.astype(jnp.bfloat16), wide, preferred_element_type=jnp.float32)


def kernel(
    table_any, inverse_any, lengths_any, dest_any, long_lengths_any,
    k_long_any, v_long_any, q_short_any, k_short_any, v_short_any, q_long_any,
    bin_out, long_out,
    table, dest, inverse, lengths, long_lengths,
    k_long, v_long, q_short, k_short, v_short, q_long,
    pool_refs, stage, landing, kv, query, top, acc, bias_ref, bin_result, long_result,
    load_sem, out_sem, mate_send, mate_recv, route_send, route_recv, y_send, y_recv,
):
    dp, ctx = lax.axis_index("dp"), lax.axis_index("ctx")
    core, x, z = dp % 2, (dp // 2) % NX, dp // (2 * NX)
    span = q_long.shape[0]

    loads = [
        (table_any.at[pl.ds(pl.multiple_of((dp // 2) * (NZ * NX * ROUTE), NZ * NX * ROUTE), NZ * NX * ROUTE)], table),
        (dest_any, dest),
        (inverse_any, inverse),
        (lengths_any, lengths),
        (long_lengths_any, long_lengths),
        (k_long_any, k_long),
        (v_long_any, v_long),
        (q_short_any, q_short),
        (k_short_any, k_short),
        (v_short_any, v_short),
        (q_long_any, q_long),
    ]
    loads = [pltpu.make_async_copy(a, b, load_sem.at[i]) for i, (a, b) in enumerate(loads)]
    for load in loads[2:] + loads[:2]:
        load.start()

    def at(z_to, x_to):
        return (((z_to + NZ) % NZ * NX + (x_to + NX) % NX) * 2 + core, ctx)

    mate = (dp + 1 - 2 * core, ctx)
    routes = [at(z, x + 1), at(z, x - 1), at(z + 1, x), at(z - 1, x)]
    rings = [(dp, (ctx + 1) % NY), (dp, (ctx + NY - 1) % NY)]

    barrier = pltpu.get_barrier_semaphore()
    for other in [mate, *routes, *rings]:
        pl.semaphore_signal(barrier, inc=1, device_id=other, device_id_type=MESH)

    def copy(source, target, send, recv, other):
        return pltpu.make_async_remote_copy(
            src_ref=source, dst_ref=target, send_sem=send, recv_sem=recv,
            device_id=other, device_id_type=MESH,
        )

    def ring_copy(n, way):
        hop = n // KVHEADS
        g = (n + way * (KVHEADS // 2)) % KVHEADS
        if way == 0:
            source, target = hop, hop + 1
        else:
            source = jnp.where(hop == 0, 0, hop + HOPS)
            target = jnp.where(hop == HOPS - 1, HOPS, hop + HOPS + 1)
        return copy(
            kv.at[source, g], kv.at[target, g], y_send.at[way, n], y_recv.at[way, n], rings[way]
        )

    for load in loads[2:5]:
        load.wait()
    row = lax.broadcasted_iota(jnp.int32, (span, HEAD_DIM), 0)
    lane = lax.broadcasted_iota(jnp.int32, (span, HEAD_DIM), 1)
    mine = lax.broadcasted_iota(jnp.int32, lengths.shape[2:], 1) == dp
    home = [jnp.sum(jnp.where(mine, lengths[0, d], 0), axis=1, keepdims=True) for d in range(2)]
    first = jnp.where(row < BIN_LEN, home[0][0:1], home[0][1:2])
    second = first + jnp.where(row < BIN_LEN, home[1][0:1], home[1][1:2])
    token = row % BIN_LEN
    short_start = doc_start(first, second, token)
    my_row = row + ctx * span
    first = long_lengths[:, 0:1]
    long_start = doc_start(first, first + long_lengths[:, 1:2], my_row)
    position = jnp.where(lane < HALF, token - short_start, my_row - long_start)
    cosine, sine = turns(position.astype(jnp.float32) * inverse[...])
    cosine_swap, sine_swap = pltpu.roll(cosine, HALF, 1), pltpu.roll(sine, HALF, 1)
    low = lane < HALF
    short_cos, short_sin = jnp.where(low, cosine, cosine_swap), jnp.where(low, -sine, sine_swap)
    long_cos, long_sin = jnp.where(low, cosine_swap, cosine), jnp.where(low, -sine_swap, sine)

    for load in loads[5:7]:
        load.wait()
    for g in range(KVHEADS):
        kv[0, g, :, :HEAD_DIM] = rotated(k_long[:, lanes(g, HEAD_DIM)], long_cos, long_sin)
        kv[0, g, :, HEAD_DIM:] = v_long[:, lanes(g, HEAD_DIM)]
    pl.semaphore_wait(barrier, 3 + DIRS)
    for n in range(2):
        for way in range(2):
            ring_copy(n, way).start()

    pools = [*pool_refs]
    streams = range(BINS * HALVES)

    def mate_copy(t):
        return copy(
            pools[t].at[pl.ds(0, CHUNKS)], pools[t].at[pl.ds(CHUNKS, CHUNKS)],
            mate_send.at[t], mate_recv.at[t], mate,
        )

    for load in loads[7:10]:
        load.wait()

    def bias_of(rows, reach):
        index = lane[rows] % reach
        allowed = (index >= short_start[rows]) & (index <= token[rows])
        return jnp.concatenate([jnp.where(allowed, 0.0, NEGATIVE)] * GROUP, 0)

    spot = lane[:EARLY]
    for j in range(BINS):
        rows = slice(j * BIN_LEN, (j + 1) * BIN_LEN)
        early = slice(j * BIN_LEN, j * BIN_LEN + EARLY)
        late = slice(j * BIN_LEN + EARLY, (j + 1) * BIN_LEN)
        early_bias, late_bias = bias_of(early, EARLY), bias_of(late, BIN_LEN)
        early_scores, late_scores = [], []
        for g in range(CHUNKS):
            heads = [
                rotated(q_short[rows, lanes(g * GROUP + i, HEAD_DIM)], short_cos[rows], short_sin[rows])
                for i in range(GROUP)
            ]
            key = rotated(k_short[rows, lanes(g, HEAD_DIM)], short_cos[rows], short_sin[rows])
            first = jnp.concatenate([q[:EARLY] for q in heads], 0)
            second = jnp.concatenate([q[EARLY:] for q in heads], 0)
            keys = jnp.concatenate([key[:EARLY]] * GROUP, 0)
            early_scores.append(score(first, keys) + early_bias)
            late_scores.append(score(second, jnp.concatenate([key] * 2, 0)) + late_bias)
        scores = jnp.concatenate(early_scores + late_scores, 0)
        weight = jnp.exp2(scores - jnp.max(scores, axis=1, keepdims=True))
        for g in range(CHUNKS):
            w = [weight[(g * GROUP + i) * EARLY :][:EARLY] for i in range(GROUP)]
            packed = w[0]
            for i in range(1, GROUP):
                packed = jnp.where(spot // EARLY == i, w[i], packed)
            w = [weight[((CHUNKS + g) * GROUP + i) * EARLY :][:EARLY] for i in range(GROUP)]
            left = jnp.where(spot < BIN_LEN, w[0], w[1])
            right = jnp.where(spot < BIN_LEN, w[2], w[3])
            pieces = [
                packed.astype(jnp.bfloat16), v_short[early, lanes(g, HEAD_DIM)],
                jnp.concatenate([left, right], 1).astype(jnp.bfloat16), v_short[late, lanes(g, HEAD_DIM)],
            ]
            for h in range(HALVES):
                for i, piece in enumerate(pieces):
                    part = slice(CUTS[i], CUTS[i + 1])
                    pools[j * HALVES + h][g, :, part] = piece[h * ROWS : (h + 1) * ROWS]
        for h in range(HALVES):
            mate_copy(j * HALVES + h).start()

    for load in loads[:2]:
        load.wait()
    masks = [dest[0, j, 0] for j in range(BINS)]

    def entry(t, place):
        mask = masks[t // HALVES]
        index = table[(mask >> 1) * ROUTE + place]
        return index + jnp.where(index < CHUNKS, (mask & 1) * CHUNKS, 0)

    def route_copy(slot, d):
        return copy(
            stage.at[slot, d], landing.at[slot, d], route_send.at[slot], route_recv.at[slot], routes[d]
        )

    def used(step):
        return range(0 if step < X_STEPS else 2, DIRS)

    def all_of(slot):
        dirs = used(slot // len(streams))
        part = pl.ds(dirs[0], len(dirs))
        return copy(
            stage.at[slot, part], landing.at[slot, part], route_send.at[slot], route_recv.at[slot], routes[0]
        )

    def collect(t, step):
        slot = len(streams) * step + t
        all_of(slot).wait_recv()
        for d in used(step):
            pools[t][OWN + DIRS * step + d] = landing[slot, d]

    def send(t, step, entries):
        slot = len(streams) * step + t
        for d in used(step):
            stage[slot, d] = pools[t][entries[d]]
            route_copy(slot, d).start()

    def ring(n):
        for way in range(2):
            if n > 0:
                ring_copy(n - 1, way).wait()
            if n + 2 < Y_SENDS:
                ring_copy(n + 2, way).start()

    shift = [0] + [-h for h in range(1, HOPS + 1)] + [h for h in range(1, NY - HOPS)]

    def prepare(t):
        query[t] = stacked_heads(q_long, t, long_cos, long_sin)
        for i in (2 * t, 2 * t + 1):
            key_index = lane + (ctx + NY + shift[i]) % NY * span
            allowed = (key_index >= long_start) & (key_index <= my_row)
            bias_ref[i] = jnp.where(allowed, 0.0, NEGATIVE)

    def attend(heads, blocks):
        begins, ends = 0 in blocks, HOPS in blocks
        bias = jnp.concatenate([bias_ref[i] for i in blocks], 1)
        bias = jnp.concatenate([bias] * GROUP, 0)
        keys = [jnp.concatenate([kv[i, g, :, :HEAD_DIM] for i in blocks], 0) for g in heads]
        values = [jnp.concatenate([kv[i, g, :, HEAD_DIM:] for i in blocks], 0) for g in heads]
        scores = [score(query[g], k) + bias for g, k in zip(heads, keys)]
        peaks = [jnp.max(s, axis=1, keepdims=True) for s in scores]
        if not begins:
            olds = [top[g][:, :1] for g in heads]
            peaks = [jnp.maximum(peak, old) for peak, old in zip(peaks, olds)]
        weights = [jnp.exp2(s - peak) for s, peak in zip(scores, peaks)]
        blended = [blend(w, v) for w, v in zip(weights, values)]
        for n, g in enumerate(heads):
            both = blended[n]
            if not begins:
                both = both + acc[g] * jnp.exp2(olds[n] - peaks[n])
            if ends:
                result = (both[:, :HEAD_DIM] / both[:, HEAD_DIM:]).astype(jnp.bfloat16)
                for i in range(GROUP):
                    long_result[:, lanes(g * GROUP + i, HEAD_DIM)] = result[i * span : (i + 1) * span]
                long_copy(g).start()
            else:
                top[g] = jnp.broadcast_to(peaks[n], top.shape[1:])
                acc[g] = both

    def long_copy(g):
        return pltpu.make_async_copy(
            long_result.at[:, lanes_at(g, WIDE)], long_out.at[:, lanes_at(g, WIDE)], out_sem.at[BINS * CHUNKS + g]
        )

    def bin_copy(m, g):
        return pltpu.make_async_copy(bin_result.at[m, g], bin_out.at[m, g], out_sem.at[m * CHUNKS + g])

    near = [0, 1, HOPS + 1]
    middle = [2, HOPS + 2]
    third = [3, HOPS + 3]
    far = [HOPS]

    nearer, rest = [near, middle], third + far
    plan = [[(prepare, 0)], [(prepare, 1)], [(prepare, 2)], [(prepare, 3)]]
    plan += [[(attend, [g], blocks)] for blocks in nearer for g in range(KVHEADS)]
    plan += [[], [(attend, [0], rest)], [(attend, [2], rest)], [(attend, [1], rest)]]

    def work(tasks):
        for task, *arguments in tasks:
            task(*arguments)

    loads[10].wait()
    for step in range(STEPS):
        for t in streams:
            entries = {d: entry(t, step * DIRS + d) for d in used(step)}
            if step == 0:
                mate_copy(t).wait()
            else:
                collect(t, step - 1)
            send(t, step, entries)
            phase = 2 * step + t // HALVES
            if t % HALVES == 0 and phase <= Y_SENDS:
                ring(phase)
            if t % HALVES == HALVES - 1:
                work(plan[phase])
            if step > 0:
                all_of(len(streams) * (step - 1) + t).wait_send()

    attend([3], rest)
    for t in streams:
        collect(t, STEPS - 1)

    swap = (dp ^ masks[0]) > (dp ^ masks[1])
    for g in range(CHUNKS):
        chunks = [
            jnp.concatenate(
                [pools[t][entry(t, DIRS * STEPS + g)] for t in range(j * HALVES, (j + 1) * HALVES)], 0
            )
            for j in range(BINS)
        ]
        bin_result[0, g] = jnp.where(swap, chunks[1], chunks[0])
        bin_result[1, g] = jnp.where(swap, chunks[0], chunks[1])
        for m in range(BINS):
            bin_copy(m, g).start()
    for t in streams:
        all_of(len(streams) * (STEPS - 1) + t).wait_send()

    for g in range(CHUNKS):
        long_copy(g).wait()
        for m in range(BINS):
            bin_copy(m, g).wait()


def finish(bins_any, long_any, out_short, out_long, bins, short, long, sem_in, sem_out):
    rows = long.shape[0] // PIECES

    def long_copies(p):
        part = pl.ds(p * rows, rows)
        return (
            pltpu.make_async_copy(long_any.at[part], long.at[part], sem_in.at[BINS + p]),
            pltpu.make_async_copy(long.at[part], out_long.at[part], sem_out.at[BINS + p]),
        )

    def short_copies(m):
        part = pl.ds(m * BIN_LEN, BIN_LEN)
        return (
            pltpu.make_async_copy(bins_any.at[m], bins.at[m], sem_in.at[m]),
            pltpu.make_async_copy(short.at[part], out_short.at[part], sem_out.at[m]),
        )

    pieces = [short_copies(m) for m in range(BINS)] + [long_copies(p) for p in range(PIECES)]
    for load, _ in pieces:
        load.start()

    spot = lax.broadcasted_iota(jnp.int32, (EARLY, HEAD_DIM), 1)

    def chosen(test):
        return jnp.where(test, 1.0, 0.0).astype(jnp.bfloat16)

    quarter = [chosen(spot // EARLY == i) for i in range(GROUP)]
    side = [chosen(spot < BIN_LEN), chosen(spot >= BIN_LEN)]

    def finished(weight, values):
        blended = blend(weight, values)
        result = (blended[:, :HEAD_DIM] / blended[:, HEAD_DIM:]).astype(jnp.bfloat16)
        return jnp.concatenate([result[i * EARLY : (i + 1) * EARLY] for i in range(GROUP)], 1)

    for m in range(BINS):
        pieces[m][0].wait()
        for g in range(CHUNKS):
            chunk = bins[m, g]
            first, first_v, second, second_v = [chunk[:, CUTS[i] : CUTS[i + 1]] for i in range(4)]
            early = jnp.concatenate([first * q for q in quarter], 0)
            late = [second[:, lanes(i // 2, HEAD_DIM)] * side[i % 2] for i in range(GROUP)]
            late = jnp.concatenate(late, 0)
            start = m * BIN_LEN
            short[start : start + EARLY, lanes(g, WIDE)] = finished(
                early, jnp.concatenate([first_v] * GROUP, 0)
            )
            short[start + EARLY : start + BIN_LEN, lanes(g, WIDE)] = finished(
                late, jnp.concatenate([first_v, second_v] * 2, 0)
            )
        if m == 0:
            for load, store in pieces[BINS:]:
                load.wait()
                store.start()
        pieces[m][1].start()
    for _, store in pieces:
        store.wait()


HBM = pl.BlockSpec(memory_space=pltpu.HBM)


def local(q_short, k_short, v_short, short_lengths, bin_dest, q_long, k_long, v_long, long_lengths):
    span = q_long.shape[0]
    table = jnp.asarray(route_table())
    inverse = jnp.asarray(np.concatenate([INVERSE, INVERSE])[None, :])
    lengths = jnp.transpose(short_lengths, (1, 3, 2, 0))
    dest = jnp.transpose(bin_dest, (1, 2, 0))

    bf16, f32, i32 = jnp.bfloat16, jnp.float32, jnp.int32
    slots = BINS * HALVES * STEPS
    dma = pltpu.SemaphoreType.DMA
    inputs = [k_long, v_long, q_short, k_short, v_short, q_long]
    bins_shape = (BINS, CHUNKS, EARLY, CUTS[-1])
    bins, long = pl.pallas_call(
        kernel,
        out_shape=[jax.ShapeDtypeStruct(bins_shape, bf16), jax.ShapeDtypeStruct(q_long.shape, bf16)],
        in_specs=[HBM] * 11,
        out_specs=[HBM, HBM],
        scratch_shapes=[
            pltpu.SMEM((NZ * NX * ROUTE,), i32),
            pltpu.SMEM(dest.shape, i32),
            pltpu.VMEM(inverse.shape, f32),
            pltpu.VMEM(lengths.shape, i32),
            pltpu.VMEM(long_lengths.shape, i32),
            *[pltpu.VMEM(a.shape, bf16) for a in inputs],
            [pltpu.VMEM((POOL, ROWS, CUTS[-1]), bf16)] * (BINS * HALVES),
            pltpu.VMEM((slots, DIRS, ROWS, CUTS[-1]), bf16),
            pltpu.VMEM((slots, DIRS, ROWS, CUTS[-1]), bf16),
            pltpu.VMEM((NY, KVHEADS, span, 2 * HEAD_DIM), bf16),
            pltpu.VMEM((KVHEADS, GROUP * span, HEAD_DIM), bf16),
            pltpu.VMEM((KVHEADS, GROUP * span, HEAD_DIM), f32),
            pltpu.VMEM((KVHEADS, GROUP * span, 2 * HEAD_DIM), f32),
            pltpu.VMEM((NY, span, span), f32),
            pltpu.VMEM(bins_shape, bf16),
            pltpu.VMEM(q_long.shape, bf16),
            dma((11,)),
            dma((BINS * CHUNKS + KVHEADS,)),
            dma((BINS * HALVES,)),
            dma((BINS * HALVES,)),
            dma((slots,)),
            dma((slots,)),
            dma((2, Y_SENDS)),
            dma((2, Y_SENDS)),
        ],
        compiler_params=pltpu.CompilerParams(
            collective_id=0, has_side_effects=True, vmem_limit_bytes=56 * 2**20
        ),
    )(table, inverse, lengths, dest, long_lengths, *inputs)
    return pl.pallas_call(
        finish,
        out_shape=[jax.ShapeDtypeStruct(q_short.shape, bf16), jax.ShapeDtypeStruct(q_long.shape, bf16)],
        in_specs=[HBM, HBM],
        out_specs=[HBM, HBM],
        scratch_shapes=[
            pltpu.VMEM(bins_shape, bf16),
            pltpu.VMEM(q_short.shape, bf16),
            pltpu.VMEM(q_long.shape, bf16),
            dma((BINS + PIECES,)),
            dma((BINS + PIECES,)),
        ],
        compiler_params=pltpu.CompilerParams(vmem_limit_bytes=56 * 2**20),
    )(bins, long)


def solution(mesh):
    in_specs = (
        P(("dp", "ctx"), None),
        P(("dp", "ctx"), None),
        P(("dp", "ctx"), None),
        P(None, "ctx", None, None),
        P(None, "ctx", None),
        P(("dp", "ctx"), None),
        P(("dp", "ctx"), None),
        P(("dp", "ctx"), None),
        P("dp", None),
    )
    out_specs = (P(("dp", "ctx"), None), P(("dp", "ctx"), None))
    return jax.shard_map(local, mesh=mesh, in_specs=in_specs, out_specs=out_specs, check_vma=False)
```

```python
import functools
import math

import jax
import jax.numpy as jnp
import numpy as np
from jax import lax
from jax.experimental import pallas as pl
from jax.experimental.pallas import tpu as pltpu
from jax.sharding import PartitionSpec as P

QHEADS = 16
KVHEADS = 4
GROUP = QHEADS // KVHEADS
HEAD_DIM = 128
HALF = HEAD_DIM // 2
WIDE = GROUP * HEAD_DIM
BIN_LEN = 64
BINS = 2
THETA = 500000.0
NEGATIVE = -1e30
SCALE = math.log2(math.e) / math.sqrt(HEAD_DIM)

NZ, NX, NY = 8, 4, 8
HALVES = 2
EARLY = BIN_LEN // 2
ROWS = EARLY // HALVES
CUTS = (0, HEAD_DIM, 2 * HEAD_DIM, 4 * HEAD_DIM, 5 * HEAD_DIM)
CHUNKS = KVHEADS
STEPS = 8
X_STEPS = 6
DIRS = 4
OWN = 2 * CHUNKS
POOL = OWN + DIRS * STEPS
PIECES = 4
ROUTE = 64
HOPS = NY // 2
Y_SENDS = 3 * KVHEADS + KVHEADS // 2
MESH = pl.DeviceIdType.MESH


def moved(place, direction):
    z, x = divmod(place, NX)
    if direction < 2:
        x = (x + (1, -1)[direction]) % NX
    else:
        z = (z + (1, -1)[direction - 2]) % NZ
    return z * NX + x


def routed(mask, x_first, spread, key):
    packets = []
    for place in range(NZ * NX):
        z, x = divmod(place, NX)
        goal_z, goal_x = divmod(place ^ mask, NX)
        for chunk in range(CHUNKS):
            dz, dx = (goal_z - z) % NZ, (goal_x - x) % NX
            if dz > NZ // 2 or (dz == NZ // 2 and chunk % 2):
                dz -= NZ
            if dx > NX // 2 or (dx == NX // 2 and (chunk // spread) % 2):
                dx -= NX
            packets.append([place, dz, dx, chunk, chunk])
    sends = []
    for step in range(STEPS):
        taken, moves = set(), []
        for p in sorted(packets, key=key):
            along_z = [2 if p[1] > 0 else 3] if p[1] else []
            along_x = [0 if p[2] > 0 else 1] if p[2] and step < X_STEPS else []
            for d in along_x + along_z if x_first else along_z + along_x:
                if (p[0], d) not in taken:
                    taken.add((p[0], d))
                    moves.append((p, d))
                    break
        for p, d in moves:
            sends.append((p[0], step * DIRS + d, p[3]))
            p[0] = moved(p[0], d)
            p[2 if d < 2 else 1] -= (1, -1)[d % 2]
            p[3] = OWN + DIRS * step + d
    if any(p[1] or p[2] for p in packets):
        return None
    return sends + [(p[0], DIRS * STEPS + p[4], p[3]) for p in packets]


@functools.cache
def route_table():
    keys = [
        lambda p: (-abs(p[1]) - abs(p[2]), -abs(p[1]), p[4]),
        lambda p: (-abs(p[2]), -abs(p[1]), p[4]),
        lambda p: (-abs(p[1]) - abs(p[2]), -abs(p[2]), p[4]),
        lambda p: (-abs(p[1]), -abs(p[2]), p[4]),
    ]
    table = np.zeros((NZ * NX, NZ * NX, ROUTE), np.int32)
    for mask in range(NZ * NX):
        tries = ((x_first, spread, key) for x_first in (0, 1) for spread in (1, 2) for key in keys)
        found = next(r for r in (routed(mask, *t) for t in tries) if r is not None)
        for place, slot, entry in found:
            table[place, mask, slot] = entry
    return table.reshape(-1)


INVERSE = np.power(THETA, -np.arange(HALF, dtype=np.float64) * (2.0 / HEAD_DIM)).astype(np.float32)
QUARTER1 = float(np.float32(1.5703125))
QUARTER2 = float(np.float32(math.floor((math.pi / 2 - QUARTER1) * 2**23) / 2**23))
QUARTER3 = float(np.float32(math.pi / 2 - QUARTER1 - QUARTER2))


def turns(angle):
    quarters = jnp.floor(angle * (2.0 / math.pi) + 0.5)
    r = ((angle - quarters * QUARTER1) - quarters * QUARTER2) - quarters * QUARTER3
    s = r * r
    sine = 1.0 / 362880
    for k in (-1.0 / 5040, 1.0 / 120, -1.0 / 6):
        sine = sine * s + k
    sine = r + r * s * sine
    cosine = 1.0 / 40320
    for k in (-1.0 / 720, 1.0 / 24, -0.5, 1.0):
        cosine = cosine * s + k
    count = quarters.astype(jnp.int32)
    odd, turned = (count & 1) == 1, (count & 2) == 2
    first, second = jnp.where(odd, sine, cosine), jnp.where(odd, cosine, sine)
    flip = turned != odd
    return jnp.where(flip, -first, first), jnp.where(turned, -second, second)


def doc_start(first, second, index):
    return jnp.where(index >= second, second, jnp.where(index >= first, first, 0))


def rotated(block, cosine, sine):
    wide = block.astype(jnp.float32)
    return (wide * cosine + pltpu.roll(wide, HALF, 1) * sine).astype(jnp.bfloat16)


def lanes(i, width):
    return slice(i * width, (i + 1) * width)


def lanes_at(i, width):
    return pl.ds(i * width, width)


def stacked_heads(q_ref, g, cosine, sine):
    heads = range(g * GROUP, (g + 1) * GROUP)
    return jnp.concatenate([rotated(q_ref[:, lanes(h, HEAD_DIM)], cosine, sine) for h in heads], 0)


def score(query, key):
    return SCALE * lax.dot_general(
        query, key, (((1,), (1,)), ((), ())), preferred_element_type=jnp.float32
    )


def blend(weight, values):
    wide = jnp.concatenate([values, jnp.ones_like(values)], 1)
    return jnp.dot(weight.astype(jnp.bfloat16), wide, preferred_element_type=jnp.float32)


def kernel(
    table_any, inverse_any, lengths_any, dest_any, long_lengths_any,
    k_long_any, v_long_any, q_short_any, k_short_any, v_short_any, q_long_any,
    bin_out, long_out,
    table, dest, inverse, lengths, long_lengths,
    k_long, v_long, q_short, k_short, v_short, q_long,
    pool_refs, stage, landing, kv, query, top, acc, bias_ref, bin_result, long_result,
    load_sem, out_sem, mate_send, mate_recv, route_send, route_recv, y_send, y_recv,
):
    dp, ctx = lax.axis_index("dp"), lax.axis_index("ctx")
    core, x, z = dp % 2, (dp // 2) % NX, dp // (2 * NX)
    span = q_long.shape[0]

    loads = [
        (table_any.at[pl.ds(pl.multiple_of((dp // 2) * (NZ * NX * ROUTE), NZ * NX * ROUTE), NZ * NX * ROUTE)], table),
        (dest_any, dest),
        (inverse_any, inverse),
        (lengths_any, lengths),
        (long_lengths_any, long_lengths),
        (k_long_any, k_long),
        (v_long_any, v_long),
        (q_short_any, q_short),
        (k_short_any, k_short),
        (v_short_any, v_short),
        (q_long_any, q_long),
    ]
    loads = [pltpu.make_async_copy(a, b, load_sem.at[i]) for i, (a, b) in enumerate(loads)]
    for load in loads[2:] + loads[:2]:
        load.start()

    def at(z_to, x_to):
        return (((z_to + NZ) % NZ * NX + (x_to + NX) % NX) * 2 + core, ctx)

    mate = (dp + 1 - 2 * core, ctx)
    routes = [at(z, x + 1), at(z, x - 1), at(z + 1, x), at(z - 1, x)]
    rings = [(dp, (ctx + 1) % NY), (dp, (ctx + NY - 1) % NY)]

    barrier = pltpu.get_barrier_semaphore()
    for other in [mate, *routes, *rings]:
        pl.semaphore_signal(barrier, inc=1, device_id=other, device_id_type=MESH)

    def copy(source, target, send, recv, other):
        return pltpu.make_async_remote_copy(
            src_ref=source, dst_ref=target, send_sem=send, recv_sem=recv,
            device_id=other, device_id_type=MESH,
        )

    def ring_copy(n, way):
        hop = n // KVHEADS
        g = (n + way * (KVHEADS // 2)) % KVHEADS
        if way == 0:
            source, target = hop, hop + 1
        else:
            source = jnp.where(hop == 0, 0, hop + HOPS)
            target = jnp.where(hop == HOPS - 1, HOPS, hop + HOPS + 1)
        return copy(
            kv.at[source, g], kv.at[target, g], y_send.at[way, n], y_recv.at[way, n], rings[way]
        )

    for load in loads[2:5]:
        load.wait()
    row = lax.broadcasted_iota(jnp.int32, (span, HEAD_DIM), 0)
    lane = lax.broadcasted_iota(jnp.int32, (span, HEAD_DIM), 1)
    mine = lax.broadcasted_iota(jnp.int32, lengths.shape[2:], 1) == dp
    home = [jnp.sum(jnp.where(mine, lengths[0, d], 0), axis=1, keepdims=True) for d in range(2)]
    first = jnp.where(row < BIN_LEN, home[0][0:1], home[0][1:2])
    second = first + jnp.where(row < BIN_LEN, home[1][0:1], home[1][1:2])
    token = row % BIN_LEN
    short_start = doc_start(first, second, token)
    my_row = row + ctx * span
    first = long_lengths[:, 0:1]
    long_start = doc_start(first, first + long_lengths[:, 1:2], my_row)
    position = jnp.where(lane < HALF, token - short_start, my_row - long_start)
    cosine, sine = turns(position.astype(jnp.float32) * inverse[...])
    cosine_swap, sine_swap = pltpu.roll(cosine, HALF, 1), pltpu.roll(sine, HALF, 1)
    low = lane < HALF
    short_cos, short_sin = jnp.where(low, cosine, cosine_swap), jnp.where(low, -sine, sine_swap)
    long_cos, long_sin = jnp.where(low, cosine_swap, cosine), jnp.where(low, -sine_swap, sine)

    for load in loads[5:7]:
        load.wait()
    for g in range(KVHEADS):
        kv[0, g, :, :HEAD_DIM] = rotated(k_long[:, lanes(g, HEAD_DIM)], long_cos, long_sin)
        kv[0, g, :, HEAD_DIM:] = v_long[:, lanes(g, HEAD_DIM)]
    pl.semaphore_wait(barrier, 3 + DIRS)
    for n in range(2):
        for way in range(2):
            ring_copy(n, way).start()

    pools = [*pool_refs]
    streams = range(BINS * HALVES)

    def mate_copy(t):
        return copy(
            pools[t].at[pl.ds(0, CHUNKS)], pools[t].at[pl.ds(CHUNKS, CHUNKS)],
            mate_send.at[t], mate_recv.at[t], mate,
        )

    for load in loads[7:10]:
        load.wait()

    def bias_of(rows, reach):
        index = lane[rows] % reach
        allowed = (index >= short_start[rows]) & (index <= token[rows])
        return jnp.concatenate([jnp.where(allowed, 0.0, NEGATIVE)] * GROUP, 0)

    spot = lane[:EARLY]
    for j in range(BINS):
        rows = slice(j * BIN_LEN, (j + 1) * BIN_LEN)
        early = slice(j * BIN_LEN, j * BIN_LEN + EARLY)
        late = slice(j * BIN_LEN + EARLY, (j + 1) * BIN_LEN)
        early_bias, late_bias = bias_of(early, EARLY), bias_of(late, BIN_LEN)
        early_scores, late_scores = [], []
        for g in range(CHUNKS):
            heads = [
                rotated(q_short[rows, lanes(g * GROUP + i, HEAD_DIM)], short_cos[rows], short_sin[rows])
                for i in range(GROUP)
            ]
            key = rotated(k_short[rows, lanes(g, HEAD_DIM)], short_cos[rows], short_sin[rows])
            first = jnp.concatenate([q[:EARLY] for q in heads], 0)
            second = jnp.concatenate([q[EARLY:] for q in heads], 0)
            keys = jnp.concatenate([key[:EARLY]] * GROUP, 0)
            early_scores.append(score(first, keys) + early_bias)
            late_scores.append(score(second, jnp.concatenate([key] * 2, 0)) + late_bias)
        scores = jnp.concatenate(early_scores + late_scores, 0)
        weight = jnp.exp2(scores - jnp.max(scores, axis=1, keepdims=True))
        for g in range(CHUNKS):
            w = [weight[(g * GROUP + i) * EARLY :][:EARLY] for i in range(GROUP)]
            packed = w[0]
            for i in range(1, GROUP):
                packed = jnp.where(spot // EARLY == i, w[i], packed)
            w = [weight[((CHUNKS + g) * GROUP + i) * EARLY :][:EARLY] for i in range(GROUP)]
            left = jnp.where(spot < BIN_LEN, w[0], w[1])
            right = jnp.where(spot < BIN_LEN, w[2], w[3])
            pieces = [
                packed.astype(jnp.bfloat16), v_short[early, lanes(g, HEAD_DIM)],
                jnp.concatenate([left, right], 1).astype(jnp.bfloat16), v_short[late, lanes(g, HEAD_DIM)],
            ]
            for h in range(HALVES):
                for i, piece in enumerate(pieces):
                    part = slice(CUTS[i], CUTS[i + 1])
                    pools[j * HALVES + h][g, :, part] = piece[h * ROWS : (h + 1) * ROWS]
        for h in range(HALVES):
            mate_copy(j * HALVES + h).start()

    for load in loads[:2]:
        load.wait()
    masks = [dest[0, j, 0] for j in range(BINS)]

    def entry(t, place):
        mask = masks[t // HALVES]
        index = table[(mask >> 1) * ROUTE + place]
        return index + jnp.where(index < CHUNKS, (mask & 1) * CHUNKS, 0)

    def route_copy(slot, d):
        return copy(
            stage.at[slot, d], landing.at[slot, d], route_send.at[slot], route_recv.at[slot], routes[d]
        )

    def used(step):
        return range(0 if step < X_STEPS else 2, DIRS)

    def all_of(slot):
        dirs = used(slot // len(streams))
        part = pl.ds(dirs[0], len(dirs))
        return copy(
            stage.at[slot, part], landing.at[slot, part], route_send.at[slot], route_recv.at[slot], routes[0]
        )

    def collect(t, step):
        slot = len(streams) * step + t
        all_of(slot).wait_recv()
        for d in used(step):
            pools[t][OWN + DIRS * step + d] = landing[slot, d]

    def send(t, step, entries):
        slot = len(streams) * step + t
        for d in used(step):
            stage[slot, d] = pools[t][entries[d]]
            route_copy(slot, d).start()

    def ring(n):
        for way in range(2):
            if n > 0:
                ring_copy(n - 1, way).wait()
            if n + 2 < Y_SENDS:
                ring_copy(n + 2, way).start()

    shift = [0] + [-h for h in range(1, HOPS + 1)] + [h for h in range(1, NY - HOPS)]

    def prepare(t):
        query[t] = stacked_heads(q_long, t, long_cos, long_sin)
        for i in (2 * t, 2 * t + 1):
            key_index = lane + (ctx + NY + shift[i]) % NY * span
            allowed = (key_index >= long_start) & (key_index <= my_row)
            bias_ref[i] = jnp.where(allowed, 0.0, NEGATIVE)

    def attend(heads, blocks):
        begins, ends = 0 in blocks, HOPS in blocks
        bias = jnp.concatenate([bias_ref[i] for i in blocks], 1)
        bias = jnp.concatenate([bias] * GROUP, 0)
        keys = [jnp.concatenate([kv[i, g, :, :HEAD_DIM] for i in blocks], 0) for g in heads]
        values = [jnp.concatenate([kv[i, g, :, HEAD_DIM:] for i in blocks], 0) for g in heads]
        scores = [score(query[g], k) + bias for g, k in zip(heads, keys)]
        peaks = [jnp.max(s, axis=1, keepdims=True) for s in scores]
        if not begins:
            olds = [top[g][:, :1] for g in heads]
            peaks = [jnp.maximum(peak, old) for peak, old in zip(peaks, olds)]
        weights = [jnp.exp2(s - peak) for s, peak in zip(scores, peaks)]
        blended = [blend(w, v) for w, v in zip(weights, values)]
        for n, g in enumerate(heads):
            both = blended[n]
            if not begins:
                both = both + acc[g] * jnp.exp2(olds[n] - peaks[n])
            if ends:
                result = (both[:, :HEAD_DIM] / both[:, HEAD_DIM:]).astype(jnp.bfloat16)
                for i in range(GROUP):
                    long_result[:, lanes(g * GROUP + i, HEAD_DIM)] = result[i * span : (i + 1) * span]
                long_copy(g).start()
            else:
                top[g] = jnp.broadcast_to(peaks[n], top.shape[1:])
                acc[g] = both

    def long_copy(g):
        return pltpu.make_async_copy(
            long_result.at[:, lanes_at(g, WIDE)], long_out.at[:, lanes_at(g, WIDE)], out_sem.at[BINS * CHUNKS + g]
        )

    def bin_copy(m, g):
        return pltpu.make_async_copy(bin_result.at[m, g], bin_out.at[m, g], out_sem.at[m * CHUNKS + g])

    near = [0, 1, HOPS + 1]
    middle = [2, HOPS + 2]
    third = [3, HOPS + 3]
    far = [HOPS]

    nearer, rest = near + middle, third + far
    plan = [[(prepare, g) for g in range(KVHEADS)]] + [[] for _ in range(7)]
    plan += [[(attend, [g], nearer)] for g in range(KVHEADS)]
    plan += [[], [(attend, [0], rest)], [(attend, [2], rest)], [(attend, [1], rest)]]

    def work(tasks):
        for task, *arguments in tasks:
            task(*arguments)

    loads[10].wait()
    for step in range(STEPS):
        for t in streams:
            entries = {d: entry(t, step * DIRS + d) for d in used(step)}
            if step == 0:
                mate_copy(t).wait()
            else:
                collect(t, step - 1)
            send(t, step, entries)
            phase = 2 * step + t // HALVES
            if t % HALVES == 0 and phase <= Y_SENDS:
                ring(phase)
            if t % HALVES == HALVES - 1:
                work(plan[phase])
            if step > 0:
                all_of(len(streams) * (step - 1) + t).wait_send()

    attend([3], rest)
    for t in streams:
        collect(t, STEPS - 1)

    swap = (dp ^ masks[0]) > (dp ^ masks[1])
    for g in range(CHUNKS):
        chunks = [
            jnp.concatenate(
                [pools[t][entry(t, DIRS * STEPS + g)] for t in range(j * HALVES, (j + 1) * HALVES)], 0
            )
            for j in range(BINS)
        ]
        bin_result[0, g] = jnp.where(swap, chunks[1], chunks[0])
        bin_result[1, g] = jnp.where(swap, chunks[0], chunks[1])
        for m in range(BINS):
            bin_copy(m, g).start()
    for t in streams:
        all_of(len(streams) * (STEPS - 1) + t).wait_send()

    for g in range(CHUNKS):
        long_copy(g).wait()
        for m in range(BINS):
            bin_copy(m, g).wait()


def finish(bins_any, long_any, out_short, out_long, bins, short, long, sem_in, sem_out):
    rows = long.shape[0] // PIECES

    def long_copies(p):
        part = pl.ds(p * rows, rows)
        return (
            pltpu.make_async_copy(long_any.at[part], long.at[part], sem_in.at[BINS + p]),
            pltpu.make_async_copy(long.at[part], out_long.at[part], sem_out.at[BINS + p]),
        )

    def short_copies(m):
        part = pl.ds(m * BIN_LEN, BIN_LEN)
        return (
            pltpu.make_async_copy(bins_any.at[m], bins.at[m], sem_in.at[m]),
            pltpu.make_async_copy(short.at[part], out_short.at[part], sem_out.at[m]),
        )

    pieces = [short_copies(m) for m in range(BINS)] + [long_copies(p) for p in range(PIECES)]
    for load, _ in pieces:
        load.start()

    spot = lax.broadcasted_iota(jnp.int32, (EARLY, HEAD_DIM), 1)

    def chosen(test):
        return jnp.where(test, 1.0, 0.0).astype(jnp.bfloat16)

    quarter = [chosen(spot // EARLY == i) for i in range(GROUP)]
    side = [chosen(spot < BIN_LEN), chosen(spot >= BIN_LEN)]

    def finished(weight, values):
        blended = blend(weight, values)
        result = (blended[:, :HEAD_DIM] / blended[:, HEAD_DIM:]).astype(jnp.bfloat16)
        return jnp.concatenate([result[i * EARLY : (i + 1) * EARLY] for i in range(GROUP)], 1)

    for m in range(BINS):
        pieces[m][0].wait()
        for g in range(CHUNKS):
            chunk = bins[m, g]
            first, first_v, second, second_v = [chunk[:, CUTS[i] : CUTS[i + 1]] for i in range(4)]
            early = jnp.concatenate([first * q for q in quarter], 0)
            late = [second[:, lanes(i // 2, HEAD_DIM)] * side[i % 2] for i in range(GROUP)]
            late = jnp.concatenate(late, 0)
            start = m * BIN_LEN
            short[start : start + EARLY, lanes(g, WIDE)] = finished(
                early, jnp.concatenate([first_v] * GROUP, 0)
            )
            short[start + EARLY : start + BIN_LEN, lanes(g, WIDE)] = finished(
                late, jnp.concatenate([first_v, second_v] * 2, 0)
            )
        if m == 0:
            for load, store in pieces[BINS:]:
                load.wait()
                store.start()
        pieces[m][1].start()
    for _, store in pieces:
        store.wait()


HBM = pl.BlockSpec(memory_space=pltpu.HBM)


def local(q_short, k_short, v_short, short_lengths, bin_dest, q_long, k_long, v_long, long_lengths):
    span = q_long.shape[0]
    table = jnp.asarray(route_table())
    inverse = jnp.asarray(np.concatenate([INVERSE, INVERSE])[None, :])
    lengths = jnp.transpose(short_lengths, (1, 3, 2, 0))
    dest = jnp.transpose(bin_dest, (1, 2, 0))

    bf16, f32, i32 = jnp.bfloat16, jnp.float32, jnp.int32
    slots = BINS * HALVES * STEPS
    dma = pltpu.SemaphoreType.DMA
    inputs = [k_long, v_long, q_short, k_short, v_short, q_long]
    bins_shape = (BINS, CHUNKS, EARLY, CUTS[-1])
    bins, long = pl.pallas_call(
        kernel,
        out_shape=[jax.ShapeDtypeStruct(bins_shape, bf16), jax.ShapeDtypeStruct(q_long.shape, bf16)],
        in_specs=[HBM] * 11,
        out_specs=[HBM, HBM],
        scratch_shapes=[
            pltpu.SMEM((NZ * NX * ROUTE,), i32),
            pltpu.SMEM(dest.shape, i32),
            pltpu.VMEM(inverse.shape, f32),
            pltpu.VMEM(lengths.shape, i32),
            pltpu.VMEM(long_lengths.shape, i32),
            *[pltpu.VMEM(a.shape, bf16) for a in inputs],
            [pltpu.VMEM((POOL, ROWS, CUTS[-1]), bf16)] * (BINS * HALVES),
            pltpu.VMEM((slots, DIRS, ROWS, CUTS[-1]), bf16),
            pltpu.VMEM((slots, DIRS, ROWS, CUTS[-1]), bf16),
            pltpu.VMEM((NY, KVHEADS, span, 2 * HEAD_DIM), bf16),
            pltpu.VMEM((KVHEADS, GROUP * span, HEAD_DIM), bf16),
            pltpu.VMEM((KVHEADS, GROUP * span, HEAD_DIM), f32),
            pltpu.VMEM((KVHEADS, GROUP * span, 2 * HEAD_DIM), f32),
            pltpu.VMEM((NY, span, span), f32),
            pltpu.VMEM(bins_shape, bf16),
            pltpu.VMEM(q_long.shape, bf16),
            dma((11,)),
            dma((BINS * CHUNKS + KVHEADS,)),
            dma((BINS * HALVES,)),
            dma((BINS * HALVES,)),
            dma((slots,)),
            dma((slots,)),
            dma((2, Y_SENDS)),
            dma((2, Y_SENDS)),
        ],
        compiler_params=pltpu.CompilerParams(
            collective_id=0, has_side_effects=True, vmem_limit_bytes=56 * 2**20
        ),
    )(table, inverse, lengths, dest, long_lengths, *inputs)
    return pl.pallas_call(
        finish,
        out_shape=[jax.ShapeDtypeStruct(q_short.shape, bf16), jax.ShapeDtypeStruct(q_long.shape, bf16)],
        in_specs=[HBM, HBM],
        out_specs=[HBM, HBM],
        scratch_shapes=[
            pltpu.VMEM(bins_shape, bf16),
            pltpu.VMEM(q_short.shape, bf16),
            pltpu.VMEM(q_long.shape, bf16),
            dma((BINS + PIECES,)),
            dma((BINS + PIECES,)),
        ],
        compiler_params=pltpu.CompilerParams(vmem_limit_bytes=56 * 2**20),
    )(bins, long)


def solution(mesh):
    in_specs = (
        P(("dp", "ctx"), None),
        P(("dp", "ctx"), None),
        P(("dp", "ctx"), None),
        P(None, "ctx", None, None),
        P(None, "ctx", None),
        P(("dp", "ctx"), None),
        P(("dp", "ctx"), None),
        P(("dp", "ctx"), None),
        P("dp", None),
    )
    out_specs = (P(("dp", "ctx"), None), P(("dp", "ctx"), None))
    return jax.shard_map(local, mesh=mesh, in_specs=in_specs, out_specs=out_specs, check_vma=False)
```

```python
import functools
import math

import jax
import jax.numpy as jnp
import numpy as np
from jax import lax
from jax.experimental import pallas as pl
from jax.experimental.pallas import tpu as pltpu
from jax.sharding import PartitionSpec as P

QHEADS = 16
KVHEADS = 4
GROUP = QHEADS // KVHEADS
HEAD_DIM = 128
HALF = HEAD_DIM // 2
WIDE = GROUP * HEAD_DIM
BIN_LEN = 64
BINS = 2
THETA = 500000.0
NEGATIVE = -1e30
SCALE = math.log2(math.e) / math.sqrt(HEAD_DIM)

NZ, NX, NY = 8, 4, 8
HALVES = 2
EARLY = BIN_LEN // 2
ROWS = EARLY // HALVES
CUTS = (0, HEAD_DIM, 2 * HEAD_DIM, 4 * HEAD_DIM, 5 * HEAD_DIM)
CHUNKS = KVHEADS
STEPS = 8
X_STEPS = 6
DIRS = 4
OWN = 2 * CHUNKS
POOL = OWN + DIRS * STEPS
PIECES = 4
ROUTE = 64
HOPS = NY // 2
Y_SENDS = 3 * KVHEADS + KVHEADS // 2
MESH = pl.DeviceIdType.MESH


def moved(place, direction):
    z, x = divmod(place, NX)
    if direction < 2:
        x = (x + (1, -1)[direction]) % NX
    else:
        z = (z + (1, -1)[direction - 2]) % NZ
    return z * NX + x


def routed(mask, x_first, spread, key):
    packets = []
    for place in range(NZ * NX):
        z, x = divmod(place, NX)
        goal_z, goal_x = divmod(place ^ mask, NX)
        for chunk in range(CHUNKS):
            dz, dx = (goal_z - z) % NZ, (goal_x - x) % NX
            if dz > NZ // 2 or (dz == NZ // 2 and chunk % 2):
                dz -= NZ
            if dx > NX // 2 or (dx == NX // 2 and (chunk // spread) % 2):
                dx -= NX
            packets.append([place, dz, dx, chunk, chunk])
    sends = []
    for step in range(STEPS):
        taken, moves = set(), []
        for p in sorted(packets, key=key):
            along_z = [2 if p[1] > 0 else 3] if p[1] else []
            along_x = [0 if p[2] > 0 else 1] if p[2] and step < X_STEPS else []
            for d in along_x + along_z if x_first else along_z + along_x:
                if (p[0], d) not in taken:
                    taken.add((p[0], d))
                    moves.append((p, d))
                    break
        for p, d in moves:
            sends.append((p[0], step * DIRS + d, p[3]))
            p[0] = moved(p[0], d)
            p[2 if d < 2 else 1] -= (1, -1)[d % 2]
            p[3] = OWN + DIRS * step + d
    if any(p[1] or p[2] for p in packets):
        return None
    return sends + [(p[0], DIRS * STEPS + p[4], p[3]) for p in packets]


@functools.cache
def route_table():
    keys = [
        lambda p: (-abs(p[1]) - abs(p[2]), -abs(p[1]), p[4]),
        lambda p: (-abs(p[2]), -abs(p[1]), p[4]),
        lambda p: (-abs(p[1]) - abs(p[2]), -abs(p[2]), p[4]),
        lambda p: (-abs(p[1]), -abs(p[2]), p[4]),
    ]
    table = np.zeros((NZ * NX, NZ * NX, ROUTE), np.int32)
    for mask in range(NZ * NX):
        tries = ((x_first, spread, key) for x_first in (0, 1) for spread in (1, 2) for key in keys)
        found = next(r for r in (routed(mask, *t) for t in tries) if r is not None)
        for place, slot, entry in found:
            table[place, mask, slot] = entry
    return table.reshape(-1)


INVERSE = np.power(THETA, -np.arange(HALF, dtype=np.float64) * (2.0 / HEAD_DIM)).astype(np.float32)
QUARTER1 = float(np.float32(1.5703125))
QUARTER2 = float(np.float32(math.floor((math.pi / 2 - QUARTER1) * 2**23) / 2**23))
QUARTER3 = float(np.float32(math.pi / 2 - QUARTER1 - QUARTER2))


def turns(angle):
    quarters = jnp.floor(angle * (2.0 / math.pi) + 0.5)
    r = ((angle - quarters * QUARTER1) - quarters * QUARTER2) - quarters * QUARTER3
    s = r * r
    sine = 1.0 / 362880
    for k in (-1.0 / 5040, 1.0 / 120, -1.0 / 6):
        sine = sine * s + k
    sine = r + r * s * sine
    cosine = 1.0 / 40320
    for k in (-1.0 / 720, 1.0 / 24, -0.5, 1.0):
        cosine = cosine * s + k
    count = quarters.astype(jnp.int32)
    odd, turned = (count & 1) == 1, (count & 2) == 2
    first, second = jnp.where(odd, sine, cosine), jnp.where(odd, cosine, sine)
    flip = turned != odd
    return jnp.where(flip, -first, first), jnp.where(turned, -second, second)


def doc_start(first, second, index):
    return jnp.where(index >= second, second, jnp.where(index >= first, first, 0))


def rotated(block, cosine, sine):
    wide = block.astype(jnp.float32)
    return (wide * cosine + pltpu.roll(wide, HALF, 1) * sine).astype(jnp.bfloat16)


def lanes(i, width):
    return slice(i * width, (i + 1) * width)


def lanes_at(i, width):
    return pl.ds(i * width, width)


def stacked_heads(q_ref, g, cosine, sine):
    heads = range(g * GROUP, (g + 1) * GROUP)
    return jnp.concatenate([rotated(q_ref[:, lanes(h, HEAD_DIM)], cosine, sine) for h in heads], 0)


def score(query, key):
    return SCALE * lax.dot_general(
        query, key, (((1,), (1,)), ((), ())), preferred_element_type=jnp.float32
    )


def blend(weight, values):
    wide = jnp.concatenate([values, jnp.ones_like(values)], 1)
    return jnp.dot(weight.astype(jnp.bfloat16), wide, preferred_element_type=jnp.float32)


def kernel(
    table_any, inverse_any, lengths_any, dest_any, long_lengths_any,
    k_long_any, v_long_any, q_short_any, k_short_any, v_short_any, q_long_any,
    bin_out, long_out,
    table, dest, inverse, lengths, long_lengths,
    k_long, v_long, q_short, k_short, v_short, q_long,
    pool_refs, stage, landing, kv, query, top, acc, bias_ref, bin_result, long_result,
    load_sem, out_sem, mate_send, mate_recv, route_send, route_recv, y_send, y_recv,
):
    dp, ctx = lax.axis_index("dp"), lax.axis_index("ctx")
    core, x, z = dp % 2, (dp // 2) % NX, dp // (2 * NX)
    span = q_long.shape[0]

    loads = [
        (table_any.at[pl.ds(pl.multiple_of((dp // 2) * (NZ * NX * ROUTE), NZ * NX * ROUTE), NZ * NX * ROUTE)], table),
        (dest_any, dest),
        (inverse_any, inverse),
        (lengths_any, lengths),
        (long_lengths_any, long_lengths),
        (k_long_any, k_long),
        (v_long_any, v_long),
        (q_short_any, q_short),
        (k_short_any, k_short),
        (v_short_any, v_short),
        (q_long_any, q_long),
    ]
    loads = [pltpu.make_async_copy(a, b, load_sem.at[i]) for i, (a, b) in enumerate(loads)]
    for load in loads[2:] + loads[:2]:
        load.start()

    def at(z_to, x_to):
        return (((z_to + NZ) % NZ * NX + (x_to + NX) % NX) * 2 + core, ctx)

    mate = (dp + 1 - 2 * core, ctx)
    routes = [at(z, x + 1), at(z, x - 1), at(z + 1, x), at(z - 1, x)]
    rings = [(dp, (ctx + 1) % NY), (dp, (ctx + NY - 1) % NY)]

    @pl.loop(1, NY)
    def _(i):
        kv[i] = jnp.zeros(kv.shape[1:], kv.dtype)

    barrier = pltpu.get_barrier_semaphore()
    for other in [mate, *routes, *rings]:
        pl.semaphore_signal(barrier, inc=1, device_id=other, device_id_type=MESH)

    def copy(source, target, send, recv, other):
        return pltpu.make_async_remote_copy(
            src_ref=source, dst_ref=target, send_sem=send, recv_sem=recv,
            device_id=other, device_id_type=MESH,
        )

    def ring_copy(n, way):
        hop = n // KVHEADS
        g = (n + way * (KVHEADS // 2)) % KVHEADS
        if way == 0:
            source, target = hop, hop + 1
        else:
            source = jnp.where(hop == 0, 0, hop + HOPS)
            target = jnp.where(hop == HOPS - 1, HOPS, hop + HOPS + 1)
        return copy(
            kv.at[source, g], kv.at[target, g], y_send.at[way, n], y_recv.at[way, n], rings[way]
        )

    def goes(n, way, sender):
        hop, g = n // KVHEADS, (n + way * (KVHEADS // 2)) % KVHEADS
        if way == 0:
            return (sender >= hop) & (sender < NY - 1)
        return (sender + hop) % NY < (HOPS if g >= KVHEADS // 2 else HOPS - 1)

    def ring_start(n, way):
        @pl.when(goes(n, way, ctx))
        def _():
            ring_copy(n, way).start()

    def ring_wait(n, way):
        @pl.when(goes(n, way, rings[1 - way][1]))
        def _():
            ring_copy(n, way).wait_recv()

        @pl.when(goes(n, way, ctx))
        def _():
            ring_copy(n, way).wait_send()

    for load in loads[2:5]:
        load.wait()
    row = lax.broadcasted_iota(jnp.int32, (span, HEAD_DIM), 0)
    lane = lax.broadcasted_iota(jnp.int32, (span, HEAD_DIM), 1)
    mine = lax.broadcasted_iota(jnp.int32, lengths.shape[2:], 1) == dp
    home = [jnp.sum(jnp.where(mine, lengths[0, d], 0), axis=1, keepdims=True) for d in range(2)]
    first = jnp.where(row < BIN_LEN, home[0][0:1], home[0][1:2])
    second = first + jnp.where(row < BIN_LEN, home[1][0:1], home[1][1:2])
    token = row % BIN_LEN
    short_start = doc_start(first, second, token)
    my_row = row + ctx * span
    first = long_lengths[:, 0:1]
    long_start = doc_start(first, first + long_lengths[:, 1:2], my_row)
    position = jnp.where(lane < HALF, token - short_start, my_row - long_start)
    cosine, sine = turns(position.astype(jnp.float32) * inverse[...])
    cosine_swap, sine_swap = pltpu.roll(cosine, HALF, 1), pltpu.roll(sine, HALF, 1)
    low = lane < HALF
    short_cos, short_sin = jnp.where(low, cosine, cosine_swap), jnp.where(low, -sine, sine_swap)
    long_cos, long_sin = jnp.where(low, cosine_swap, cosine), jnp.where(low, -sine_swap, sine)

    for load in loads[5:7]:
        load.wait()
    for g in range(KVHEADS):
        kv[0, g, :, :HEAD_DIM] = rotated(k_long[:, lanes(g, HEAD_DIM)], long_cos, long_sin)
        kv[0, g, :, HEAD_DIM:] = v_long[:, lanes(g, HEAD_DIM)]
    pl.semaphore_wait(barrier, 3 + DIRS)
    for n in range(2):
        for way in range(2):
            ring_start(n, way)

    pools = [*pool_refs]
    streams = range(BINS * HALVES)

    def mate_copy(t):
        return copy(
            pools[t].at[pl.ds(0, CHUNKS)], pools[t].at[pl.ds(CHUNKS, CHUNKS)],
            mate_send.at[t], mate_recv.at[t], mate,
        )

    for load in loads[7:10]:
        load.wait()

    def bias_of(rows, reach):
        index = lane[rows] % reach
        allowed = (index >= short_start[rows]) & (index <= token[rows])
        return jnp.concatenate([jnp.where(allowed, 0.0, NEGATIVE)] * GROUP, 0)

    spot = lane[:EARLY]
    for j in range(BINS):
        rows = slice(j * BIN_LEN, (j + 1) * BIN_LEN)
        early = slice(j * BIN_LEN, j * BIN_LEN + EARLY)
        late = slice(j * BIN_LEN + EARLY, (j + 1) * BIN_LEN)
        early_bias, late_bias = bias_of(early, EARLY), bias_of(late, BIN_LEN)
        early_scores, late_scores = [], []
        for g in range(CHUNKS):
            heads = [
                rotated(q_short[rows, lanes(g * GROUP + i, HEAD_DIM)], short_cos[rows], short_sin[rows])
                for i in range(GROUP)
            ]
            key = rotated(k_short[rows, lanes(g, HEAD_DIM)], short_cos[rows], short_sin[rows])
            first = jnp.concatenate([q[:EARLY] for q in heads], 0)
            second = jnp.concatenate([q[EARLY:] for q in heads], 0)
            keys = jnp.concatenate([key[:EARLY]] * GROUP, 0)
            early_scores.append(score(first, keys) + early_bias)
            late_scores.append(score(second, jnp.concatenate([key] * 2, 0)) + late_bias)
        scores = jnp.concatenate(early_scores + late_scores, 0)
        weight = jnp.exp2(scores - jnp.max(scores, axis=1, keepdims=True))
        for g in range(CHUNKS):
            w = [weight[(g * GROUP + i) * EARLY :][:EARLY] for i in range(GROUP)]
            packed = w[0]
            for i in range(1, GROUP):
                packed = jnp.where(spot // EARLY == i, w[i], packed)
            w = [weight[((CHUNKS + g) * GROUP + i) * EARLY :][:EARLY] for i in range(GROUP)]
            left = jnp.where(spot < BIN_LEN, w[0], w[1])
            right = jnp.where(spot < BIN_LEN, w[2], w[3])
            pieces = [
                packed.astype(jnp.bfloat16), v_short[early, lanes(g, HEAD_DIM)],
                jnp.concatenate([left, right], 1).astype(jnp.bfloat16), v_short[late, lanes(g, HEAD_DIM)],
            ]
            for h in range(HALVES):
                for i, piece in enumerate(pieces):
                    part = slice(CUTS[i], CUTS[i + 1])
                    pools[j * HALVES + h][g, :, part] = piece[h * ROWS : (h + 1) * ROWS]
        for h in range(HALVES):
            mate_copy(j * HALVES + h).start()

    for load in loads[:2]:
        load.wait()
    masks = [dest[0, j, 0] for j in range(BINS)]

    def entry(t, place):
        mask = masks[t // HALVES]
        index = table[(mask >> 1) * ROUTE + place]
        return index + jnp.where(index < CHUNKS, (mask & 1) * CHUNKS, 0)

    def route_copy(slot, d):
        return copy(
            stage.at[slot, d], landing.at[slot, d], route_send.at[slot], route_recv.at[slot], routes[d]
        )

    def used(step):
        return range(0 if step < X_STEPS else 2, DIRS)

    def all_of(slot):
        dirs = used(slot // len(streams))
        part = pl.ds(dirs[0], len(dirs))
        return copy(
            stage.at[slot, part], landing.at[slot, part], route_send.at[slot], route_recv.at[slot], routes[0]
        )

    def collect(t, step):
        slot = len(streams) * step + t
        all_of(slot).wait_recv()
        for d in used(step):
            pools[t][OWN + DIRS * step + d] = landing[slot, d]

    def send(t, step, entries):
        slot = len(streams) * step + t
        for d in used(step):
            stage[slot, d] = pools[t][entries[d]]
            route_copy(slot, d).start()

    def ring(n):
        for way in range(2):
            if n > 0:
                ring_wait(n - 1, way)
            if n + 2 < Y_SENDS:
                ring_start(n + 2, way)

    shift = [0] + [-h for h in range(1, HOPS + 1)] + [h for h in range(1, NY - HOPS)]

    def prepare(t):
        query[t] = stacked_heads(q_long, t, long_cos, long_sin)
        for i in (2 * t, 2 * t + 1):
            key_index = lane + (ctx + NY + shift[i]) % NY * span
            allowed = (key_index >= long_start) & (key_index <= my_row)
            bias_ref[i] = jnp.where(allowed, 0.0, NEGATIVE)

    def attend(heads, blocks):
        begins, ends = 0 in blocks, HOPS in blocks
        bias = jnp.concatenate([bias_ref[i] for i in blocks], 1)
        bias = jnp.concatenate([bias] * GROUP, 0)
        keys = [jnp.concatenate([kv[i, g, :, :HEAD_DIM] for i in blocks], 0) for g in heads]
        values = [jnp.concatenate([kv[i, g, :, HEAD_DIM:] for i in blocks], 0) for g in heads]
        scores = [score(query[g], k) + bias for g, k in zip(heads, keys)]
        peaks = [jnp.max(s, axis=1, keepdims=True) for s in scores]
        if not begins:
            olds = [top[g][:, :1] for g in heads]
            peaks = [jnp.maximum(peak, old) for peak, old in zip(peaks, olds)]
        weights = [jnp.exp2(s - peak) for s, peak in zip(scores, peaks)]
        blended = [blend(w, v) for w, v in zip(weights, values)]
        for n, g in enumerate(heads):
            both = blended[n]
            if not begins:
                both = both + acc[g] * jnp.exp2(olds[n] - peaks[n])
            if ends:
                result = (both[:, :HEAD_DIM] / both[:, HEAD_DIM:]).astype(jnp.bfloat16)
                for i in range(GROUP):
                    long_result[:, lanes(g * GROUP + i, HEAD_DIM)] = result[i * span : (i + 1) * span]
                long_copy(g).start()
            else:
                top[g] = jnp.broadcast_to(peaks[n], top.shape[1:])
                acc[g] = both

    def long_copy(g):
        return pltpu.make_async_copy(
            long_result.at[:, lanes_at(g, WIDE)], long_out.at[:, lanes_at(g, WIDE)], out_sem.at[BINS * CHUNKS + g]
        )

    def bin_copy(m, g):
        return pltpu.make_async_copy(bin_result.at[m, g], bin_out.at[m, g], out_sem.at[m * CHUNKS + g])

    near = [0, 1, HOPS + 1]
    middle = [2, HOPS + 2]
    third = [3, HOPS + 3]
    far = [HOPS]

    nearer, rest = [near, middle], third + far
    plan = [[(prepare, 0)], [(prepare, 1)], [(prepare, 2)], [(prepare, 3)]]
    plan += [[(attend, [g], blocks)] for blocks in nearer for g in range(KVHEADS)]
    plan += [[], [(attend, [0], rest)], [(attend, [2], rest)], [(attend, [1], rest)]]

    def work(tasks):
        for task, *arguments in tasks:
            task(*arguments)

    loads[10].wait()
    for step in range(STEPS):
        for t in streams:
            entries = {d: entry(t, step * DIRS + d) for d in used(step)}
            if step == 0:
                mate_copy(t).wait()
            else:
                collect(t, step - 1)
            send(t, step, entries)
            phase = 2 * step + t // HALVES
            if t % HALVES == 0 and phase <= Y_SENDS:
                ring(phase)
            if t % HALVES == HALVES - 1:
                work(plan[phase])
            if step > 0:
                all_of(len(streams) * (step - 1) + t).wait_send()

    attend([3], rest)
    for t in streams:
        collect(t, STEPS - 1)

    swap = (dp ^ masks[0]) > (dp ^ masks[1])
    for g in range(CHUNKS):
        chunks = [
            jnp.concatenate(
                [pools[t][entry(t, DIRS * STEPS + g)] for t in range(j * HALVES, (j + 1) * HALVES)], 0
            )
            for j in range(BINS)
        ]
        bin_result[0, g] = jnp.where(swap, chunks[1], chunks[0])
        bin_result[1, g] = jnp.where(swap, chunks[0], chunks[1])
        for m in range(BINS):
            bin_copy(m, g).start()
    for t in streams:
        all_of(len(streams) * (STEPS - 1) + t).wait_send()

    for g in range(CHUNKS):
        long_copy(g).wait()
        for m in range(BINS):
            bin_copy(m, g).wait()


def finish(bins_any, long_any, out_short, out_long, bins, short, long, sem_in, sem_out):
    rows = long.shape[0] // PIECES

    def long_copies(p):
        part = pl.ds(p * rows, rows)
        return (
            pltpu.make_async_copy(long_any.at[part], long.at[part], sem_in.at[BINS + p]),
            pltpu.make_async_copy(long.at[part], out_long.at[part], sem_out.at[BINS + p]),
        )

    def short_copies(m):
        part = pl.ds(m * BIN_LEN, BIN_LEN)
        return (
            pltpu.make_async_copy(bins_any.at[m], bins.at[m], sem_in.at[m]),
            pltpu.make_async_copy(short.at[part], out_short.at[part], sem_out.at[m]),
        )

    pieces = [short_copies(m) for m in range(BINS)] + [long_copies(p) for p in range(PIECES)]
    for load, _ in pieces:
        load.start()

    spot = lax.broadcasted_iota(jnp.int32, (EARLY, HEAD_DIM), 1)

    def chosen(test):
        return jnp.where(test, 1.0, 0.0).astype(jnp.bfloat16)

    quarter = [chosen(spot // EARLY == i) for i in range(GROUP)]
    side = [chosen(spot < BIN_LEN), chosen(spot >= BIN_LEN)]

    def finished(weight, values):
        blended = blend(weight, values)
        result = (blended[:, :HEAD_DIM] / blended[:, HEAD_DIM:]).astype(jnp.bfloat16)
        return jnp.concatenate([result[i * EARLY : (i + 1) * EARLY] for i in range(GROUP)], 1)

    for m in range(BINS):
        pieces[m][0].wait()
        for g in range(CHUNKS):
            chunk = bins[m, g]
            first, first_v, second, second_v = [chunk[:, CUTS[i] : CUTS[i + 1]] for i in range(4)]
            early = jnp.concatenate([first * q for q in quarter], 0)
            late = [second[:, lanes(i // 2, HEAD_DIM)] * side[i % 2] for i in range(GROUP)]
            late = jnp.concatenate(late, 0)
            start = m * BIN_LEN
            short[start : start + EARLY, lanes(g, WIDE)] = finished(
                early, jnp.concatenate([first_v] * GROUP, 0)
            )
            short[start + EARLY : start + BIN_LEN, lanes(g, WIDE)] = finished(
                late, jnp.concatenate([first_v, second_v] * 2, 0)
            )
        if m == 0:
            for load, store in pieces[BINS:]:
                load.wait()
                store.start()
        pieces[m][1].start()
    for _, store in pieces:
        store.wait()


HBM = pl.BlockSpec(memory_space=pltpu.HBM)


def local(q_short, k_short, v_short, short_lengths, bin_dest, q_long, k_long, v_long, long_lengths):
    span = q_long.shape[0]
    table = jnp.asarray(route_table())
    inverse = jnp.asarray(np.concatenate([INVERSE, INVERSE])[None, :])
    lengths = jnp.transpose(short_lengths, (1, 3, 2, 0))
    dest = jnp.transpose(bin_dest, (1, 2, 0))

    bf16, f32, i32 = jnp.bfloat16, jnp.float32, jnp.int32
    slots = BINS * HALVES * STEPS
    dma = pltpu.SemaphoreType.DMA
    inputs = [k_long, v_long, q_short, k_short, v_short, q_long]
    bins_shape = (BINS, CHUNKS, EARLY, CUTS[-1])
    bins, long = pl.pallas_call(
        kernel,
        out_shape=[jax.ShapeDtypeStruct(bins_shape, bf16), jax.ShapeDtypeStruct(q_long.shape, bf16)],
        in_specs=[HBM] * 11,
        out_specs=[HBM, HBM],
        scratch_shapes=[
            pltpu.SMEM((NZ * NX * ROUTE,), i32),
            pltpu.SMEM(dest.shape, i32),
            pltpu.VMEM(inverse.shape, f32),
            pltpu.VMEM(lengths.shape, i32),
            pltpu.VMEM(long_lengths.shape, i32),
            *[pltpu.VMEM(a.shape, bf16) for a in inputs],
            [pltpu.VMEM((POOL, ROWS, CUTS[-1]), bf16)] * (BINS * HALVES),
            pltpu.VMEM((slots, DIRS, ROWS, CUTS[-1]), bf16),
            pltpu.VMEM((slots, DIRS, ROWS, CUTS[-1]), bf16),
            pltpu.VMEM((NY, KVHEADS, span, 2 * HEAD_DIM), bf16),
            pltpu.VMEM((KVHEADS, GROUP * span, HEAD_DIM), bf16),
            pltpu.VMEM((KVHEADS, GROUP * span, HEAD_DIM), f32),
            pltpu.VMEM((KVHEADS, GROUP * span, 2 * HEAD_DIM), f32),
            pltpu.VMEM((NY, span, span), f32),
            pltpu.VMEM(bins_shape, bf16),
            pltpu.VMEM(q_long.shape, bf16),
            dma((11,)),
            dma((BINS * CHUNKS + KVHEADS,)),
            dma((BINS * HALVES,)),
            dma((BINS * HALVES,)),
            dma((slots,)),
            dma((slots,)),
            dma((2, Y_SENDS)),
            dma((2, Y_SENDS)),
        ],
        compiler_params=pltpu.CompilerParams(
            collective_id=0, has_side_effects=True, vmem_limit_bytes=56 * 2**20
        ),
    )(table, inverse, lengths, dest, long_lengths, *inputs)
    return pl.pallas_call(
        finish,
        out_shape=[jax.ShapeDtypeStruct(q_short.shape, bf16), jax.ShapeDtypeStruct(q_long.shape, bf16)],
        in_specs=[HBM, HBM],
        out_specs=[HBM, HBM],
        scratch_shapes=[
            pltpu.VMEM(bins_shape, bf16),
            pltpu.VMEM(q_short.shape, bf16),
            pltpu.VMEM(q_long.shape, bf16),
            dma((BINS + PIECES,)),
            dma((BINS + PIECES,)),
        ],
        compiler_params=pltpu.CompilerParams(vmem_limit_bytes=56 * 2**20),
    )(bins, long)


def solution(mesh):
    in_specs = (
        P(("dp", "ctx"), None),
        P(("dp", "ctx"), None),
        P(("dp", "ctx"), None),
        P(None, "ctx", None, None),
        P(None, "ctx", None),
        P(("dp", "ctx"), None),
        P(("dp", "ctx"), None),
        P(("dp", "ctx"), None),
        P("dp", None),
    )
    out_specs = (P(("dp", "ctx"), None), P(("dp", "ctx"), None))
    return jax.shard_map(local, mesh=mesh, in_specs=in_specs, out_specs=out_specs, check_vma=False)
```
